128 devices in a mesh: dp: 8 (over z, core), seq: 16 (over y, x).
Axes of the slice: x: 4, y: 4, z: 4, core: 2. Of those that a mesh axis runs over, the one named last changes fastest.
Arguments:
- seq_in: bfloat16 [8, 4096, 512], P('dp', 'seq'), may hold values from -6 to 6
- w_first: bfloat16 [5, 512, 512], replicated, may hold values from -0.125 to 0.125
- w_second: bfloat16 [5, 512, 1024], replicated, may hold values from -0.125 to 0.125
- head_vec: float32 [1024], replicated, may hold values from -5 to 5
- track_cot: bfloat16 [8, 2048, 1024], P('dp', 'seq'), may hold values from -6 to 6
- donor_pos: int32 [8, 256], P('dp', 'seq'), may hold values from 0 to 2047
- acceptor_pos: int32 [8, 256], P('dp', 'seq'), may hold values from 0 to 2047
- pair_cot: float32 [8, 256], P('dp', 'seq'), may hold values from -6 to 6
- live_pairs: int32 [8, 16], P('dp', 'seq'), may hold values from 1 to 16, 128 in all within a row
Outputs:
- scores: float32 [8, 256], P('dp', 'seq')
- grad_first: float32 [2560, 512], P(('dp', 'seq'))
- grad_second: float32 [2560, 1024], P(('dp', 'seq'))
- grad_input: bfloat16 [8, 4096, 512], P('dp', 'seq')
- grad_head: float32 [1024], replicated
The draws below stay inside these ranges and needn't reach their ends.
Inputs may be any that keep to these rules, and one draw needn't show every extreme that they name: The first live_pairs[g, s] of device s's 16 slots are live, the rest are ignored; in each sequence the counts sum to half of all slots, and at least one device holds 16 live pairs.
All inputs are finite; a program needn't handle non-finite values.
Results may differ from the reference program's by a relative error of at most 0.015.
Values may be sent and summed in bfloat16 or wider, within the bound.
No kernel may reach another device: no remote copies, remote signals or barrier semaphores. Data moves between devices by JAX's collectives and lax.ppermute only.
A program may use at most 128 MiB of HBM per device.

```python
import math
import jax
import jax.numpy as jnp
import numpy as np
from jax import lax

C1 = 512
C2 = 1024
KW = 5
PAIR_DEV = 16
L1 = 4096
L2 = 2048
PAIRS = 256
GROUPS = 8
N_SEQ = 16


def place_ends(values, own_key, low, top_value):
    shape = values.shape
    spot = [jax.random.randint(jax.random.fold_in(own_key, axis), (), 0, shape[axis]) for axis in range(len(shape))]
    values = values.at[tuple(spot)].set(low)
    longest = shape.index(max(shape))
    spot[longest] = (spot[longest] + 1) % shape[longest]
    return values.at[tuple(spot)].set(top_value)


def raised(array, rng, source, target, blocks, factor):
    def block_of(axis_at):
        return (jnp.arange(array.shape[axis_at]) // (array.shape[axis_at] // blocks)).reshape((-1,) + (1,) * (array.ndim - 1 - axis_at))

    first = jax.random.permutation(rng, blocks)[block_of(target)]
    other_side = (block_of(target) + blocks // 2) % blocks
    return jnp.where((block_of(source) == first) | (block_of(source) == other_side), factor * array, array)


def block_scale(stream_key, extent, cuts, least, largest):
    level = 1.0
    for axis_at, blocks in cuts:
        draws = jax.random.uniform(jax.random.fold_in(jax.random.fold_in(stream_key, 6), axis_at), (blocks,), jnp.float32, least / len(cuts), largest / len(cuts))
        level = level * jnp.repeat(jnp.exp(draws), extent[axis_at] // blocks).reshape((-1,) + (1,) * (len(extent) - 1 - axis_at))
    return level


def split_up(count, total, reach, slope):
    loads = [(1 << 20) // math.isqrt(rank ** slope) + 1 for rank in range(2, count + 1)]
    rest, holding = total - reach - (count - 1), [1] * (count - 1)
    while rest > 0:
        candidates = [i for i in range(count - 1) if holding[i] < reach]
        mass, left = sum([loads[i] for i in candidates]), rest
        for i in candidates:
            addition = min(reach - holding[i], max(1, left * loads[i] // mass), rest)
            holding[i] = holding[i] + addition
            rest = rest - addition
    return np.array([reach] + holding)


def ragged(key, count, total, bound, skew):
    if count == 2:
        one = jax.random.randint(key, (), max(1, total - bound), min(bound, total - 1) + 1)
        return jnp.stack([one, total - one])
    lengths = jnp.asarray(split_up(count, total, bound, skew), jnp.int32)
    pairs = (count - 1) // 2
    giver, sink = lengths[1:1 + 2 * pairs:2], lengths[2:2 + 2 * pairs:2]
    room = jnp.minimum(giver - 1, bound - sink)
    moved = jax.random.randint(jax.random.fold_in(key, 1), (pairs,), 0, 1 << 20) % (room + 1)
    lengths = lengths.at[1:1 + 2 * pairs:2].set(giver - moved).at[2:2 + 2 * pairs:2].set(sink + moved)
    return lengths[jax.random.permutation(jax.random.fold_in(key, 2), count)]


def gaussian(key, shape, scale, most, shards=(), held_as=jnp.bfloat16):
    gain = block_scale(key, shape, shards, -0.22, 0.18) if shards else 1.0
    result = jax.random.normal(key, shape, jnp.float32) * scale * gain
    return jnp.minimum(jnp.maximum(result, -most), most).astype(held_as)


def noise_with(rng, shape, deviation, most, shards, heavy, kind=jnp.bfloat16):
    drawn = deviation * jax.random.normal(rng, shape, jnp.float32)
    if shards:
        drawn = drawn * block_scale(rng, shape, shards, -0.22, 0.18)
    return jnp.clip(raised(drawn, jax.random.fold_in(rng, 3), *heavy), -most, most).astype(kind)


def setup_inputs(seed: int = 0) -> dict:
    key_list = jax.random.split(jax.random.key(seed), 10)
    seq_in = noise_with(key_list[0], (GROUPS, L1, C1), 1.0, 6.0, ((0, 8), (1, 16)), (1, 2, 16, 2.0))
    w_first = gaussian(key_list[1], (KW, C1, C1), (KW * C1) ** -0.5, 0.125)
    w_second = gaussian(key_list[2], (KW, C1, C2), (KW * C1) ** -0.5, 0.125)
    head_vec = gaussian(key_list[3], (C2,), 1.0, 5.0, (), jnp.float32)
    track_cot = gaussian(key_list[4], (GROUPS, L2, C2), 1.0, 6.0, ((0, 8), (1, 16)))
    donor_pos = place_ends(jax.random.randint(key_list[5], (GROUPS, PAIRS), 0, L2), jax.random.fold_in(key_list[5], 1), 0, L2 - 1).astype(jnp.int32)
    acceptor_pos = place_ends(jax.random.randint(key_list[6], (GROUPS, PAIRS), 0, L2), jax.random.fold_in(key_list[6], 1), 0, L2 - 1).astype(jnp.int32)
    pair_cot = gaussian(key_list[7], (GROUPS, PAIRS), 1.0, 6.0, ((0, 8), (1, 16)), jnp.float32)
    live_pairs = jax.vmap(lambda own: ragged(own, N_SEQ, PAIR_DEV * N_SEQ // 2, PAIR_DEV, 2))(jax.random.split(key_list[8], GROUPS)).reshape((GROUPS, N_SEQ)).astype(jnp.int32)
    return {"seq_in": seq_in, "w_first": w_first, "w_second": w_second, "head_vec": head_vec, "track_cot": track_cot, "donor_pos": donor_pos, "acceptor_pos": acceptor_pos, "pair_cot": pair_cot, "live_pairs": live_pairs}


def unfold_taps(extended, row_count, tap_count):
    return jnp.concatenate([extended[tap_index:tap_index + row_count] for tap_index in range(tap_count)], axis=1)

def transposed_conv(grad_pre, flat_weight, row_count, chan_in, tap_count):
    spread = lax.dot_general(grad_pre, flat_weight, (((1,), (1,)), ((), ())), preferred_element_type=jnp.float32)
    margin = tap_count // 2
    summed_taps = jnp.zeros((row_count + 2 * margin, chan_in), jnp.float32)
    for tap_index in range(tap_count):
        piece = spread[:, tap_index * chan_in:(tap_index + 1) * chan_in]
        summed_taps = summed_taps + jnp.pad(piece, ((tap_index, tap_count - 1 - tap_index), (0, 0)))
    return summed_taps[margin:margin + row_count]

def reference(seq_in, w_first, w_second, head_vec, track_cot, donor_pos, acceptor_pos, pair_cot, live_pairs):
    first_mat = w_first.reshape(KW * C1, C1)
    second_mat = w_second.reshape(KW * C1, C2)
    pair_scale = C2 ** (-0.5)
    margin = KW // 2
    slot_ids = jnp.arange(PAIRS, dtype=jnp.int32)
    grad_first = jnp.zeros((KW * C1, C1), jnp.float32)
    grad_second = jnp.zeros((KW * C1, C2), jnp.float32)
    grad_head = jnp.zeros((C2,), jnp.float32)
    score_list = []
    input_list = []
    for group_index in range(GROUPS):
        inputs = seq_in[group_index]
        input_cols = unfold_taps(jnp.pad(inputs, ((margin, margin), (0, 0))), L1, KW)
        pre_first = jnp.dot(input_cols, first_mat, preferred_element_type=jnp.float32)
        y_first = inputs.astype(jnp.float32) + jax.nn.gelu(pre_first)
        pooled = (0.5 * (y_first[0::2] + y_first[1::2])).astype(jnp.bfloat16)
        pooled_cols = unfold_taps(jnp.pad(pooled, ((margin, margin), (0, 0))), L2, KW)
        pre_second = jnp.dot(pooled_cols, second_mat, preferred_element_type=jnp.float32)
        encoded = jax.nn.gelu(pre_second).astype(jnp.bfloat16)
        live_mask = slot_ids % PAIR_DEV < jnp.repeat(live_pairs[group_index], PAIR_DEV)
        donor_rows = encoded[donor_pos[group_index]].astype(jnp.float32)
        accept_rows = encoded[acceptor_pos[group_index]].astype(jnp.float32)
        score_list.append(jnp.where(live_mask, lax.optimization_barrier(jnp.sum(donor_rows * accept_rows * head_vec, axis=1)) * pair_scale, 0.0))
        pair_weight = jnp.where(live_mask, pair_cot[group_index], 0.0) * pair_scale
        grad_head = grad_head + lax.optimization_barrier(jnp.sum(pair_weight[:, None] * donor_rows * accept_rows, axis=0))
        donor_grad = (pair_weight[:, None] * head_vec * accept_rows).astype(jnp.bfloat16)
        accept_grad = (pair_weight[:, None] * head_vec * donor_rows).astype(jnp.bfloat16)
        grad_encoded = track_cot[group_index].astype(jnp.float32)
        grad_encoded = grad_encoded.at[donor_pos[group_index]].add(donor_grad.astype(jnp.float32))
        grad_encoded = grad_encoded.at[acceptor_pos[group_index]].add(accept_grad.astype(jnp.float32))
        grad_pre2 = jax.vjp(jax.nn.gelu, pre_second)[1](grad_encoded)[0].astype(jnp.bfloat16)
        grad_second = grad_second + lax.dot_general(pooled_cols, grad_pre2, (((0,), (0,)), ((), ())), preferred_element_type=jnp.float32)
        grad_pooled = transposed_conv(grad_pre2, second_mat, L2, C1, KW)
        grad_y = jnp.repeat(grad_pooled * 0.5, 2, axis=0)
        grad_pre1 = jax.vjp(jax.nn.gelu, pre_first)[1](grad_y)[0].astype(jnp.bfloat16)
        grad_first = grad_first + lax.dot_general(input_cols, grad_pre1, (((0,), (0,)), ((), ())), preferred_element_type=jnp.float32)
        input_list.append((grad_y + transposed_conv(grad_pre1, first_mat, L1, C1, KW)).astype(jnp.bfloat16))
    return (jnp.stack(score_list), grad_first, grad_second, jnp.stack(input_list), grad_head)
```

```python
import jax
import jax.numpy as jnp
from jax import lax
from jax.sharding import PartitionSpec as P

BF = jnp.bfloat16
F32 = jnp.float32
ROOT = 0.7978845608028654
CUBE = 0.044715


def gelu_both(pre):
    square = pre * pre
    bent = jnp.tanh(ROOT * pre * (1.0 + CUBE * square))
    half = 0.5 * (1.0 + bent)
    slope = half + 0.5 * pre * (1.0 - bent * bent) * (ROOT * (1.0 + 3.0 * CUBE * square))
    return pre * half, slope


def dot(left, right, dims=((1,), (0,))):
    return lax.dot_general(left, right, (dims, ((), ())), preferred_element_type=F32)


def edges(inputs, track, count):
    forward = [(i, i + 1) for i in range(count - 1)]
    backward = [(i + 1, i) for i in range(count - 1)]
    last = jnp.concatenate([inputs[-12:], track[-3:].reshape(6, 512)], axis=0)
    first = jnp.concatenate([inputs[:12], track[:3].reshape(6, 512)], axis=0)
    return lax.ppermute(last, "seq", forward), lax.ppermute(first, "seq", backward)


def forward_part(inputs, left, right, w_first, w_second, seq_index):
    zeros = jnp.zeros((20, 512), BF)
    ext = jnp.concatenate([zeros, left[:12], inputs, right[:12], zeros], axis=0)
    pre_first = sum(dot(ext[14 + k : 302 + k], w_first[k]) for k in range(5))
    act, slope_first = gelu_both(pre_first)
    spot = seq_index * 256 - 16 + jnp.arange(288, dtype=jnp.int32)[:, None]
    slope_first = jnp.where((spot >= 0) & (spot < 4096), slope_first, 0.0)
    y_first = ext[16:304].astype(F32) + act
    pooled = 0.5 * (y_first[0::2] + y_first[1::2])
    spot = seq_index * 128 - 8 + jnp.arange(144, dtype=jnp.int32)[:, None]
    pooled = jnp.where((spot >= 0) & (spot < 2048), pooled, 0.0).astype(BF)
    wide = jnp.pad(pooled, ((8, 8), (0, 0)))
    pre_second = sum(dot(wide[6 + k : 150 + k], w_second[k]) for k in range(5))
    act, slope_second = gelu_both(pre_second)
    return pooled[8:136], act[8:136].astype(BF), slope_first, slope_second


def pair_part(got, head_mine):
    flat = got.reshape(1280, 128)
    info = got[:, 64:, :].reshape(256, 128).astype(F32)
    donor = (info[:, 0] * 64.0 + info[:, 1]).astype(jnp.int32)
    accept = (info[:, 2] * 64.0 + info[:, 3]).astype(jnp.int32)
    weight = (info[:, 4] + info[:, 5])[:, None]
    spots = jnp.concatenate([donor, accept])
    row_of = (spots // 128) * 80 + spots % 64
    pick = (row_of[:, None] == jnp.arange(1280, dtype=jnp.int32)[None, :]).astype(BF)
    rows = dot(pick, flat)
    rows = jnp.where((spots % 128 < 64)[:, None], rows[:, :64], rows[:, 64:])
    donor_rows, accept_rows = rows[:256], rows[256:]
    both = donor_rows * accept_rows
    partial = jnp.sum(both * head_mine, axis=1)
    head_term = jnp.sum(weight * both, axis=0)
    scaled = weight * head_mine
    grads = jnp.concatenate([scaled * accept_rows, scaled * donor_rows], axis=0).astype(BF)
    index = jnp.arange(1280, dtype=jnp.int32)
    block, row = index // 80, index % 80
    low = jnp.where(row < 64, block * 128 + row, jnp.where(row < 67, block * 128 + row - 67, -1))
    high = jnp.where(row < 64, block * 128 + 64 + row, jnp.where(row < 67, block * 128 + 64 + row, -1))
    low_pick = (low[:, None] == spots[None, :]).astype(BF)
    high_pick = (high[:, None] == spots[None, :]).astype(BF)
    sent = jnp.concatenate([dot(low_pick, grads), dot(high_pick, grads)], axis=1).astype(BF)
    top = lax.reduce_precision(partial, 8, 7)
    extra = jnp.concatenate([top, partial - top]).astype(BF).reshape(4, 128)
    sent = sent.reshape(16, 80, 128).at[:, 68:72].set(extra[None])
    return sent, head_term


def backward_part(back, track, left, right, slope_first, slope_second, w_first, w_second):
    main = back[:, :64].reshape(16, 64, 2, 64).transpose(2, 1, 0, 3).reshape(128, 1024)
    edge = back[:, 64:67].reshape(16, 3, 2, 64).transpose(2, 1, 0, 3).reshape(2, 3, 1024)
    zeros = jnp.zeros((5, 1024), F32)
    junction = jnp.concatenate([zeros, edge[0].astype(F32), main.astype(F32), edge[1].astype(F32), zeros])
    track_all = jnp.concatenate(
        [zeros.astype(BF), left[12:18].reshape(3, 1024), track, right[12:18].reshape(3, 1024), zeros.astype(BF)]
    )
    grad_second_pre = ((track_all.astype(F32) + junction) * slope_second).astype(BF)
    wide = jnp.pad(grad_second_pre, ((8, 8), (0, 0)))
    grad_pooled = sum(dot(wide[10 - k : 154 - k], w_second[k], ((1,), (1,))) for k in range(5))
    grad_y = jnp.repeat(0.5 * grad_pooled, 2, axis=0)
    grad_first_pre = (grad_y * slope_first).astype(BF)
    return grad_second_pre, grad_first_pre, grad_y


def input_part(grad_y, grad_first_pre, w_first):
    spread = sum(dot(grad_first_pre[18 - k : 274 - k], w_first[k], ((1,), (1,))) for k in range(5))
    return (grad_y[16:272] + spread).astype(BF)


def term_part(columns, got, dp_index):
    first = jnp.zeros((512, 5, 64), F32)
    second = jnp.zeros((512, 5, 128), F32)
    for step in range(8):
        part = lax.dynamic_index_in_dim(got, dp_index ^ step, 0, keepdims=False)
        grad_1 = jnp.concatenate([part[:144, :64], part[:144, 64:]], axis=0)
        grad_2 = jnp.pad(part[144:], ((8, 8), (0, 0)))
        wide_1 = jnp.concatenate([grad_1[18 - k : 274 - k] for k in range(5)], axis=1)
        wide_2 = jnp.concatenate([grad_2[18 - k : 146 - k] for k in range(5)], axis=1)
        first = first + dot(columns[step][:, :256], wide_1).reshape(512, 5, 64)
        second = second + dot(columns[step][:, 256:], wide_2).reshape(512, 5, 128)
    return first.transpose(1, 0, 2).reshape(2560, 64), second.transpose(1, 0, 2).reshape(2560, 128)


def per_device(
    seq_in, w_first, w_second, head_vec, track_cot, donor_pos, acceptor_pos, pair_cot, live_pairs
):
    seq_index = lax.axis_index("seq")
    dp_index = lax.axis_index("dp")
    inputs, track = seq_in[0], track_cot[0]
    left, right = edges(inputs, track, 16)
    pooled, encoded, slope_first, slope_second = forward_part(
        inputs, left, right, w_first, w_second, seq_index
    )

    live_mine = jnp.arange(16, dtype=jnp.int32) < live_pairs[0, 0]
    weight = jnp.where(live_mine, pair_cot[0], 0.0) * (1024 ** -0.5)
    top = lax.reduce_precision(weight, 8, 7)
    info = jnp.stack(
        [
            (donor_pos[0] >> 6).astype(F32),
            (donor_pos[0] & 63).astype(F32),
            (acceptor_pos[0] >> 6).astype(F32),
            (acceptor_pos[0] & 63).astype(F32),
            top,
            weight - top,
        ],
        axis=1,
    ).astype(BF)
    info = jnp.pad(info, ((0, 0), (0, 122)))
    main = encoded.reshape(2, 64, 16, 64).transpose(2, 1, 0, 3).reshape(16, 64, 128)
    message = jnp.concatenate([main, jnp.broadcast_to(info[None], (16, 16, 128))], axis=1)
    got = lax.all_to_all(message, "seq", 0, 0, tiled=True)

    mine = jnp.concatenate([inputs, pooled], axis=0).T
    columns = [mine] + [
        lax.ppermute(mine, "dp", [(i, i ^ step) for i in range(8)]) for step in range(1, 8)
    ]

    head_mine = lax.dynamic_slice_in_dim(head_vec, seq_index * 64, 64)
    sent, head_term = pair_part(got, head_mine[None, :])
    back = lax.all_to_all(sent, "seq", 0, 0, tiled=True)
    pieces = jnp.sum(back[:, 68:72].astype(F32), axis=0)
    whole = (pieces[:2] + pieces[2:]).reshape(256)
    scores = jnp.where(
        live_mine, lax.dynamic_slice_in_dim(whole, seq_index * 16, 16) * (1024 ** -0.5), 0.0
    )

    grad_2, grad_1, grad_y = backward_part(
        back, track, left, right, slope_first, slope_second, w_first, w_second
    )
    part_1 = grad_1.reshape(2, 144, 8, 64).transpose(2, 1, 0, 3).reshape(8, 144, 128)
    part_2 = grad_2.reshape(144, 8, 128).transpose(1, 0, 2)
    grads = lax.all_to_all(jnp.concatenate([part_1, part_2], axis=1), "dp", 0, 0, tiled=True)
    grad_input = input_part(grad_y, grad_1, w_first)
    first, second = term_part(columns, grads, dp_index)

    top = lax.reduce_precision(head_term, 8, 7)
    head_row = jnp.concatenate([top, head_term - top]).astype(BF)
    terms = jnp.concatenate(
        [
            second.astype(BF).reshape(128, 20, 128),
            first.astype(BF).reshape(128, 2, 10, 64).transpose(0, 2, 1, 3).reshape(128, 10, 128),
            jnp.broadcast_to(head_row[None, None], (128, 1, 128)),
            jnp.zeros((128, 1, 128), BF),
        ],
        axis=1,
    )
    final = lax.all_to_all(terms, ("dp", "seq"), 0, 0, tiled=True).reshape(8, 16, 32, 128)
    summed = jnp.sum(final[:, :, :30].astype(F32), axis=1)
    out_second = summed[:, :20].transpose(1, 0, 2).reshape(20, 1024)
    out_first = summed[:, 20:].reshape(8, 10, 2, 64).transpose(2, 1, 0, 3).reshape(20, 512)
    head = jnp.sum(final[:, :, 30].astype(F32), axis=0)
    grad_head = (head[:, :64] + head[:, 64:]).reshape(1024)
    return (scores[None], out_first, out_second, grad_input[None], grad_head)


def solution(mesh):
    in_specs = (
        P("dp", "seq", None),
        P(),
        P(),
        P(),
        P("dp", "seq", None),
        P("dp", "seq"),
        P("dp", "seq"),
        P("dp", "seq"),
        P("dp", "seq"),
    )
    out_specs = (
        P("dp", "seq"),
        P(("dp", "seq"), None),
        P(("dp", "seq"), None),
        P("dp", "seq", None),
        P(),
    )
    return jax.shard_map(
        per_device, mesh=mesh, in_specs=in_specs, out_specs=out_specs, check_vma=False
    )
```

```python
import jax
import jax.numpy as jnp
from jax import lax
from jax.experimental import pallas as pl
from jax.experimental.pallas import tpu as pltpu
from jax.sharding import PartitionSpec as P

BF = jnp.bfloat16
F32 = jnp.float32
ROOT = 0.7978845608028654
CUBE = 0.044715


def gelu_both(pre):
    square = pre * pre
    bent = jnp.tanh(ROOT * pre * (1.0 + CUBE * square))
    half = 0.5 * (1.0 + bent)
    slope = half + 0.5 * pre * (1.0 - bent * bent) * (ROOT * (1.0 + 3.0 * CUBE * square))
    return pre * half, slope


def dot(left, right, dims=((1,), (0,))):
    return lax.dot_general(left, right, (dims, ((), ())), preferred_element_type=F32)


def edges(inputs, track, count):
    forward = [(i, i + 1) for i in range(count - 1)]
    backward = [(i + 1, i) for i in range(count - 1)]
    last = jnp.concatenate([inputs[-12:], track[-3:].reshape(6, 512)], axis=0)
    first = jnp.concatenate([inputs[:12], track[:3].reshape(6, 512)], axis=0)
    return lax.ppermute(last, "seq", forward), lax.ppermute(first, "seq", backward)


VMEM = pl.BlockSpec(memory_space=pltpu.VMEM)
SMEM = pl.BlockSpec(memory_space=pltpu.SMEM)
ANY = pl.BlockSpec(memory_space=pl.ANY)
MEBI = 1024 * 1024


def rounded(value):
    return value.astype(BF).astype(F32)


def half_lanes(rows):
    return lax.broadcasted_iota(jnp.int32, (rows, 128), 1) < 64


def swap(value):
    return pltpu.roll(value, 64, 1)


def forward_kernel(
    seq_ref,
    live_ref,
    inputs_ref,
    left_ref,
    right_ref,
    donor_ref,
    accept_ref,
    cot_ref,
    first_any,
    second_any,
    mess_ref,
    pooled_ref,
    slope_1_ref,
    slope_2_ref,
    first_mat,
    second_mat,
    ext,
    act_scr,
    wide,
    sems,
):
    copy_1 = pltpu.make_async_copy(first_any, first_mat, sems.at[0])
    copy_2 = pltpu.make_async_copy(second_any, second_mat, sems.at[1])
    copy_1.start()
    copy_2.start()
    seq_index = seq_ref[0]
    ext[0:32, :] = jnp.zeros((32, 512), F32)
    ext[288:320, :] = jnp.zeros((32, 512), F32)
    ext[20:32, :] = left_ref[0:12, :].astype(F32)
    ext[32:288, :] = inputs_ref[...].astype(F32)
    ext[288:300, :] = right_ref[0:12, :].astype(F32)
    taps = jnp.concatenate([ext[14 + k : 302 + k, :].astype(BF) for k in range(5)], axis=1)
    copy_1.wait()
    pre = dot(taps, first_mat[...])
    act, slope = gelu_both(pre)
    spot = seq_index * 256 - 16 + lax.broadcasted_iota(jnp.int32, (288, 1), 0)
    slope_1_ref[...] = jnp.where((spot >= 0) & (spot < 4096), slope, 0.0)
    y_first = ext[16:304, :] + act
    for tile in range(4):
        lanes = slice(128 * tile, 128 * tile + 128)
        act_scr[288 * tile : 288 * tile + 288, :] = y_first[:, lanes]
        even = act_scr[pl.ds(288 * tile, 144, 2), :]
        wide[8:152, lanes] = even + act_scr[pl.ds(288 * tile + 1, 144, 2), :]
    spot = seq_index * 128 - 8 + lax.broadcasted_iota(jnp.int32, (144, 1), 0)
    pooled = jnp.where((spot >= 0) & (spot < 2048), 0.5 * wide[8:152, :], 0.0)
    wide[0:8, :] = jnp.zeros((8, 512), F32)
    wide[152:160, :] = jnp.zeros((8, 512), F32)
    wide[8:152, :] = pooled
    pooled_ref[...] = wide[16:144, :].astype(BF)
    taps = jnp.concatenate([wide[6 + k : 150 + k, :].astype(BF) for k in range(5)], axis=1)
    copy_2.wait()
    pre = dot(taps, second_mat[...])
    act, slope = gelu_both(pre)
    slope_2_ref[...] = slope

    same = lax.broadcasted_iota(jnp.int32, (16, 16), 0) == lax.broadcasted_iota(
        jnp.int32, (16, 16), 1
    )

    def column(row):
        return jnp.sum(jnp.where(same, row, 0.0), axis=1, keepdims=True)

    donor, accept = donor_ref[...], accept_ref[...]
    live = lax.broadcasted_iota(jnp.int32, (1, 16), 1) < live_ref[0]
    weight = column(jnp.where(live, cot_ref[...], 0.0) * (1024 ** -0.5))
    lane = lax.broadcasted_iota(jnp.int32, (16, 128), 1)
    info = jnp.zeros((16, 128), F32)
    for place, value in enumerate(
        [
            column((donor >> 6).astype(F32)),
            column((donor & 63).astype(F32)),
            column((accept >> 6).astype(F32)),
            column((accept & 63).astype(F32)),
            weight,
            weight - rounded(weight),
        ]
    ):
        info = jnp.where(lane == place, value, info)
    info = info.astype(BF)
    left = half_lanes(64)
    for pair in range(8):
        top = act[8:72, 128 * pair : 128 * pair + 128]
        low = act[72:136, 128 * pair : 128 * pair + 128]
        mess_ref[2 * pair, 0:64, :] = jnp.where(left, top, swap(low)).astype(BF)
        mess_ref[2 * pair + 1, 0:64, :] = jnp.where(left, swap(top), low).astype(BF)
    for target in range(16):
        mess_ref[target, 64:80, :] = info


def forward_part(seq_index, live, inputs, left, right, donor, accept, cot, w_first, w_second):
    return pl.pallas_call(
        forward_kernel,
        out_shape=[
            jax.ShapeDtypeStruct((16, 80, 128), BF),
            jax.ShapeDtypeStruct((128, 512), BF),
            jax.ShapeDtypeStruct((288, 512), F32),
            jax.ShapeDtypeStruct((144, 1024), F32),
        ],
        in_specs=[SMEM, SMEM] + [VMEM] * 6 + [ANY, ANY],
        out_specs=[VMEM] * 4,
        scratch_shapes=[
            pltpu.VMEM((2560, 512), BF),
            pltpu.VMEM((2560, 1024), BF),
            pltpu.VMEM((320, 512), F32),
            pltpu.VMEM((1152, 128), F32),
            pltpu.VMEM((160, 512), F32),
            pltpu.SemaphoreType.DMA((2,)),
        ],
        compiler_params=pltpu.CompilerParams(vmem_limit_bytes=24 * MEBI),
        cost_estimate=pl.CostEstimate(
            flops=15 * 10**8, bytes_accessed=10 * 10**6, transcendentals=3 * 10**5
        ),
        name="forward",
    )(
        seq_index, live, inputs, left, right, donor, accept, cot,
        w_first.reshape(2560, 512), w_second.reshape(2560, 1024),
    )


def pair_kernel(seq_ref, got_ref, head_ref, sent_ref, term_ref):
    seq_index = seq_ref[0]
    head_row = head_ref[pl.ds(seq_index // 2, 1), :]
    head_row = jnp.where(seq_index % 2 == 0, head_row, swap(head_row))[:, :64]
    flat = jnp.concatenate([got_ref[i] for i in range(16)], axis=0)
    info = jnp.concatenate([got_ref[i, 64:80, :].astype(F32) for i in range(16)], axis=0)
    donor = (info[:, 0:1] * 64.0 + info[:, 1:2]).astype(jnp.int32)
    accept = (info[:, 2:3] * 64.0 + info[:, 3:4]).astype(jnp.int32)
    weight = info[:, 4:5] + info[:, 5:6]
    spots = jnp.concatenate([donor, accept], axis=0)
    row_of = (spots >> 7) * 80 + (spots & 63)
    pick = (row_of == lax.broadcasted_iota(jnp.int32, (512, 1280), 1)).astype(F32).astype(BF)
    rows = dot(pick, flat)
    rows = jnp.where((spots & 127) < 64, rows, swap(rows))[:, :64]
    donor_rows, accept_rows = rows[:256], rows[256:]
    both = donor_rows * accept_rows
    partial = jnp.sum(both * head_row, axis=1, keepdims=True)
    term = jnp.sum(weight * both, axis=0, keepdims=True)
    term_high = rounded(term)
    term_ref[...] = jnp.concatenate([term_high, term - term_high], axis=1)
    scaled = weight * head_row
    grads = jnp.concatenate([scaled * accept_rows, scaled * donor_rows], axis=0)
    blank = jnp.zeros((512, 64), F32)
    grads = jnp.concatenate(
        [
            jnp.concatenate([grads, blank], axis=1),
            jnp.concatenate([blank, grads], axis=1),
        ],
        axis=0,
    ).astype(BF)
    lane = lax.broadcasted_iota(jnp.int32, (256, 128), 1)
    turned = jnp.where(
        lane == 0,
        donor.astype(F32),
        jnp.where(lane == 1, accept.astype(F32), jnp.where(lane == 2, partial, 0.0)),
    ).T
    spot_row = jnp.concatenate([turned[0:1, :], turned[1:2, :]], axis=1).astype(jnp.int32)
    high = rounded(turned[2:3, :])
    rest = turned[2:3, :] - high
    extra = jnp.concatenate(
        [
            jnp.zeros((4, 128), F32),
            high[:, :128],
            high[:, 128:],
            rest[:, :128],
            rest[:, 128:],
            jnp.zeros((8, 128), F32),
        ],
        axis=0,
    )
    index = lax.broadcasted_iota(jnp.int32, (80, 1), 0)
    low_edge = jnp.where(index < 67, index - 67, -4096)
    high_edge = jnp.where(index < 67, index + 64, -4096)
    low_row = jnp.where(index < 64, index, low_edge)
    high_row = jnp.where(index < 64, index + 64, high_edge)
    for target in range(16):
        base = 128 * target
        low_pick = (low_row + base == spot_row).astype(F32)
        high_pick = (high_row + base == spot_row).astype(F32)
        piece = dot(jnp.concatenate([low_pick, high_pick], axis=1).astype(BF), grads)
        sent_ref[target, 0:64, :] = piece[0:64].astype(BF)
        sent_ref[target, 64:80, :] = (piece[64:80] + extra).astype(BF)


def pair_part(seq_index, got, head_vec):
    return pl.pallas_call(
        pair_kernel,
        out_shape=[
            jax.ShapeDtypeStruct((16, 80, 128), BF),
            jax.ShapeDtypeStruct((1, 128), F32),
        ],
        in_specs=[SMEM, VMEM, VMEM],
        out_specs=[VMEM] * 2,
        compiler_params=pltpu.CompilerParams(vmem_limit_bytes=24 * MEBI),
        cost_estimate=pl.CostEstimate(
            flops=5 * 10**8, bytes_accessed=10**6, transcendentals=0
        ),
        name="pairs",
    )(seq_index, got, head_vec.reshape(8, 128))


def backward_kernel(
    back_ref,
    track_ref,
    left_ref,
    right_ref,
    slope_1_ref,
    slope_2_ref,
    second_any,
    mess_ref,
    grad_1_ref,
    grad_y_ref,
    second_mat,
    wide,
    grad_y,
    grad_1,
    sems,
):
    copy = pltpu.make_async_copy(second_any, second_mat, sems.at[0])
    copy.start()
    left = half_lanes(64)
    edge = half_lanes(16)
    wide[0:16, :] = jnp.zeros((16, 1024), F32)
    wide[144:160, :] = jnp.zeros((16, 1024), F32)
    for pair in range(8):
        lanes = slice(128 * pair, 128 * pair + 128)
        one = back_ref[2 * pair, 0:64, :].astype(F32)
        two = back_ref[2 * pair + 1, 0:64, :].astype(F32)
        wide[16:80, lanes] = jnp.where(left, one, swap(two))
        wide[80:144, lanes] = jnp.where(left, swap(one), two)
        one = back_ref[2 * pair, 64:80, :].astype(F32)
        two = back_ref[2 * pair + 1, 64:80, :].astype(F32)
        wide[13:16, lanes] = jnp.where(edge, one, swap(two))[0:3]
        wide[144:147, lanes] = jnp.where(edge, swap(one), two)[0:3]
    near, far = left_ref[...].astype(F32), right_ref[...].astype(F32)
    for row in range(3):
        for half in range(2):
            lanes = slice(512 * half, 512 * half + 512)
            source = 12 + 2 * row + half
            wide[13 + row : 14 + row, lanes] = (
                wide[13 + row : 14 + row, lanes] + near[source : source + 1, :]
            )
            wide[144 + row : 145 + row, lanes] = (
                wide[144 + row : 145 + row, lanes] + far[source : source + 1, :]
            )
    wide[16:144, :] = wide[16:144, :] + track_ref[...].astype(F32)
    wide[8:152, :] = wide[8:152, :] * slope_2_ref[...]
    for target in range(8):
        mess_ref[target, 144:288, :] = wide[8:152, 128 * target : 128 * target + 128].astype(BF)
    copy.wait()
    pooled = jnp.zeros((144, 512), F32)
    for k in range(5):
        pooled = pooled + dot(
            wide[10 - k + 0 : 154 - k, :].astype(BF),
            second_mat[512 * k : 512 * k + 512, :],
            ((1,), (1,)),
        )
    pooled = 0.5 * pooled
    for tile in range(4):
        lanes = slice(128 * tile, 128 * tile + 128)
        grad_y[pl.ds(288 * tile, 144, 2), :] = pooled[:, lanes]
        grad_y[pl.ds(288 * tile + 1, 144, 2), :] = pooled[:, lanes]
        value = grad_y[288 * tile : 288 * tile + 288, :]
        grad_y_ref[:, lanes] = value[16:272]
        value = value * slope_1_ref[:, lanes]
        grad_1[:, lanes] = value
        grad_1_ref[:, lanes] = value.astype(BF)
    left = half_lanes(144)
    for pair in range(4):
        lanes = slice(128 * pair, 128 * pair + 128)
        one = grad_1[8:152, lanes]
        two = grad_1[136:280, lanes]
        mess_ref[2 * pair, 0:144, :] = jnp.where(left, one, swap(two)).astype(BF)
        mess_ref[2 * pair + 1, 0:144, :] = jnp.where(left, swap(one), two).astype(BF)


def backward_part(back, track, left, right, slope_first, slope_second, w_second):
    return pl.pallas_call(
        backward_kernel,
        out_shape=[
            jax.ShapeDtypeStruct((8, 288, 128), BF),
            jax.ShapeDtypeStruct((288, 512), BF),
            jax.ShapeDtypeStruct((256, 512), F32),
        ],
        in_specs=[VMEM] * 6 + [ANY],
        out_specs=[VMEM] * 3,
        scratch_shapes=[
            pltpu.VMEM((2560, 1024), BF),
            pltpu.VMEM((160, 1024), F32),
            pltpu.VMEM((1152, 128), F32),
            pltpu.VMEM((288, 512), F32),
            pltpu.SemaphoreType.DMA((1,)),
        ],
        compiler_params=pltpu.CompilerParams(vmem_limit_bytes=24 * MEBI),
        cost_estimate=pl.CostEstimate(
            flops=8 * 10**8, bytes_accessed=10 * 10**6, transcendentals=0
        ),
        name="backward",
    )(back, track, left, right, slope_first, slope_second, w_second.reshape(2560, 1024))


def input_part(grad_y, grad_first_pre, w_first):
    spread = sum(dot(grad_first_pre[18 - k : 274 - k], w_first[k], ((1,), (1,))) for k in range(5))
    return (grad_y + spread).astype(BF)


def term_kernel(dp_ref, *refs):
    own_ref, other_ref, got_ref, head_ref, out_ref = refs[:5]
    part_scr, wide_1, wide_2, sum_1, sum_2, mess = refs[5:]
    columns = [(own_ref, other_ref)[step % 2].at[step // 2] for step in range(8)]
    left = half_lanes(128)
    for step in range(8):
        part_scr[...] = got_ref[dp_ref[0] ^ step].astype(F32)
        taps = [part_scr[10 - k : 138 - k, :] for k in range(5)]
        for k in range(5):
            wide_2[128 * step : 128 * step + 128, 128 * k : 128 * k + 128] = part_scr[
                154 - k : 282 - k, :
            ].astype(BF)
        top = [
            jnp.where(left, taps[0], swap(taps[1])),
            jnp.where(left, taps[2], swap(taps[3])),
            taps[4],
        ]
        low = [
            jnp.where(left, swap(taps[0]), taps[1]),
            jnp.where(left, swap(taps[2]), taps[3]),
            swap(taps[4]),
        ]
        for place in range(3):
            lanes = slice(128 * place, 128 * place + 128)
            wide_1[256 * step : 256 * step + 128, lanes] = top[place].astype(BF)
            wide_1[256 * step + 128 : 256 * step + 256, lanes] = low[place].astype(BF)
    lefts = jnp.concatenate([ref[:, 0:256] for ref in columns], axis=1)
    first = dot(lefts, wide_1[...])
    lefts = jnp.concatenate([ref[:, 256:384] for ref in columns], axis=1)
    second = dot(lefts, wide_2[...])
    left = half_lanes(512)
    for k in range(5):
        sum_2[512 * k : 512 * k + 512, :] = second[:, 128 * k : 128 * k + 128]
        tile = first[:, 128 * (k // 2) : 128 * (k // 2) + 128]
        turned = swap(tile)
        sum_1[512 * k : 512 * k + 512, :] = (
            jnp.where(left, tile, turned) if k % 2 == 0 else jnp.where(left, turned, tile)
        )
    left = half_lanes(10)
    head = jnp.concatenate([head_ref[...], jnp.zeros((1, 128), F32)], axis=0)
    for owner in range(128):
        row = 20 * owner
        mess[0:20, :] = sum_2[row : row + 20, :]
        mess[20:30, :] = jnp.where(left, sum_1[row : row + 10, :], sum_1[row + 10 : row + 20, :])
        mess[30:32, :] = head
        out_ref[owner] = mess[...].astype(BF)


def term_part(own, other, got, head_row, dp_index):
    return pl.pallas_call(
        term_kernel,
        out_shape=jax.ShapeDtypeStruct((128, 32, 128), BF),
        in_specs=[SMEM] + [VMEM] * 4,
        out_specs=VMEM,
        scratch_shapes=[
            pltpu.VMEM((288, 128), F32),
            pltpu.VMEM((2048, 384), BF),
            pltpu.VMEM((1024, 640), BF),
            pltpu.VMEM((2560, 128), F32),
            pltpu.VMEM((2560, 128), F32),
            pltpu.VMEM((32, 128), F32),
        ],
        compiler_params=pltpu.CompilerParams(vmem_limit_bytes=24 * MEBI),
        cost_estimate=pl.CostEstimate(flops=3 * 10**9, bytes_accessed=5 * 10**6, transcendentals=0),
        name="terms",
    )(jnp.reshape(dp_index, (1,)), own, other, got, head_row)


def per_device(
    seq_in, w_first, w_second, head_vec, track_cot, donor_pos, acceptor_pos, pair_cot, live_pairs
):
    seq_index = lax.axis_index("seq")
    seq_cell = jnp.reshape(seq_index, (1,))
    dp_index = lax.axis_index("dp")
    inputs, track = seq_in[0], track_cot[0]
    left, right = edges(inputs, track, 16)
    message, pooled, slope_first, slope_second = forward_part(
        seq_cell, live_pairs[0], inputs, left, right, donor_pos, acceptor_pos, pair_cot,
        w_first, w_second,
    )
    got = lax.all_to_all(message, "seq", 0, 0, tiled=True)

    mine = jnp.concatenate([inputs, pooled], axis=0).T
    own = jnp.stack(
        [mine]
        + [lax.ppermute(mine, "dp", [(i, i ^ step) for i in range(8)]) for step in (2, 4, 6)]
    )
    sent, head_row = pair_part(seq_cell, got, head_vec)
    own, sent = lax.optimization_barrier((own, sent))
    other = lax.ppermute(own, "dp", [(i, i ^ 1) for i in range(8)])
    back = lax.all_to_all(sent, "seq", 0, 0, tiled=True)
    back, other = lax.optimization_barrier((back, other))
    pieces = jnp.sum(back[:, 68:72].astype(F32), axis=0)
    pieces = (pieces[:2] + pieces[2:]).reshape(256)
    live_mine = jnp.arange(16, dtype=jnp.int32) < live_pairs[0, 0]
    scores = jnp.where(
        live_mine, lax.dynamic_slice_in_dim(pieces, seq_index * 16, 16) * (1024 ** -0.5), 0.0
    )

    message, grad_1, grad_y = backward_part(
        back, track, left, right, slope_first, slope_second, w_second
    )
    grads = lax.all_to_all(message, "dp", 0, 0, tiled=True)
    grad_input = input_part(grad_y, grad_1, w_first)
    terms = term_part(own, other, grads, head_row, dp_index)
    final = lax.all_to_all(terms, ("dp", "seq"), 0, 0, tiled=True).reshape(8, 16, 32, 128)
    summed = jnp.sum(final[:, :, :30].astype(F32), axis=1)
    out_second = summed[:, :20].transpose(1, 0, 2).reshape(20, 1024)
    out_first = summed[:, 20:].reshape(8, 10, 2, 64).transpose(2, 1, 0, 3).reshape(20, 512)
    head = jnp.sum(final[:, :, 30].astype(F32), axis=0)
    grad_head = (head[:, :64] + head[:, 64:]).reshape(1024)
    return (scores[None], out_first, out_second, grad_input[None], grad_head)


def solution(mesh):
    in_specs = (
        P("dp", "seq", None),
        P(),
        P(),
        P(),
        P("dp", "seq", None),
        P("dp", "seq"),
        P("dp", "seq"),
        P("dp", "seq"),
        P("dp", "seq"),
    )
    out_specs = (
        P("dp", "seq"),
        P(("dp", "seq"), None),
        P(("dp", "seq"), None),
        P("dp", "seq", None),
        P(),
    )
    return jax.shard_map(
        per_device, mesh=mesh, in_specs=in_specs, out_specs=out_specs, check_vma=False
    )
```

```python
import jax
import jax.numpy as jnp
from jax import lax
from jax.experimental import pallas as pl
from jax.experimental.pallas import tpu as pltpu
from jax.sharding import PartitionSpec as P

BF = jnp.bfloat16
F32 = jnp.float32
ROOT = 0.7978845608028654
CUBE = 0.044715


def gelu_both(pre):
    square = pre * pre
    bent = jnp.tanh(ROOT * pre * (1.0 + CUBE * square))
    half = 0.5 * (1.0 + bent)
    slope = half + 0.5 * pre * (1.0 - bent * bent) * (ROOT * (1.0 + 3.0 * CUBE * square))
    return pre * half, slope


def dot(left, right, dims=((1,), (0,))):
    return lax.dot_general(left, right, (dims, ((), ())), preferred_element_type=F32)


VMEM = pl.BlockSpec(memory_space=pltpu.VMEM)
SMEM = pl.BlockSpec(memory_space=pltpu.SMEM)
HBM = pl.BlockSpec(memory_space=pltpu.HBM)
MEBI = 1024 * 1024
GRANT = 56


def rounded(value):
    return value.astype(BF).astype(F32)


def half_lanes(rows):
    return lax.broadcasted_iota(jnp.int32, (rows, 128), 1) < 64


def swap(value):
    return pltpu.roll(value, 64, 1)


def started(moves, sems):
    copies = []
    for place, (source, target) in enumerate(moves):
        copies.append(pltpu.make_async_copy(source, target, sems.at[place]))
        copies[place].start()
    return copies


def wait_for(copies):
    for copy in copies:
        copy.wait()


def edge_kernel(inputs_hbm, track_hbm, last_hbm, first_hbm, rows_scr, track_scr, out_scr, sems):
    wait_for(
        started(
            [
                (inputs_hbm.at[pl.ds(240, 16)], rows_scr.at[0]),
                (inputs_hbm.at[pl.ds(0, 16)], rows_scr.at[1]),
                (track_hbm.at[pl.ds(112, 16)], track_scr.at[0]),
                (track_hbm.at[pl.ds(0, 16)], track_scr.at[1]),
            ],
            sems,
        )
    )
    blank = jnp.zeros((14, 512), F32)
    for side in range(2):
        start, skip = ((4, 13), (0, 0))[side]
        track = track_scr[side].astype(F32)
        pieces = [rows_scr[side].astype(F32)[start : start + 12]]
        for row in range(skip, skip + 3):
            pieces += [track[row : row + 1, :512], track[row : row + 1, 512:]]
        out_scr[side] = jnp.concatenate(pieces + [blank], axis=0).astype(BF)
    wait_for(started([(out_scr.at[0], last_hbm), (out_scr.at[1], first_hbm)], sems))


def edges(inputs, track, count):
    last, first = pl.pallas_call(
        edge_kernel,
        out_shape=[jax.ShapeDtypeStruct((32, 512), BF)] * 2,
        in_specs=[HBM] * 2,
        out_specs=[HBM] * 2,
        scratch_shapes=[
            pltpu.VMEM((2, 16, 512), BF),
            pltpu.VMEM((2, 16, 1024), BF),
            pltpu.VMEM((2, 32, 512), BF),
            pltpu.SemaphoreType.DMA((4,)),
        ],
        compiler_params=pltpu.CompilerParams(vmem_limit_bytes=GRANT * MEBI),
        name="edges",
    )(inputs, track)
    forward = [(i, i + 1) for i in range(count - 1)]
    backward = [(i + 1, i) for i in range(count - 1)]
    return lax.ppermute(last, "seq", forward), lax.ppermute(first, "seq", backward)


def forward_kernel(seq_ref, live_ref, *refs):
    sources, outs, held, staged, work = refs[:8], refs[8:12], refs[12:20], refs[20:24], refs[24:]
    inputs_ref, left_ref, right_ref, first_mat, second_mat, donor_ref, accept_ref, cot_ref = held
    mess_ref, pooled_ref, slope_1_ref, slope_2_ref = staged
    ext, act_scr, wide, sems, out_sems = work
    copies = started(list(zip(sources, held)), sems)

    def send(place):
        copy = pltpu.make_async_copy(staged[place], outs[place], out_sems.at[place])
        copy.start()
        return copy

    seq_index = seq_ref[0]
    ext[0:32, :] = jnp.zeros((32, 512), F32)
    ext[288:320, :] = jnp.zeros((32, 512), F32)
    wait_for(copies[:3])
    ext[20:32, :] = left_ref[0:12, :].astype(F32)
    ext[32:288, :] = inputs_ref[...].astype(F32)
    ext[288:300, :] = right_ref[0:12, :].astype(F32)
    taps = jnp.concatenate([ext[14 + k : 302 + k, :].astype(BF) for k in range(5)], axis=1)
    copies[3].wait()
    pre = dot(taps, first_mat[...])
    act, slope = gelu_both(pre)
    spot = seq_index * 256 - 16 + lax.broadcasted_iota(jnp.int32, (288, 1), 0)
    slope_1_ref[...] = jnp.where((spot >= 0) & (spot < 4096), slope, 0.0)
    sent = [send(2)]
    y_first = ext[16:304, :] + act
    for tile in range(4):
        lanes = slice(128 * tile, 128 * tile + 128)
        act_scr[288 * tile : 288 * tile + 288, :] = y_first[:, lanes]
        even = act_scr[pl.ds(288 * tile, 144, 2), :]
        wide[8:152, lanes] = even + act_scr[pl.ds(288 * tile + 1, 144, 2), :]
    spot = seq_index * 128 - 8 + lax.broadcasted_iota(jnp.int32, (144, 1), 0)
    pooled = jnp.where((spot >= 0) & (spot < 2048), 0.5 * wide[8:152, :], 0.0)
    wide[0:8, :] = jnp.zeros((8, 512), F32)
    wide[152:160, :] = jnp.zeros((8, 512), F32)
    wide[8:152, :] = pooled
    pooled_ref[...] = wide[16:144, :].astype(BF)
    sent.append(send(1))
    taps = jnp.concatenate([wide[6 + k : 150 + k, :].astype(BF) for k in range(5)], axis=1)
    copies[4].wait()
    pre = dot(taps, second_mat[...])
    act, slope = gelu_both(pre)
    slope_2_ref[...] = slope
    sent.append(send(3))
    wait_for(copies[5:])

    same = lax.broadcasted_iota(jnp.int32, (16, 16), 0) == lax.broadcasted_iota(
        jnp.int32, (16, 16), 1
    )

    def column(row):
        return jnp.sum(jnp.where(same, row, 0.0), axis=1, keepdims=True)

    donor, accept = donor_ref[...], accept_ref[...]
    live = lax.broadcasted_iota(jnp.int32, (1, 16), 1) < live_ref[0]
    weight = column(jnp.where(live, cot_ref[...], 0.0) * (1024 ** -0.5))
    lane = lax.broadcasted_iota(jnp.int32, (16, 128), 1)
    info = jnp.zeros((16, 128), F32)
    for place, value in enumerate(
        [
            column((donor >> 6).astype(F32)),
            column((donor & 63).astype(F32)),
            column((accept >> 6).astype(F32)),
            column((accept & 63).astype(F32)),
            weight,
            weight - rounded(weight),
        ]
    ):
        info = jnp.where(lane == place, value, info)
    info = info.astype(BF)
    left = half_lanes(64)
    for pair in range(8):
        top = act[8:72, 128 * pair : 128 * pair + 128]
        low = act[72:136, 128 * pair : 128 * pair + 128]
        mess_ref[2 * pair, 0:64, :] = jnp.where(left, top, swap(low)).astype(BF)
        mess_ref[2 * pair + 1, 0:64, :] = jnp.where(left, swap(top), low).astype(BF)
    for target in range(16):
        mess_ref[target, 64:80, :] = info
    sent.append(send(0))
    wait_for(sent)


def forward_part(seq_index, live, inputs, left, right, donor, accept, cot, w_first, w_second):
    return pl.pallas_call(
        forward_kernel,
        out_shape=[
            jax.ShapeDtypeStruct((16, 80, 128), BF),
            jax.ShapeDtypeStruct((128, 512), BF),
            jax.ShapeDtypeStruct((288, 512), F32),
            jax.ShapeDtypeStruct((144, 1024), F32),
        ],
        in_specs=[SMEM, SMEM] + [HBM] * 8,
        out_specs=[HBM] * 4,
        scratch_shapes=[
            pltpu.VMEM((256, 512), BF),
            pltpu.VMEM((32, 512), BF),
            pltpu.VMEM((32, 512), BF),
            pltpu.VMEM((2560, 512), BF),
            pltpu.VMEM((2560, 1024), BF),
            pltpu.VMEM((1, 16), jnp.int32),
            pltpu.VMEM((1, 16), jnp.int32),
            pltpu.VMEM((1, 16), F32),
            pltpu.VMEM((16, 80, 128), BF),
            pltpu.VMEM((128, 512), BF),
            pltpu.VMEM((288, 512), F32),
            pltpu.VMEM((144, 1024), F32),
            pltpu.VMEM((320, 512), F32),
            pltpu.VMEM((1152, 128), F32),
            pltpu.VMEM((160, 512), F32),
            pltpu.SemaphoreType.DMA((8,)),
            pltpu.SemaphoreType.DMA((4,)),
        ],
        compiler_params=pltpu.CompilerParams(vmem_limit_bytes=GRANT * MEBI),
        cost_estimate=pl.CostEstimate(
            flops=15 * 10**8, bytes_accessed=10 * 10**6, transcendentals=3 * 10**5
        ),
        name="forward",
    )(
        seq_index, live, inputs, left, right,
        w_first.reshape(2560, 512), w_second.reshape(2560, 1024), donor, accept, cot,
    )


def pair_kernel(
    seq_ref, got_hbm, head_hbm, sent_hbm, term_hbm, got_ref, head_ref, sent_ref, term_ref, sems
):
    wait_for(started([(got_hbm, got_ref), (head_hbm, head_ref)], sems))
    seq_index = seq_ref[0]
    head_row = head_ref[pl.ds(seq_index // 2, 1), :]
    head_row = jnp.where(seq_index % 2 == 0, head_row, swap(head_row))[:, :64]
    flat = jnp.concatenate([got_ref[i] for i in range(16)], axis=0)
    info = jnp.concatenate([got_ref[i, 64:80, :].astype(F32) for i in range(16)], axis=0)
    donor = (info[:, 0:1] * 64.0 + info[:, 1:2]).astype(jnp.int32)
    accept = (info[:, 2:3] * 64.0 + info[:, 3:4]).astype(jnp.int32)
    weight = info[:, 4:5] + info[:, 5:6]
    spots = jnp.concatenate([donor, accept], axis=0)
    row_of = (spots >> 7) * 80 + (spots & 63)
    pick = (row_of == lax.broadcasted_iota(jnp.int32, (512, 1280), 1)).astype(F32).astype(BF)
    rows = dot(pick, flat)
    rows = jnp.where((spots & 127) < 64, rows, swap(rows))[:, :64]
    donor_rows, accept_rows = rows[:256], rows[256:]
    both = donor_rows * accept_rows
    partial = jnp.sum(both * head_row, axis=1, keepdims=True)
    term = jnp.sum(weight * both, axis=0, keepdims=True)
    term_high = rounded(term)
    term_ref[...] = jnp.concatenate([term_high, term - term_high], axis=1)
    copies = [pltpu.make_async_copy(term_ref, term_hbm, sems.at[4])]
    copies[0].start()
    scaled = weight * head_row
    grads = jnp.concatenate([scaled * accept_rows, scaled * donor_rows], axis=0)
    blank = jnp.zeros((512, 64), F32)
    grads = jnp.concatenate(
        [
            jnp.concatenate([grads, blank], axis=1),
            jnp.concatenate([blank, grads], axis=1),
        ],
        axis=0,
    ).astype(BF)
    lane = lax.broadcasted_iota(jnp.int32, (256, 128), 1)
    turned = jnp.where(
        lane == 0,
        donor.astype(F32),
        jnp.where(lane == 1, accept.astype(F32), jnp.where(lane == 2, partial, 0.0)),
    ).T
    spot_row = jnp.concatenate([turned[0:1, :], turned[1:2, :]], axis=1).astype(jnp.int32)
    high = rounded(turned[2:3, :])
    rest = turned[2:3, :] - high
    extra = jnp.concatenate(
        [
            jnp.zeros((4, 128), F32),
            high[:, :128],
            high[:, 128:],
            rest[:, :128],
            rest[:, 128:],
            jnp.zeros((8, 128), F32),
        ],
        axis=0,
    )
    index = lax.broadcasted_iota(jnp.int32, (80, 1), 0)
    low_edge = jnp.where(index < 67, index - 67, -4096)
    high_edge = jnp.where(index < 67, index + 64, -4096)
    low_row = jnp.where(index < 64, index, low_edge)
    high_row = jnp.where(index < 64, index + 64, high_edge)
    for target in range(16):
        base = 128 * target
        low_pick = (low_row + base == spot_row).astype(F32)
        high_pick = (high_row + base == spot_row).astype(F32)
        piece = dot(jnp.concatenate([low_pick, high_pick], axis=1).astype(BF), grads)
        sent_ref[target, 0:64, :] = piece[0:64].astype(BF)
        sent_ref[target, 64:80, :] = (piece[64:80] + extra).astype(BF)
        if target % 4 == 3:
            part = pl.ds(target - 3, 4)
            copies.append(
                pltpu.make_async_copy(sent_ref.at[part], sent_hbm.at[part], sems.at[target // 4])
            )
            copies[-1].start()
    wait_for(copies)


def pair_part(seq_index, got, head_vec):
    return pl.pallas_call(
        pair_kernel,
        out_shape=[
            jax.ShapeDtypeStruct((16, 80, 128), BF),
            jax.ShapeDtypeStruct((1, 128), F32),
        ],
        in_specs=[SMEM, HBM, HBM],
        out_specs=[HBM] * 2,
        scratch_shapes=[
            pltpu.VMEM((16, 80, 128), BF),
            pltpu.VMEM((8, 128), F32),
            pltpu.VMEM((16, 80, 128), BF),
            pltpu.VMEM((1, 128), F32),
            pltpu.SemaphoreType.DMA((5,)),
        ],
        compiler_params=pltpu.CompilerParams(vmem_limit_bytes=GRANT * MEBI),
        cost_estimate=pl.CostEstimate(
            flops=5 * 10**8, bytes_accessed=10**6, transcendentals=0
        ),
        name="pairs",
    )(seq_index, got, head_vec.reshape(8, 128))


def backward_kernel(seq_ref, live_ref, *refs):
    sources, second_hbm, outs = refs[:6], refs[6], refs[7:11]
    held, second_mat, staged = refs[11:17], refs[17], refs[18:22]
    back_ref, track_ref, left_ref, right_ref, slope_2_ref, slope_1_ref = held
    mess_ref, grad_1_ref, grad_y_ref, scores_ref = staged
    wide, grad_y, grad_1, sems, out_sems = refs[22:]
    parts = [pl.ds(512 * k, 512) for k in range(5)]
    copies = started(
        list(zip(sources, held)) + [(second_hbm.at[part], second_mat.at[part]) for part in parts],
        sems,
    )

    def send(place, part, sem):
        copy = pltpu.make_async_copy(part(staged[place]), part(outs[place]), out_sems.at[sem])
        copy.start()
        return copy

    def all_of(ref):
        return ref

    left = half_lanes(64)
    edge = half_lanes(16)
    wide[0:16, :] = jnp.zeros((16, 1024), F32)
    wide[144:160, :] = jnp.zeros((16, 1024), F32)
    copies[0].wait()
    for pair in range(8):
        lanes = slice(128 * pair, 128 * pair + 128)
        one = back_ref[2 * pair, 0:64, :].astype(F32)
        two = back_ref[2 * pair + 1, 0:64, :].astype(F32)
        wide[16:80, lanes] = jnp.where(left, one, swap(two))
        wide[80:144, lanes] = jnp.where(left, swap(one), two)
        one = back_ref[2 * pair, 64:80, :].astype(F32)
        two = back_ref[2 * pair + 1, 64:80, :].astype(F32)
        wide[13:16, lanes] = jnp.where(edge, one, swap(two))[0:3]
        wide[144:147, lanes] = jnp.where(edge, swap(one), two)[0:3]
    wait_for(copies[1:4])
    near, far = left_ref[...].astype(F32), right_ref[...].astype(F32)
    for row in range(3):
        for half in range(2):
            lanes = slice(512 * half, 512 * half + 512)
            source = 12 + 2 * row + half
            wide[13 + row : 14 + row, lanes] = (
                wide[13 + row : 14 + row, lanes] + near[source : source + 1, :]
            )
            wide[144 + row : 145 + row, lanes] = (
                wide[144 + row : 145 + row, lanes] + far[source : source + 1, :]
            )
    wide[16:144, :] = wide[16:144, :] + track_ref[...].astype(F32)
    copies[4].wait()
    wide[8:152, :] = wide[8:152, :] * slope_2_ref[...]
    for target in range(8):
        mess_ref[target, 144:288, :] = wide[8:152, 128 * target : 128 * target + 128].astype(BF)
    sent = [send(0, lambda ref: ref.at[:, pl.ds(144, 144)], 0)]
    pooled = jnp.zeros((144, 512), F32)
    for k in range(5):
        copies[6 + k].wait()
        pooled = pooled + dot(
            wide[10 - k : 154 - k, :].astype(BF),
            second_mat[512 * k : 512 * k + 512, :],
            ((1,), (1,)),
        )
    pooled = 0.5 * pooled
    copies[5].wait()
    for tile in range(4):
        lanes = slice(128 * tile, 128 * tile + 128)
        grad_y[pl.ds(288 * tile, 144, 2), :] = pooled[:, lanes]
        grad_y[pl.ds(288 * tile + 1, 144, 2), :] = pooled[:, lanes]
        value = grad_y[288 * tile : 288 * tile + 288, :]
        grad_y_ref[:, lanes] = value[16:272]
        value = value * slope_1_ref[:, lanes]
        grad_1[:, lanes] = value
        grad_1_ref[:, lanes] = value.astype(BF)
    sent += [send(1, all_of, 1), send(2, all_of, 2)]
    left = half_lanes(144)
    for pair in range(4):
        lanes = slice(128 * pair, 128 * pair + 128)
        one = grad_1[8:152, lanes]
        two = grad_1[136:280, lanes]
        mess_ref[2 * pair, 0:144, :] = jnp.where(left, one, swap(two)).astype(BF)
        mess_ref[2 * pair + 1, 0:144, :] = jnp.where(left, swap(one), two).astype(BF)
    sent.append(send(0, lambda ref: ref.at[:, pl.ds(0, 144)], 3))
    total = jnp.zeros((16, 128), F32)
    for source in range(16):
        total = total + back_ref[source, 64:80, :].astype(F32)
    seq_index = seq_ref[0]
    row = jnp.where(seq_index < 8, total[4:5] + total[6:7], total[5:6] + total[7:8])
    row = pltpu.roll(row, 128 - 16 * (seq_index % 8), 1)[:, :16]
    live = lax.broadcasted_iota(jnp.int32, (1, 16), 1) < live_ref[0]
    scores_ref[...] = jnp.where(live, row * (1024 ** -0.5), 0.0)
    sent.append(send(3, all_of, 4))
    wait_for(sent)


def backward_part(seq_cell, live, back, track, left, right, slope_first, slope_second, w_second):
    return pl.pallas_call(
        backward_kernel,
        out_shape=[
            jax.ShapeDtypeStruct((8, 288, 128), BF),
            jax.ShapeDtypeStruct((288, 512), BF),
            jax.ShapeDtypeStruct((256, 512), F32),
            jax.ShapeDtypeStruct((1, 16), F32),
        ],
        in_specs=[SMEM] * 2 + [HBM] * 7,
        out_specs=[HBM] * 4,
        scratch_shapes=[
            pltpu.VMEM((16, 80, 128), BF),
            pltpu.VMEM((128, 1024), BF),
            pltpu.VMEM((32, 512), BF),
            pltpu.VMEM((32, 512), BF),
            pltpu.VMEM((144, 1024), F32),
            pltpu.VMEM((288, 512), F32),
            pltpu.VMEM((2560, 1024), BF),
            pltpu.VMEM((8, 288, 128), BF),
            pltpu.VMEM((288, 512), BF),
            pltpu.VMEM((256, 512), F32),
            pltpu.VMEM((1, 16), F32),
            pltpu.VMEM((160, 1024), F32),
            pltpu.VMEM((1152, 128), F32),
            pltpu.VMEM((288, 512), F32),
            pltpu.SemaphoreType.DMA((11,)),
            pltpu.SemaphoreType.DMA((5,)),
        ],
        compiler_params=pltpu.CompilerParams(vmem_limit_bytes=GRANT * MEBI),
        cost_estimate=pl.CostEstimate(
            flops=8 * 10**8, bytes_accessed=10 * 10**6, transcendentals=0
        ),
        name="backward",
    )(
        seq_cell, live, back, track, left, right, slope_second, slope_first,
        w_second.reshape(2560, 1024),
    )


def input_part(grad_y, grad_first_pre, w_first):
    spread = sum(dot(grad_first_pre[18 - k : 274 - k], w_first[k], ((1,), (1,))) for k in range(5))
    return (grad_y + spread).astype(BF)


def term_kernel(dp_ref, *refs):
    sources, out_hbm, held, out_ref = refs[:10], refs[10], refs[11:21], refs[21]
    part_scr, wide_1, wide_2, sum_1, sum_2, mess, sems, out_sems = refs[22:]
    got_ref, head_ref, columns = held[0], held[1], held[2:]
    copies = started(list(zip(sources, held)), sems)
    copies[0].wait()
    left = half_lanes(128)
    for step in range(8):
        part_scr[...] = got_ref[dp_ref[0] ^ step].astype(F32)
        taps = [part_scr[10 - k : 138 - k, :] for k in range(5)]
        for k in range(5):
            wide_2[128 * step : 128 * step + 128, 128 * k : 128 * k + 128] = part_scr[
                154 - k : 282 - k, :
            ].astype(BF)
        top = [
            jnp.where(left, taps[0], swap(taps[1])),
            jnp.where(left, taps[2], swap(taps[3])),
            taps[4],
        ]
        low = [
            jnp.where(left, swap(taps[0]), taps[1]),
            jnp.where(left, swap(taps[2]), taps[3]),
            swap(taps[4]),
        ]
        for place in range(3):
            lanes = slice(128 * place, 128 * place + 128)
            wide_1[256 * step : 256 * step + 128, lanes] = top[place].astype(BF)
            wide_1[256 * step + 128 : 256 * step + 256, lanes] = low[place].astype(BF)
    wait_for(copies[1:])
    lefts = jnp.concatenate([ref[:, 0:256] for ref in columns], axis=1)
    first = dot(lefts, wide_1[...])
    lefts = jnp.concatenate([ref[:, 256:384] for ref in columns], axis=1)
    second = dot(lefts, wide_2[...])
    left = half_lanes(512)
    for k in range(5):
        sum_2[512 * k : 512 * k + 512, :] = second[:, 128 * k : 128 * k + 128]
        tile = first[:, 128 * (k // 2) : 128 * (k // 2) + 128]
        turned = swap(tile)
        sum_1[512 * k : 512 * k + 512, :] = (
            jnp.where(left, tile, turned) if k % 2 == 0 else jnp.where(left, turned, tile)
        )
    left = half_lanes(10)
    head = jnp.concatenate([head_ref[...], jnp.zeros((1, 128), F32)], axis=0)
    sent = []
    for owner in range(128):
        row = 20 * owner
        mess[0:20, :] = sum_2[row : row + 20, :]
        mess[20:30, :] = jnp.where(left, sum_1[row : row + 10, :], sum_1[row + 10 : row + 20, :])
        mess[30:32, :] = head
        out_ref[owner] = mess[...].astype(BF)
        if owner % 32 == 31:
            part = pl.ds(owner - 31, 32)
            sent.append(
                pltpu.make_async_copy(out_ref.at[part], out_hbm.at[part], out_sems.at[owner // 32])
            )
            sent[-1].start()
    wait_for(sent)


def term_part(columns, got, head_row, dp_index):
    return pl.pallas_call(
        term_kernel,
        out_shape=jax.ShapeDtypeStruct((128, 32, 128), BF),
        in_specs=[SMEM] + [HBM] * 10,
        out_specs=HBM,
        scratch_shapes=[
            pltpu.VMEM((8, 288, 128), BF),
            pltpu.VMEM((1, 128), F32),
        ]
        + [pltpu.VMEM((512, 384), BF)] * 8
        + [
            pltpu.VMEM((128, 32, 128), BF),
            pltpu.VMEM((288, 128), F32),
            pltpu.VMEM((2048, 384), BF),
            pltpu.VMEM((1024, 640), BF),
            pltpu.VMEM((2560, 128), F32),
            pltpu.VMEM((2560, 128), F32),
            pltpu.VMEM((32, 128), F32),
            pltpu.SemaphoreType.DMA((10,)),
            pltpu.SemaphoreType.DMA((4,)),
        ],
        compiler_params=pltpu.CompilerParams(vmem_limit_bytes=GRANT * MEBI),
        cost_estimate=pl.CostEstimate(flops=3 * 10**9, bytes_accessed=5 * 10**6, transcendentals=0),
        name="terms",
    )(jnp.reshape(dp_index, (1,)), got, head_row, *columns)


def final_kernel(final_hbm, first_ref, second_ref, head_ref, final_ref, sems):
    parts = [pl.ds(32 * i, 32) for i in range(4)]
    copies = started([(final_hbm.at[part], final_ref.at[part]) for part in parts], sems)
    left = half_lanes(10)
    for pair in range(4):
        copies[pair].wait()
        sums = []
        for block in (2 * pair, 2 * pair + 1):
            total = final_ref[16 * block].astype(F32)
            for source in range(1, 16):
                total = total + final_ref[16 * block + source].astype(F32)
            second_ref[:, 128 * block : 128 * block + 128] = total[0:20]
            sums.append(total[20:30])
        one, two = sums
        lanes = slice(128 * pair, 128 * pair + 128)
        first_ref[0:10, lanes] = jnp.where(left, one, swap(two))
        first_ref[10:20, lanes] = jnp.where(left, swap(one), two)
    left = half_lanes(16)
    for pair in range(8):
        sums = []
        for source in (2 * pair, 2 * pair + 1):
            total = final_ref[source, 16:32, :].astype(F32)
            for block in range(1, 8):
                total = total + final_ref[16 * block + source, 16:32, :].astype(F32)
            sums.append(total + swap(total))
        head_ref[pair : pair + 1, :] = jnp.where(left, sums[0], sums[1])[14:15]


def final_part(final):
    return pl.pallas_call(
        final_kernel,
        out_shape=[
            jax.ShapeDtypeStruct((20, 512), F32),
            jax.ShapeDtypeStruct((20, 1024), F32),
            jax.ShapeDtypeStruct((8, 128), F32),
        ],
        in_specs=[HBM],
        out_specs=[VMEM] * 3,
        scratch_shapes=[pltpu.VMEM((128, 32, 128), BF), pltpu.SemaphoreType.DMA((4,))],
        compiler_params=pltpu.CompilerParams(vmem_limit_bytes=GRANT * MEBI),
        name="final",
    )(final)


def per_device(
    seq_in, w_first, w_second, head_vec, track_cot, donor_pos, acceptor_pos, pair_cot, live_pairs
):
    seq_index = lax.axis_index("seq")
    seq_cell = jnp.reshape(seq_index, (1,))
    dp_index = lax.axis_index("dp")
    inputs, track = seq_in[0], track_cot[0]
    left, right = edges(inputs, track, 16)
    message, pooled, slope_first, slope_second = forward_part(
        seq_cell, live_pairs[0], inputs, left, right, donor_pos, acceptor_pos, pair_cot,
        w_first, w_second,
    )
    got = lax.all_to_all(message, "seq", 0, 0, tiled=True)

    mine = jnp.concatenate([inputs, pooled], axis=0).T

    def passed(value, step):
        return lax.ppermute(value, "dp", [(i, i ^ step) for i in range(8)])

    own = [mine] + [passed(mine, step) for step in (2, 4, 6)]
    sent, head_row = pair_part(seq_cell, got, head_vec)
    back = lax.all_to_all(sent, "seq", 0, 0, tiled=True)
    back, *own = lax.optimization_barrier((back, *own))
    message, grad_1, grad_y, scores = backward_part(
        seq_cell, live_pairs[0], back, track, left, right, slope_first, slope_second, w_second
    )
    other = [passed(value, 1) for value in own]
    columns = [(own, other)[step % 2][step // 2] for step in range(8)]
    grads = lax.all_to_all(message, "dp", 0, 0, tiled=True)
    grad_input = input_part(grad_y, grad_1, w_first)
    terms = term_part(columns, grads, head_row, dp_index)
    final = lax.all_to_all(terms, ("dp", "seq"), 0, 0, tiled=True)
    out_first, out_second, grad_head = final_part(final)
    return (scores, out_first, out_second, grad_input[None], grad_head.reshape(1024))


def solution(mesh):
    in_specs = (
        P("dp", "seq", None),
        P(),
        P(),
        P(),
        P("dp", "seq", None),
        P("dp", "seq"),
        P("dp", "seq"),
        P("dp", "seq"),
        P("dp", "seq"),
    )
    out_specs = (
        P("dp", "seq"),
        P(("dp", "seq"), None),
        P(("dp", "seq"), None),
        P("dp", "seq", None),
        P(),
    )
    return jax.shard_map(
        per_device, mesh=mesh, in_specs=in_specs, out_specs=out_specs, check_vma=False
    )
```

```python
import jax
import jax.numpy as jnp
from jax import lax
from jax.experimental import pallas as pl
from jax.experimental.pallas import tpu as pltpu
from jax.sharding import PartitionSpec as P

BF = jnp.bfloat16
F32 = jnp.float32
ROOT = 0.7978845608028654
CUBE = 0.044715


def gelu_both(pre):
    square = pre * pre
    bent = jnp.tanh(ROOT * pre * (1.0 + CUBE * square))
    half = 0.5 * (1.0 + bent)
    slope = half + 0.5 * pre * (1.0 - bent * bent) * (ROOT * (1.0 + 3.0 * CUBE * square))
    return pre * half, slope


def dot(left, right, dims=((1,), (0,))):
    return lax.dot_general(left, right, (dims, ((), ())), preferred_element_type=F32)


VMEM = pl.BlockSpec(memory_space=pltpu.VMEM)
SMEM = pl.BlockSpec(memory_space=pltpu.SMEM)
HBM = pl.BlockSpec(memory_space=pltpu.HBM)
ANY = pl.BlockSpec(memory_space=pl.ANY)
MEBI = 1024 * 1024


def rounded(value):
    return value.astype(BF).astype(F32)


def half_lanes(rows):
    return lax.broadcasted_iota(jnp.int32, (rows, 128), 1) < 64


def swap(value):
    return pltpu.roll(value, 64, 1)


def started(moves, sems):
    copies = []
    for place, (source, target) in enumerate(moves):
        copies.append(pltpu.make_async_copy(source, target, sems.at[place]))
        copies[place].start()
    return copies


def wait_for(copies):
    for copy in copies:
        copy.wait()


def within(rows, seam, shift, seq_index):
    row = lax.broadcasted_iota(jnp.int32, (rows, 1), 0)
    return ((row >= seam) == (row + shift >= seam)) | (seq_index != 15)


def edge_kernel(inputs_hbm, track_hbm, out_hbm, rows_scr, track_scr, out_scr, sems):
    wait_for(
        started(
            [
                (inputs_hbm.at[pl.ds(0, 32)], rows_scr),
                (track_hbm.at[pl.ds(0, 16)], track_scr),
            ],
            sems,
        )
    )
    track = track_scr[...].astype(F32)
    pieces = [rows_scr[...].astype(F32)[:24]]
    for row in range(9):
        pieces += [track[row : row + 1, :512], track[row : row + 1, 512:]]
    pieces.append(jnp.zeros((6, 512), F32))
    out_scr[...] = jnp.concatenate(pieces, axis=0).astype(BF)
    wait_for(started([(out_scr, out_hbm)], sems))


def edges(inputs, track, count):
    first = pl.pallas_call(
        edge_kernel,
        out_shape=jax.ShapeDtypeStruct((48, 512), BF),
        in_specs=[HBM] * 2,
        out_specs=HBM,
        scratch_shapes=[
            pltpu.VMEM((32, 512), BF),
            pltpu.VMEM((16, 1024), BF),
            pltpu.VMEM((48, 512), BF),
            pltpu.SemaphoreType.DMA((2,)),
        ],
        compiler_params=pltpu.CompilerParams(vmem_limit_bytes=56 * MEBI),
        name="edges",
    )(inputs, track)
    return lax.ppermute(first, "seq", [(i, (i - 1) % count) for i in range(count)])


def forward_kernel(seq_ref, live_ref, *refs):
    sources, outs, held, staged, work = refs[:7], refs[7:11], refs[11:18], refs[18:22], refs[22:]
    inputs_ref, right_ref, first_mat, second_mat, donor_ref, accept_ref, cot_ref = held
    mess_ref, mine_ref, slope_1_ref, slope_2_ref = staged
    ext, act_scr, wide, sems, out_sems = work
    copies = started(list(zip(sources, held)), sems)

    def send(place):
        copy = pltpu.make_async_copy(staged[place], outs[place], out_sems.at[place])
        copy.start()
        return copy

    seq_index = seq_ref[0]
    ext[0:32, :] = jnp.zeros((32, 512), F32)
    ext[288:320, :] = jnp.zeros((32, 512), F32)
    wait_for(copies[:2])
    ext[20:276, :] = inputs_ref[...].astype(F32)
    ext[276:300, :] = right_ref[...].astype(F32)[:24]
    taps = jnp.concatenate(
        [
            jnp.where(within(288, 260, k - 2, seq_index), ext[14 + k : 302 + k, :], 0.0).astype(BF)
            for k in range(5)
        ],
        axis=1,
    )
    copies[2].wait()
    pre = dot(taps, first_mat[...])
    act, slope = gelu_both(pre)
    slope_1_ref[...] = slope
    sent = [send(2)]
    y_first = ext[16:304, :] + act
    for tile in range(4):
        lanes = slice(128 * tile, 128 * tile + 128)
        act_scr[288 * tile : 288 * tile + 288, :] = y_first[:, lanes]
        even = act_scr[pl.ds(288 * tile, 144, 2), :]
        wide[8:152, lanes] = even + act_scr[pl.ds(288 * tile + 1, 144, 2), :]
    pooled = 0.5 * wide[8:152, :]
    wide[0:8, :] = jnp.zeros((8, 512), F32)
    wide[152:160, :] = jnp.zeros((8, 512), F32)
    wide[8:152, :] = pooled
    mine_ref[0:256, :] = ext[32:288, :].astype(BF)
    mine_ref[256:384, :] = wide[16:144, :].astype(BF)
    sent.append(send(1))
    taps = jnp.concatenate(
        [
            jnp.where(within(144, 130, k - 2, seq_index), wide[6 + k : 150 + k, :], 0.0).astype(BF)
            for k in range(5)
        ],
        axis=1,
    )
    copies[3].wait()
    pre = dot(taps, second_mat[...])
    act, slope = gelu_both(pre)
    slope_2_ref[...] = slope
    sent.append(send(3))
    wait_for(copies[4:])

    same = lax.broadcasted_iota(jnp.int32, (16, 16), 0) == lax.broadcasted_iota(
        jnp.int32, (16, 16), 1
    )

    def column(row):
        return jnp.sum(jnp.where(same, row, 0.0), axis=1, keepdims=True)

    donor, accept = (donor_ref[...] - 6) & 2047, (accept_ref[...] - 6) & 2047
    live = lax.broadcasted_iota(jnp.int32, (1, 16), 1) < live_ref[0]
    weight = column(jnp.where(live, cot_ref[...], 0.0) * (1024 ** -0.5))
    lane = lax.broadcasted_iota(jnp.int32, (16, 128), 1)
    info = jnp.zeros((16, 128), F32)
    for place, value in enumerate(
        [
            column((donor >> 6).astype(F32)),
            column((donor & 63).astype(F32)),
            column((accept >> 6).astype(F32)),
            column((accept & 63).astype(F32)),
            weight,
            weight - rounded(weight),
        ]
    ):
        info = jnp.where(lane == place, value, info)
    info = info.astype(BF)
    left = half_lanes(64)
    for pair in range(8):
        top = act[8:72, 128 * pair : 128 * pair + 128]
        low = act[72:136, 128 * pair : 128 * pair + 128]
        mess_ref[2 * pair, 0:64, :] = jnp.where(left, top, swap(low)).astype(BF)
        mess_ref[2 * pair + 1, 0:64, :] = jnp.where(left, swap(top), low).astype(BF)
    for target in range(16):
        mess_ref[target, 64:80, :] = info
    sent.append(send(0))
    wait_for(sent)


def forward_part(seq_index, live, inputs, right, donor, accept, cot, w_first, w_second):
    return pl.pallas_call(
        forward_kernel,
        out_shape=[
            jax.ShapeDtypeStruct((16, 80, 128), BF),
            jax.ShapeDtypeStruct((384, 512), BF),
            jax.ShapeDtypeStruct((288, 512), F32),
            jax.ShapeDtypeStruct((144, 1024), F32),
        ],
        in_specs=[SMEM, SMEM, HBM, ANY] + [HBM] * 5,
        out_specs=[HBM] * 4,
        scratch_shapes=[
            pltpu.VMEM((256, 512), BF),
            pltpu.VMEM((48, 512), BF),
            pltpu.VMEM((2560, 512), BF),
            pltpu.VMEM((2560, 1024), BF),
            pltpu.VMEM((1, 16), jnp.int32),
            pltpu.VMEM((1, 16), jnp.int32),
            pltpu.VMEM((1, 16), F32),
            pltpu.VMEM((16, 80, 128), BF),
            pltpu.VMEM((384, 512), BF),
            pltpu.VMEM((288, 512), F32),
            pltpu.VMEM((144, 1024), F32),
            pltpu.VMEM((320, 512), F32),
            pltpu.VMEM((1152, 128), F32),
            pltpu.VMEM((160, 512), F32),
            pltpu.SemaphoreType.DMA((7,)),
            pltpu.SemaphoreType.DMA((4,)),
        ],
        compiler_params=pltpu.CompilerParams(vmem_limit_bytes=56 * MEBI),
        cost_estimate=pl.CostEstimate(
            flops=15 * 10**8, bytes_accessed=10 * 10**6, transcendentals=3 * 10**5
        ),
        name="forward",
    )(
        seq_index, live, inputs, right,
        w_first.reshape(2560, 512), w_second.reshape(2560, 1024), donor, accept, cot,
    )


def pair_kernel(
    seq_ref, got_ref, head_hbm, sent_hbm, term_hbm, head_ref, sent_ref, term_ref, sems
):
    wait_for(started([(head_hbm, head_ref)], sems))
    seq_index = seq_ref[0]
    head_row = head_ref[pl.ds(seq_index // 2, 1), :]
    head_row = jnp.where(seq_index % 2 == 0, head_row, swap(head_row))[:, :64]
    flat = jnp.concatenate([got_ref[i] for i in range(16)], axis=0)
    info = jnp.concatenate([got_ref[i, 64:80, :].astype(F32) for i in range(16)], axis=0)
    donor = (info[:, 0:1] * 64.0 + info[:, 1:2]).astype(jnp.int32)
    accept = (info[:, 2:3] * 64.0 + info[:, 3:4]).astype(jnp.int32)
    weight = info[:, 4:5] + info[:, 5:6]
    spots = jnp.concatenate([donor, accept], axis=0)
    row_of = (spots >> 7) * 80 + (spots & 63)
    pick = (row_of == lax.broadcasted_iota(jnp.int32, (512, 1280), 1)).astype(F32).astype(BF)
    rows = dot(pick, flat)
    rows = jnp.where((spots & 127) < 64, rows, swap(rows))[:, :64]
    donor_rows, accept_rows = rows[:256], rows[256:]
    both = donor_rows * accept_rows
    partial = jnp.sum(both * head_row, axis=1, keepdims=True)
    term = jnp.sum(weight * both, axis=0, keepdims=True)
    term_high = rounded(term)
    term_ref[...] = jnp.concatenate([term_high, term - term_high], axis=1)
    copies = [pltpu.make_async_copy(term_ref, term_hbm, sems.at[4])]
    copies[0].start()
    scaled = weight * head_row
    grads = jnp.concatenate([scaled * accept_rows, scaled * donor_rows], axis=0)
    blank = jnp.zeros((512, 64), F32)
    grads = jnp.concatenate(
        [
            jnp.concatenate([grads, blank], axis=1),
            jnp.concatenate([blank, grads], axis=1),
        ],
        axis=0,
    ).astype(BF)
    lane = lax.broadcasted_iota(jnp.int32, (256, 128), 1)
    turned = jnp.where(
        lane == 0,
        donor.astype(F32),
        jnp.where(lane == 1, accept.astype(F32), jnp.where(lane == 2, partial, 0.0)),
    ).T
    spot_row = jnp.concatenate([turned[0:1, :], turned[1:2, :]], axis=1).astype(jnp.int32)
    high = rounded(turned[2:3, :])
    rest = turned[2:3, :] - high
    extra = jnp.concatenate(
        [
            jnp.zeros((4, 128), F32),
            high[:, :128],
            high[:, 128:],
            rest[:, :128],
            rest[:, 128:],
            jnp.zeros((8, 128), F32),
        ],
        axis=0,
    )
    index = lax.broadcasted_iota(jnp.int32, (80, 1), 0)
    low_row = jnp.where(index < 64, index, index - 67)
    high_row = index + 64
    for target in range(16):
        base = 128 * target
        low_pick = (jnp.where(index < 67, (low_row + base) & 2047, -1) == spot_row).astype(F32)
        high_pick = (jnp.where(index < 67, (high_row + base) & 2047, -1) == spot_row).astype(F32)
        piece = dot(jnp.concatenate([low_pick, high_pick], axis=1).astype(BF), grads)
        sent_ref[target, 0:64, :] = piece[0:64].astype(BF)
        sent_ref[target, 64:80, :] = (piece[64:80] + extra).astype(BF)
        if target % 4 == 3:
            part = pl.ds(target - 3, 4)
            copies.append(
                pltpu.make_async_copy(sent_ref.at[part], sent_hbm.at[part], sems.at[target // 4])
            )
            copies[-1].start()
    wait_for(copies)


def pair_part(seq_index, got, head_vec):
    return pl.pallas_call(
        pair_kernel,
        out_shape=[
            jax.ShapeDtypeStruct((16, 80, 128), BF),
            jax.ShapeDtypeStruct((1, 128), F32),
        ],
        in_specs=[SMEM, VMEM, HBM],
        out_specs=[HBM] * 2,
        scratch_shapes=[
            pltpu.VMEM((8, 128), F32),
            pltpu.VMEM((16, 80, 128), BF),
            pltpu.VMEM((1, 128), F32),
            pltpu.SemaphoreType.DMA((5,)),
        ],
        compiler_params=pltpu.CompilerParams(vmem_limit_bytes=52 * MEBI),
        cost_estimate=pl.CostEstimate(
            flops=5 * 10**8, bytes_accessed=10**6, transcendentals=0
        ),
        name="pairs",
    )(seq_index, got, head_vec.reshape(8, 128))


def backward_kernel(seq_ref, live_ref, back_ref, *refs):
    sources, second_hbm, outs = refs[:4], refs[4], refs[5:9]
    held, second_mat, staged = refs[9:13], refs[13], refs[14:18]
    track_ref, right_ref, slope_2_ref, slope_1_ref = held
    mess_ref, grad_1_ref, grad_y_ref, scores_ref = staged
    wide, grad_y, grad_1, sems, out_sems = refs[18:]
    seq_index = seq_ref[0]
    parts = [pl.ds(512 * k, 512) for k in range(5)]
    copies = started(
        list(zip(sources, held)) + [(second_hbm.at[part], second_mat.at[part]) for part in parts],
        sems,
    )

    def send(place, part, sem):
        copy = pltpu.make_async_copy(part(staged[place]), part(outs[place]), out_sems.at[sem])
        copy.start()
        return copy

    def all_of(ref):
        return ref

    left = half_lanes(64)
    edge = half_lanes(16)
    wide[0:16, :] = jnp.zeros((16, 1024), F32)
    wide[144:160, :] = jnp.zeros((16, 1024), F32)
    for pair in range(8):
        lanes = slice(128 * pair, 128 * pair + 128)
        one = back_ref[2 * pair, 0:64, :].astype(F32)
        two = back_ref[2 * pair + 1, 0:64, :].astype(F32)
        wide[16:80, lanes] = jnp.where(left, one, swap(two))
        wide[80:144, lanes] = jnp.where(left, swap(one), two)
        one = back_ref[2 * pair, 64:80, :].astype(F32)
        two = back_ref[2 * pair + 1, 64:80, :].astype(F32)
        wide[13:16, lanes] = jnp.where(edge, one, swap(two))[0:3]
        wide[144:147, lanes] = jnp.where(edge, swap(one), two)[0:3]
    wait_for(copies[:2])
    far = right_ref[...].astype(F32)
    for row in range(9):
        for half in range(2):
            lanes = slice(512 * half, 512 * half + 512)
            source = 24 + 2 * row + half
            wide[138 + row : 139 + row, lanes] = (
                wide[138 + row : 139 + row, lanes] + far[source : source + 1, :]
            )
    wide[13:138, :] = wide[13:138, :] + track_ref[...].astype(F32)[3:128]
    copies[2].wait()
    wide[8:152, :] = wide[8:152, :] * slope_2_ref[...]
    for target in range(8):
        mess_ref[target, 144:288, :] = wide[8:152, 128 * target : 128 * target + 128].astype(BF)
    sent = [send(0, lambda ref: ref.at[:, pl.ds(144, 144)], 0)]
    pooled = jnp.zeros((144, 512), F32)
    for k in range(5):
        copies[4 + k].wait()
        pooled = pooled + dot(
            jnp.where(within(144, 130, 2 - k, seq_index), wide[10 - k : 154 - k, :], 0.0).astype(BF),
            second_mat[512 * k : 512 * k + 512, :],
            ((1,), (1,)),
        )
    pooled = 0.5 * pooled
    copies[3].wait()
    for tile in range(4):
        lanes = slice(128 * tile, 128 * tile + 128)
        grad_y[pl.ds(288 * tile, 144, 2), :] = pooled[:, lanes]
        grad_y[pl.ds(288 * tile + 1, 144, 2), :] = pooled[:, lanes]
        value = grad_y[288 * tile : 288 * tile + 288, :]
        grad_y_ref[:, lanes] = value[16:272]
        value = value * slope_1_ref[:, lanes]
        grad_1[:, lanes] = value
        grad_1_ref[:, lanes] = value.astype(BF)
    sent += [send(1, all_of, 1), send(2, all_of, 2)]
    left = half_lanes(144)
    for pair in range(4):
        lanes = slice(128 * pair, 128 * pair + 128)
        one = grad_1[8:152, lanes]
        two = grad_1[136:280, lanes]
        mess_ref[2 * pair, 0:144, :] = jnp.where(left, one, swap(two)).astype(BF)
        mess_ref[2 * pair + 1, 0:144, :] = jnp.where(left, swap(one), two).astype(BF)
    sent.append(send(0, lambda ref: ref.at[:, pl.ds(0, 144)], 3))
    total = jnp.zeros((16, 128), F32)
    for source in range(16):
        total = total + back_ref[source, 64:80, :].astype(F32)
    row = jnp.where(seq_index < 8, total[4:5] + total[6:7], total[5:6] + total[7:8])
    row = pltpu.roll(row, 128 - 16 * (seq_index % 8), 1)[:, :16]
    live = lax.broadcasted_iota(jnp.int32, (1, 16), 1) < live_ref[0]
    scores_ref[...] = jnp.where(live, row * (1024 ** -0.5), 0.0)
    sent.append(send(3, all_of, 4))
    wait_for(sent)


def backward_part(seq_cell, live, back, track, right, slope_first, slope_second, w_second):
    return pl.pallas_call(
        backward_kernel,
        out_shape=[
            jax.ShapeDtypeStruct((8, 288, 128), BF),
            jax.ShapeDtypeStruct((288, 512), BF),
            jax.ShapeDtypeStruct((256, 512), F32),
            jax.ShapeDtypeStruct((1, 16), F32),
        ],
        in_specs=[SMEM] * 2 + [VMEM] + [HBM] * 5,
        out_specs=[HBM] * 4,
        scratch_shapes=[
            pltpu.VMEM((128, 1024), BF),
            pltpu.VMEM((48, 512), BF),
            pltpu.VMEM((144, 1024), F32),
            pltpu.VMEM((288, 512), F32),
            pltpu.VMEM((2560, 1024), BF),
            pltpu.VMEM((8, 288, 128), BF),
            pltpu.VMEM((288, 512), BF),
            pltpu.VMEM((256, 512), F32),
            pltpu.VMEM((1, 16), F32),
            pltpu.VMEM((160, 1024), F32),
            pltpu.VMEM((1152, 128), F32),
            pltpu.VMEM((288, 512), F32),
            pltpu.SemaphoreType.DMA((9,)),
            pltpu.SemaphoreType.DMA((5,)),
        ],
        compiler_params=pltpu.CompilerParams(vmem_limit_bytes=52 * MEBI),
        cost_estimate=pl.CostEstimate(
            flops=8 * 10**8, bytes_accessed=10 * 10**6, transcendentals=0
        ),
        name="backward",
    )(
        seq_cell, live, back, track, right, slope_second, slope_first,
        w_second.reshape(2560, 1024),
    )


def input_kernel(seq_ref, *refs):
    sources, (out_ref, tail_ref), held, (grad_1, sems) = refs[:3], refs[3:5], refs[5:8], refs[8:]
    grad_ref, grad_y_ref, first_mat = held
    copies = started(list(zip(sources, held)), sems)
    copies[0].wait()
    grad_1[...] = grad_ref[...].astype(F32)
    wait_for(copies[1:])
    total = grad_y_ref[...]
    for k in range(5):
        rows = jnp.where(within(256, 244, 2 - k, seq_ref[0]), grad_1[18 - k : 274 - k, :], 0.0)
        total = total + dot(
            rows.astype(BF), first_mat[512 * k : 512 * k + 512, :], ((1,), (1,))
        )
    out_ref[...] = total.astype(BF)
    tail_ref[...] = total[240:256].astype(BF)


def input_part(seq_cell, grad_y, grad_first_pre, w_first):
    return pl.pallas_call(
        input_kernel,
        out_shape=[
            jax.ShapeDtypeStruct((256, 512), BF),
            jax.ShapeDtypeStruct((16, 512), BF),
        ],
        in_specs=[SMEM] + [HBM] * 3,
        out_specs=[VMEM] * 2,
        scratch_shapes=[
            pltpu.VMEM((288, 512), BF),
            pltpu.VMEM((256, 512), F32),
            pltpu.VMEM((2560, 512), BF),
            pltpu.VMEM((288, 512), F32),
            pltpu.SemaphoreType.DMA((3,)),
        ],
        compiler_params=pltpu.CompilerParams(vmem_limit_bytes=52 * MEBI),
        cost_estimate=pl.CostEstimate(
            flops=7 * 10**8, bytes_accessed=4 * 10**6, transcendentals=0
        ),
        name="inputs",
    )(seq_cell, grad_first_pre, grad_y, w_first.reshape(2560, 512))


def term_kernel(dp_ref, seq_ref, *refs):
    got_ref, head_ref, sources, out_hbm, out_ref = refs[0], refs[1], refs[2:10], refs[10], refs[11]
    columns = refs[12:20]
    part_scr, wide_1, wide_2, sum_1, sum_2, mess, sems, out_sems = refs[20:]
    copies = started(list(zip(sources, columns)), sems)
    left = half_lanes(128)
    fit_1 = [half_lanes(16) | within(16, 4, 2 - k, seq_ref[0]) for k in range(5)]
    fit_2 = [within(16, 10, 2 - k, seq_ref[0]) for k in range(5)]
    for step in range(8):
        part_scr[...] = got_ref[dp_ref[0] ^ step].astype(F32)
        taps = []
        for k in range(5):
            ends = jnp.where(fit_1[k], part_scr[122 - k : 138 - k, :], 0.0)
            taps.append(jnp.concatenate([part_scr[10 - k : 122 - k, :], ends], axis=0))
            lanes = slice(128 * k, 128 * k + 128)
            wide_2[128 * step : 128 * step + 112, lanes] = part_scr[154 - k : 266 - k, :].astype(BF)
            wide_2[128 * step + 112 : 128 * step + 128, lanes] = jnp.where(
                fit_2[k], part_scr[266 - k : 282 - k, :], 0.0
            ).astype(BF)
        top = [
            jnp.where(left, taps[0], swap(taps[1])),
            jnp.where(left, taps[2], swap(taps[3])),
            taps[4],
        ]
        low = [
            jnp.where(left, swap(taps[0]), taps[1]),
            jnp.where(left, swap(taps[2]), taps[3]),
            swap(taps[4]),
        ]
        for place in range(3):
            lanes = slice(128 * place, 128 * place + 128)
            wide_1[256 * step : 256 * step + 128, lanes] = top[place].astype(BF)
            wide_1[256 * step + 128 : 256 * step + 256, lanes] = low[place].astype(BF)
    wait_for(copies)
    lefts = jnp.concatenate([ref[:, 0:256] for ref in columns], axis=1)
    first = dot(lefts, wide_1[...])
    lefts = jnp.concatenate([ref[:, 256:384] for ref in columns], axis=1)
    second = dot(lefts, wide_2[...])
    left = half_lanes(512)
    for k in range(5):
        sum_2[512 * k : 512 * k + 512, :] = second[:, 128 * k : 128 * k + 128]
        tile = first[:, 128 * (k // 2) : 128 * (k // 2) + 128]
        turned = swap(tile)
        sum_1[512 * k : 512 * k + 512, :] = (
            jnp.where(left, tile, turned) if k % 2 == 0 else jnp.where(left, turned, tile)
        )
    left = half_lanes(10)
    head = jnp.concatenate([head_ref[...], jnp.zeros((1, 128), F32)], axis=0)
    sent = []
    for owner in range(128):
        row = 20 * owner
        mess[0:20, :] = sum_2[row : row + 20, :]
        mess[20:30, :] = jnp.where(left, sum_1[row : row + 10, :], sum_1[row + 10 : row + 20, :])
        mess[30:32, :] = head
        out_ref[owner] = mess[...].astype(BF)
        if owner % 32 == 31:
            part = pl.ds(owner - 31, 32)
            sent.append(
                pltpu.make_async_copy(out_ref.at[part], out_hbm.at[part], out_sems.at[owner // 32])
            )
            sent[-1].start()
    wait_for(sent)


def term_part(columns, got, head_row, dp_index, seq_cell):
    return pl.pallas_call(
        term_kernel,
        out_shape=jax.ShapeDtypeStruct((128, 32, 128), BF),
        in_specs=[SMEM] * 2 + [VMEM] * 2 + [HBM] * 8,
        out_specs=HBM,
        scratch_shapes=[
            pltpu.VMEM((128, 32, 128), BF),
        ]
        + [pltpu.VMEM((512, 384), BF)] * 8
        + [
            pltpu.VMEM((288, 128), F32),
            pltpu.VMEM((2048, 384), BF),
            pltpu.VMEM((1024, 640), BF),
            pltpu.VMEM((2560, 128), F32),
            pltpu.VMEM((2560, 128), F32),
            pltpu.VMEM((32, 128), F32),
            pltpu.SemaphoreType.DMA((8,)),
            pltpu.SemaphoreType.DMA((4,)),
        ],
        compiler_params=pltpu.CompilerParams(vmem_limit_bytes=52 * MEBI),
        cost_estimate=pl.CostEstimate(flops=3 * 10**9, bytes_accessed=5 * 10**6, transcendentals=0),
        name="terms",
    )(jnp.reshape(dp_index, (1,)), seq_cell, got, head_row, *columns)


def final_kernel(final_ref, first_ref, second_ref, head_ref):
    left = half_lanes(10)
    for pair in range(4):
        sums = []
        for block in (2 * pair, 2 * pair + 1):
            total = final_ref[16 * block].astype(F32)
            for source in range(1, 16):
                total = total + final_ref[16 * block + source].astype(F32)
            second_ref[:, 128 * block : 128 * block + 128] = total[0:20]
            sums.append(total[20:30])
        one, two = sums
        lanes = slice(128 * pair, 128 * pair + 128)
        first_ref[0:10, lanes] = jnp.where(left, one, swap(two))
        first_ref[10:20, lanes] = jnp.where(left, swap(one), two)
    left = half_lanes(16)
    for pair in range(8):
        sums = []
        for source in (2 * pair, 2 * pair + 1):
            total = final_ref[source, 16:32, :].astype(F32)
            for block in range(1, 8):
                total = total + final_ref[16 * block + source, 16:32, :].astype(F32)
            sums.append(total + swap(total))
        head_ref[pair : pair + 1, :] = jnp.where(left, sums[0], sums[1])[14:15]


def final_part(final):
    return pl.pallas_call(
        final_kernel,
        out_shape=[
            jax.ShapeDtypeStruct((20, 512), F32),
            jax.ShapeDtypeStruct((20, 1024), F32),
            jax.ShapeDtypeStruct((8, 128), F32),
        ],
        in_specs=[VMEM],
        out_specs=[VMEM] * 3,
        compiler_params=pltpu.CompilerParams(vmem_limit_bytes=50 * MEBI),
        name="final",
    )(final)


def per_device(
    seq_in, w_first, w_second, head_vec, track_cot, donor_pos, acceptor_pos, pair_cot, live_pairs
):
    seq_index = lax.axis_index("seq")
    seq_cell = jnp.reshape(seq_index, (1,))
    dp_index = lax.axis_index("dp")
    inputs, track = seq_in[0], track_cot[0]
    right = edges(inputs, track, 16)
    message, mine, slope_first, slope_second = forward_part(
        seq_cell, live_pairs[0], inputs, right, donor_pos, acceptor_pos, pair_cot,
        w_first, w_second,
    )
    got = lax.all_to_all(message, "seq", 0, 0, tiled=True)

    mine = mine.T

    def passed(value, step):
        return lax.ppermute(value, "dp", [(i, i ^ step) for i in range(8)])

    own = [mine] + [passed(mine, step) for step in (2, 4, 6)]
    sent, head_row = pair_part(seq_cell, got, head_vec)
    back = lax.all_to_all(sent, "seq", 0, 0, tiled=True)
    back, *own = lax.optimization_barrier((back, *own))
    message, grad_1, grad_y, scores = backward_part(
        seq_cell, live_pairs[0], back, track, right, slope_first, slope_second, w_second
    )
    other = [passed(value, 1) for value in own]
    columns = [(own, other)[step % 2][step // 2] for step in range(8)]
    grads = lax.all_to_all(message, "dp", 0, 0, tiled=True)
    grad_input, tail = input_part(seq_cell, grad_y, grad_1, w_first)
    before = lax.ppermute(tail, "seq", [(i, (i + 1) % 16) for i in range(16)])
    terms = term_part(columns, grads, head_row, dp_index, seq_cell)
    terms, before = lax.optimization_barrier((terms, before))
    grad_input = jnp.concatenate([before[4:], grad_input[:244]], axis=0)
    final = lax.all_to_all(terms, ("dp", "seq"), 0, 0, tiled=True)
    out_first, out_second, grad_head = final_part(final)
    return (scores, out_first, out_second, grad_input[None], grad_head.reshape(1024))


def solution(mesh):
    in_specs = (
        P("dp", "seq", None),
        P(),
        P(),
        P(),
        P("dp", "seq", None),
        P("dp", "seq"),
        P("dp", "seq"),
        P("dp", "seq"),
        P("dp", "seq"),
    )
    out_specs = (
        P("dp", "seq"),
        P(("dp", "seq"), None),
        P(("dp", "seq"), None),
        P("dp", "seq", None),
        P(),
    )
    return jax.shard_map(
        per_device, mesh=mesh, in_specs=in_specs, out_specs=out_specs, check_vma=False
    )
```

```python
import jax
import jax.numpy as jnp
from jax import lax
from jax.experimental import pallas as pl
from jax.experimental.pallas import tpu as pltpu
from jax.sharding import PartitionSpec as P

BF = jnp.bfloat16
F32 = jnp.float32
ROOT = 0.7978845608028654
CUBE = 0.044715


def gelu_both(pre):
    square = pre * pre
    bent = jnp.tanh(ROOT * pre * (1.0 + CUBE * square))
    half = 0.5 * (1.0 + bent)
    slope = half + 0.5 * pre * (1.0 - bent * bent) * (ROOT * (1.0 + 3.0 * CUBE * square))
    return pre * half, slope


def dot(left, right, dims=((1,), (0,))):
    return lax.dot_general(left, right, (dims, ((), ())), preferred_element_type=F32)


VMEM = pl.BlockSpec(memory_space=pltpu.VMEM)
SMEM = pl.BlockSpec(memory_space=pltpu.SMEM)
HBM = pl.BlockSpec(memory_space=pltpu.HBM)
ANY = pl.BlockSpec(memory_space=pl.ANY)
MEBI = 1024 * 1024


def rounded(value):
    return value.astype(BF).astype(F32)


def half_lanes(rows):
    return lax.broadcasted_iota(jnp.int32, (rows, 128), 1) < 64


def swap(value):
    return pltpu.roll(value, 64, 1)


def started(moves, sems):
    copies = []
    for place, (source, target) in enumerate(moves):
        copies.append(pltpu.make_async_copy(source, target, sems.at[place]))
        copies[place].start()
    return copies


def wait_for(copies):
    for copy in copies:
        copy.wait()


def within(rows, seam, shift, seq_index):
    row = lax.broadcasted_iota(jnp.int32, (rows, 1), 0)
    return ((row >= seam) == (row + shift >= seam)) | (seq_index != 15)


def edge_kernel(inputs_hbm, track_hbm, out_hbm, rows_scr, track_scr, out_scr, sems):
    wait_for(
        started(
            [
                (inputs_hbm.at[pl.ds(0, 32)], rows_scr),
                (track_hbm.at[pl.ds(0, 16)], track_scr),
            ],
            sems,
        )
    )
    track = track_scr[...].astype(F32)
    pieces = [rows_scr[...].astype(F32)[:24]]
    for row in range(9):
        pieces += [track[row : row + 1, :512], track[row : row + 1, 512:]]
    pieces.append(jnp.zeros((6, 512), F32))
    out_scr[...] = jnp.concatenate(pieces, axis=0).astype(BF)
    wait_for(started([(out_scr, out_hbm)], sems))


def edges(inputs, track, count):
    first = pl.pallas_call(
        edge_kernel,
        out_shape=jax.ShapeDtypeStruct((48, 512), BF),
        in_specs=[HBM] * 2,
        out_specs=HBM,
        scratch_shapes=[
            pltpu.VMEM((32, 512), BF),
            pltpu.VMEM((16, 1024), BF),
            pltpu.VMEM((48, 512), BF),
            pltpu.SemaphoreType.DMA((2,)),
        ],
        compiler_params=pltpu.CompilerParams(vmem_limit_bytes=56 * MEBI),
        name="edges",
    )(inputs, track)
    return lax.ppermute(first, "seq", [(i, (i - 1) % count) for i in range(count)])


def forward_kernel(seq_ref, live_ref, *refs):
    sources, outs, held, staged, work = refs[:7], refs[7:11], refs[11:18], refs[18:22], refs[22:]
    inputs_ref, right_ref, first_mat, second_mat, donor_ref, accept_ref, cot_ref = held
    mess_ref, mine_ref, slope_1_ref, slope_2_ref = staged
    ext, act_scr, wide, sems, out_sems = work
    copies = started(list(zip(sources, held)), sems)

    def send(place):
        copy = pltpu.make_async_copy(staged[place], outs[place], out_sems.at[place])
        copy.start()
        return copy

    seq_index = seq_ref[0]
    ext[0:32, :] = jnp.zeros((32, 512), F32)
    ext[288:320, :] = jnp.zeros((32, 512), F32)
    wait_for(copies[:2])
    ext[20:276, :] = inputs_ref[...].astype(F32)
    ext[276:300, :] = right_ref[...].astype(F32)[:24]
    taps = jnp.concatenate(
        [
            jnp.where(within(288, 260, k - 2, seq_index), ext[14 + k : 302 + k, :], 0.0).astype(BF)
            for k in range(5)
        ],
        axis=1,
    )
    copies[2].wait()
    pre = dot(taps, first_mat[...])
    act, slope = gelu_both(pre)
    slope_1_ref[...] = slope
    sent = [send(2)]
    y_first = ext[16:304, :] + act
    for tile in range(4):
        lanes = slice(128 * tile, 128 * tile + 128)
        act_scr[288 * tile : 288 * tile + 288, :] = y_first[:, lanes]
        even = act_scr[pl.ds(288 * tile, 144, 2), :]
        wide[8:152, lanes] = even + act_scr[pl.ds(288 * tile + 1, 144, 2), :]
    pooled = 0.5 * wide[8:152, :]
    wide[0:8, :] = jnp.zeros((8, 512), F32)
    wide[152:160, :] = jnp.zeros((8, 512), F32)
    wide[8:152, :] = pooled
    mine_ref[0:256, :] = ext[32:288, :].astype(BF)
    mine_ref[256:384, :] = wide[16:144, :].astype(BF)
    sent.append(send(1))
    taps = jnp.concatenate(
        [
            jnp.where(within(144, 130, k - 2, seq_index), wide[6 + k : 150 + k, :], 0.0).astype(BF)
            for k in range(5)
        ],
        axis=1,
    )
    copies[3].wait()
    pre = dot(taps, second_mat[...])
    act, slope = gelu_both(pre)
    slope_2_ref[...] = slope
    sent.append(send(3))
    wait_for(copies[4:])

    same = lax.broadcasted_iota(jnp.int32, (16, 16), 0) == lax.broadcasted_iota(
        jnp.int32, (16, 16), 1
    )

    def column(row):
        return jnp.sum(jnp.where(same, row, 0.0), axis=1, keepdims=True)

    donor, accept = (donor_ref[...] - 6) & 2047, (accept_ref[...] - 6) & 2047
    live = lax.broadcasted_iota(jnp.int32, (1, 16), 1) < live_ref[0]
    weight = column(jnp.where(live, cot_ref[...], 0.0) * (1024 ** -0.5))
    lane = lax.broadcasted_iota(jnp.int32, (16, 128), 1)
    info = jnp.zeros((16, 128), F32)
    for place, value in enumerate(
        [
            column((donor >> 6).astype(F32)),
            column((donor & 63).astype(F32)),
            column((accept >> 6).astype(F32)),
            column((accept & 63).astype(F32)),
            weight,
            weight - rounded(weight),
        ]
    ):
        info = jnp.where(lane == place, value, info)
    info = info.astype(BF)
    left = half_lanes(64)
    for pair in range(8):
        top = act[8:72, 128 * pair : 128 * pair + 128]
        low = act[72:136, 128 * pair : 128 * pair + 128]
        mess_ref[2 * pair, 0:64, :] = jnp.where(left, top, swap(low)).astype(BF)
        mess_ref[2 * pair + 1, 0:64, :] = jnp.where(left, swap(top), low).astype(BF)
    for target in range(16):
        mess_ref[target, 64:80, :] = info
    sent.append(send(0))
    wait_for(sent)


def forward_part(seq_index, live, inputs, right, donor, accept, cot, w_first, w_second):
    return pl.pallas_call(
        forward_kernel,
        out_shape=[
            jax.ShapeDtypeStruct((16, 80, 128), BF),
            jax.ShapeDtypeStruct((384, 512), BF),
            jax.ShapeDtypeStruct((288, 512), F32),
            jax.ShapeDtypeStruct((144, 1024), F32),
        ],
        in_specs=[SMEM, SMEM, HBM, ANY] + [HBM] * 5,
        out_specs=[HBM] * 4,
        scratch_shapes=[
            pltpu.VMEM((256, 512), BF),
            pltpu.VMEM((48, 512), BF),
            pltpu.VMEM((2560, 512), BF),
            pltpu.VMEM((2560, 1024), BF),
            pltpu.VMEM((1, 16), jnp.int32),
            pltpu.VMEM((1, 16), jnp.int32),
            pltpu.VMEM((1, 16), F32),
            pltpu.VMEM((16, 80, 128), BF),
            pltpu.VMEM((384, 512), BF),
            pltpu.VMEM((288, 512), F32),
            pltpu.VMEM((144, 1024), F32),
            pltpu.VMEM((320, 512), F32),
            pltpu.VMEM((1152, 128), F32),
            pltpu.VMEM((160, 512), F32),
            pltpu.SemaphoreType.DMA((7,)),
            pltpu.SemaphoreType.DMA((4,)),
        ],
        compiler_params=pltpu.CompilerParams(vmem_limit_bytes=56 * MEBI),
        cost_estimate=pl.CostEstimate(
            flops=15 * 10**8, bytes_accessed=10 * 10**6, transcendentals=3 * 10**5
        ),
        name="forward",
    )(
        seq_index, live, inputs, right,
        w_first.reshape(2560, 512), w_second.reshape(2560, 1024), donor, accept, cot,
    )


def pair_kernel(
    seq_ref, got_ref, head_hbm, sent_hbm, term_hbm, head_ref, sent_ref, term_ref, sems
):
    wait_for(started([(head_hbm, head_ref)], sems))
    seq_index = seq_ref[0]
    head_row = head_ref[pl.ds(seq_index // 2, 1), :]
    head_row = jnp.where(seq_index % 2 == 0, head_row, swap(head_row))[:, :64]
    flat = jnp.concatenate([got_ref[i] for i in range(16)], axis=0)
    info = jnp.concatenate([got_ref[i, 64:80, :].astype(F32) for i in range(16)], axis=0)
    donor = (info[:, 0:1] * 64.0 + info[:, 1:2]).astype(jnp.int32)
    accept = (info[:, 2:3] * 64.0 + info[:, 3:4]).astype(jnp.int32)
    weight = info[:, 4:5] + info[:, 5:6]
    spots = jnp.concatenate([donor, accept], axis=0)
    row_of = (spots >> 7) * 80 + (spots & 63)
    pick = (row_of == lax.broadcasted_iota(jnp.int32, (512, 1280), 1)).astype(F32).astype(BF)
    rows = dot(pick, flat)
    rows = jnp.where((spots & 127) < 64, rows, swap(rows))[:, :64]
    donor_rows, accept_rows = rows[:256], rows[256:]
    both = donor_rows * accept_rows
    partial = jnp.sum(both * head_row, axis=1, keepdims=True)
    term = jnp.sum(weight * both, axis=0, keepdims=True)
    term_high = rounded(term)
    term_ref[...] = jnp.concatenate([term_high, term - term_high], axis=1)
    copies = [pltpu.make_async_copy(term_ref, term_hbm, sems.at[4])]
    copies[0].start()
    scaled = weight * head_row
    grads = jnp.concatenate([scaled * accept_rows, scaled * donor_rows], axis=0)
    blank = jnp.zeros((512, 64), F32)
    grads = jnp.concatenate(
        [
            jnp.concatenate([grads, blank], axis=1),
            jnp.concatenate([blank, grads], axis=1),
        ],
        axis=0,
    ).astype(BF)
    lane = lax.broadcasted_iota(jnp.int32, (256, 128), 1)
    turned = jnp.where(
        lane == 0,
        donor.astype(F32),
        jnp.where(lane == 1, accept.astype(F32), jnp.where(lane == 2, partial, 0.0)),
    ).T
    spot_row = jnp.concatenate([turned[0:1, :], turned[1:2, :]], axis=1).astype(jnp.int32)
    high = rounded(turned[2:3, :])
    rest = turned[2:3, :] - high
    extra = jnp.concatenate(
        [
            jnp.zeros((4, 128), F32),
            high[:, :128],
            high[:, 128:],
            rest[:, :128],
            rest[:, 128:],
            jnp.zeros((8, 128), F32),
        ],
        axis=0,
    )
    index = lax.broadcasted_iota(jnp.int32, (80, 1), 0)
    low_row = jnp.where(index < 64, index, index - 67)
    high_row = index + 64
    for group in range(4):
        picks = []
        for target in range(4 * group, 4 * group + 4):
            base = 128 * target
            low_pick = jnp.where(index < 67, (low_row + base) & 2047, -1) == spot_row
            high_pick = jnp.where(index < 67, (high_row + base) & 2047, -1) == spot_row
            picks.append(jnp.concatenate([low_pick.astype(F32), high_pick.astype(F32)], axis=1))
        pieces = dot(jnp.concatenate(picks, axis=0).astype(BF), grads)
        for place in range(4):
            target = 4 * group + place
            piece = pieces[80 * place : 80 * place + 80]
            sent_ref[target, 0:64, :] = piece[0:64].astype(BF)
            sent_ref[target, 64:80, :] = (piece[64:80] + extra).astype(BF)
        part = pl.ds(4 * group, 4)
        copies.append(pltpu.make_async_copy(sent_ref.at[part], sent_hbm.at[part], sems.at[group]))
        copies[-1].start()
    wait_for(copies)


def pair_part(seq_index, got, head_vec):
    return pl.pallas_call(
        pair_kernel,
        out_shape=[
            jax.ShapeDtypeStruct((16, 80, 128), BF),
            jax.ShapeDtypeStruct((1, 128), F32),
        ],
        in_specs=[SMEM, VMEM, HBM],
        out_specs=[HBM] * 2,
        scratch_shapes=[
            pltpu.VMEM((8, 128), F32),
            pltpu.VMEM((16, 80, 128), BF),
            pltpu.VMEM((1, 128), F32),
            pltpu.SemaphoreType.DMA((5,)),
        ],
        compiler_params=pltpu.CompilerParams(vmem_limit_bytes=52 * MEBI),
        cost_estimate=pl.CostEstimate(
            flops=5 * 10**8, bytes_accessed=10**6, transcendentals=0
        ),
        name="pairs",
    )(seq_index, got, head_vec.reshape(8, 128))


def backward_kernel(seq_ref, live_ref, back_ref, *refs):
    sources, second_hbm, outs = refs[:4], refs[4], refs[5:9]
    held, second_mat, staged = refs[9:13], refs[13], refs[14:18]
    track_ref, right_ref, slope_2_ref, slope_1_ref = held
    mess_ref, grad_1_ref, grad_y_ref, scores_ref = staged
    wide, grad_y, grad_1, sems, out_sems = refs[18:]
    seq_index = seq_ref[0]
    parts = [pl.ds(512 * k, 512) for k in range(5)]
    copies = started(
        list(zip(sources, held)) + [(second_hbm.at[part], second_mat.at[part]) for part in parts],
        sems,
    )

    def send(place, part, sem):
        copy = pltpu.make_async_copy(part(staged[place]), part(outs[place]), out_sems.at[sem])
        copy.start()
        return copy

    def all_of(ref):
        return ref

    left = half_lanes(64)
    edge = half_lanes(16)
    wide[0:16, :] = jnp.zeros((16, 1024), F32)
    wide[144:160, :] = jnp.zeros((16, 1024), F32)
    for pair in range(8):
        lanes = slice(128 * pair, 128 * pair + 128)
        one = back_ref[2 * pair, 0:64, :].astype(F32)
        two = back_ref[2 * pair + 1, 0:64, :].astype(F32)
        wide[16:80, lanes] = jnp.where(left, one, swap(two))
        wide[80:144, lanes] = jnp.where(left, swap(one), two)
        one = back_ref[2 * pair, 64:80, :].astype(F32)
        two = back_ref[2 * pair + 1, 64:80, :].astype(F32)
        wide[13:16, lanes] = jnp.where(edge, one, swap(two))[0:3]
        wide[144:147, lanes] = jnp.where(edge, swap(one), two)[0:3]
    wait_for(copies[:2])
    far = right_ref[...].astype(F32)
    for row in range(9):
        for half in range(2):
            lanes = slice(512 * half, 512 * half + 512)
            source = 24 + 2 * row + half
            wide[138 + row : 139 + row, lanes] = (
                wide[138 + row : 139 + row, lanes] + far[source : source + 1, :]
            )
    wide[13:138, :] = wide[13:138, :] + track_ref[...].astype(F32)[3:128]
    copies[2].wait()
    wide[8:152, :] = wide[8:152, :] * slope_2_ref[...]
    for target in range(8):
        mess_ref[target, 144:288, :] = wide[8:152, 128 * target : 128 * target + 128].astype(BF)
    sent = [send(0, lambda ref: ref.at[:, pl.ds(144, 144)], 0)]
    pooled = jnp.zeros((144, 512), F32)
    for k in range(5):
        copies[4 + k].wait()
        pooled = pooled + dot(
            jnp.where(within(144, 130, 2 - k, seq_index), wide[10 - k : 154 - k, :], 0.0).astype(BF),
            second_mat[512 * k : 512 * k + 512, :],
            ((1,), (1,)),
        )
    pooled = 0.5 * pooled
    copies[3].wait()
    for tile in range(4):
        lanes = slice(128 * tile, 128 * tile + 128)
        grad_y[pl.ds(288 * tile, 144, 2), :] = pooled[:, lanes]
        grad_y[pl.ds(288 * tile + 1, 144, 2), :] = pooled[:, lanes]
        value = grad_y[288 * tile : 288 * tile + 288, :]
        grad_y_ref[:, lanes] = value[16:272]
        value = value * slope_1_ref[:, lanes]
        grad_1[:, lanes] = value
        grad_1_ref[:, lanes] = value.astype(BF)
    sent += [send(1, all_of, 1), send(2, all_of, 2)]
    left = half_lanes(144)
    for pair in range(4):
        lanes = slice(128 * pair, 128 * pair + 128)
        one = grad_1[8:152, lanes]
        two = grad_1[136:280, lanes]
        mess_ref[2 * pair, 0:144, :] = jnp.where(left, one, swap(two)).astype(BF)
        mess_ref[2 * pair + 1, 0:144, :] = jnp.where(left, swap(one), two).astype(BF)
    sent.append(send(0, lambda ref: ref.at[:, pl.ds(0, 144)], 3))
    total = jnp.zeros((16, 128), F32)
    for source in range(16):
        total = total + back_ref[source, 64:80, :].astype(F32)
    row = jnp.where(seq_index < 8, total[4:5] + total[6:7], total[5:6] + total[7:8])
    row = pltpu.roll(row, 128 - 16 * (seq_index % 8), 1)[:, :16]
    live = lax.broadcasted_iota(jnp.int32, (1, 16), 1) < live_ref[0]
    scores_ref[...] = jnp.where(live, row * (1024 ** -0.5), 0.0)
    sent.append(send(3, all_of, 4))
    wait_for(sent)


def backward_part(seq_cell, live, back, track, right, slope_first, slope_second, w_second):
    return pl.pallas_call(
        backward_kernel,
        out_shape=[
            jax.ShapeDtypeStruct((8, 288, 128), BF),
            jax.ShapeDtypeStruct((288, 512), BF),
            jax.ShapeDtypeStruct((256, 512), F32),
            jax.ShapeDtypeStruct((1, 16), F32),
        ],
        in_specs=[SMEM] * 2 + [VMEM] + [HBM] * 5,
        out_specs=[HBM] * 4,
        scratch_shapes=[
            pltpu.VMEM((128, 1024), BF),
            pltpu.VMEM((48, 512), BF),
            pltpu.VMEM((144, 1024), F32),
            pltpu.VMEM((288, 512), F32),
            pltpu.VMEM((2560, 1024), BF),
            pltpu.VMEM((8, 288, 128), BF),
            pltpu.VMEM((288, 512), BF),
            pltpu.VMEM((256, 512), F32),
            pltpu.VMEM((1, 16), F32),
            pltpu.VMEM((160, 1024), F32),
            pltpu.VMEM((1152, 128), F32),
            pltpu.VMEM((288, 512), F32),
            pltpu.SemaphoreType.DMA((9,)),
            pltpu.SemaphoreType.DMA((5,)),
        ],
        compiler_params=pltpu.CompilerParams(vmem_limit_bytes=52 * MEBI),
        cost_estimate=pl.CostEstimate(
            flops=8 * 10**8, bytes_accessed=10 * 10**6, transcendentals=0
        ),
        name="backward",
    )(
        seq_cell, live, back, track, right, slope_second, slope_first,
        w_second.reshape(2560, 1024),
    )


def input_kernel(seq_ref, *refs):
    sources, (out_ref, tail_ref), held, (grad_1, sems) = refs[:3], refs[3:5], refs[5:8], refs[8:]
    grad_ref, grad_y_ref, first_mat = held
    copies = started(list(zip(sources, held)), sems)
    copies[0].wait()
    grad_1[...] = grad_ref[...].astype(F32)
    wait_for(copies[1:])
    total = grad_y_ref[...]
    for k in range(5):
        rows = jnp.where(within(256, 244, 2 - k, seq_ref[0]), grad_1[18 - k : 274 - k, :], 0.0)
        total = total + dot(
            rows.astype(BF), first_mat[512 * k : 512 * k + 512, :], ((1,), (1,))
        )
    out_ref[...] = total.astype(BF)
    tail_ref[...] = total[240:256].astype(BF)


def input_part(seq_cell, grad_y, grad_first_pre, w_first):
    return pl.pallas_call(
        input_kernel,
        out_shape=[
            jax.ShapeDtypeStruct((256, 512), BF),
            jax.ShapeDtypeStruct((16, 512), BF),
        ],
        in_specs=[SMEM] + [HBM] * 3,
        out_specs=[VMEM] * 2,
        scratch_shapes=[
            pltpu.VMEM((288, 512), BF),
            pltpu.VMEM((256, 512), F32),
            pltpu.VMEM((2560, 512), BF),
            pltpu.VMEM((288, 512), F32),
            pltpu.SemaphoreType.DMA((3,)),
        ],
        compiler_params=pltpu.CompilerParams(vmem_limit_bytes=52 * MEBI),
        cost_estimate=pl.CostEstimate(
            flops=7 * 10**8, bytes_accessed=4 * 10**6, transcendentals=0
        ),
        name="inputs",
    )(seq_cell, grad_first_pre, grad_y, w_first.reshape(2560, 512))


def term_kernel(dp_ref, seq_ref, *refs):
    sources, out_hbm, held, out_ref = refs[:10], refs[10], refs[11:21], refs[21]
    part_scr, wide_1, wide_2, sum_1, sum_2, mess, sems, out_sems = refs[22:]
    got_ref, head_ref, columns = held[0], held[1], held[2:]
    copies = started(list(zip(sources, held)), sems)
    copies[0].wait()
    left = half_lanes(128)
    fit_1 = [half_lanes(16) | within(16, 4, 2 - k, seq_ref[0]) for k in range(5)]
    fit_2 = [within(16, 10, 2 - k, seq_ref[0]) for k in range(5)]
    for step in range(8):
        part_scr[...] = got_ref[dp_ref[0] ^ step].astype(F32)
        taps = []
        for k in range(5):
            ends = jnp.where(fit_1[k], part_scr[122 - k : 138 - k, :], 0.0)
            taps.append(jnp.concatenate([part_scr[10 - k : 122 - k, :], ends], axis=0))
            lanes = slice(128 * k, 128 * k + 128)
            wide_2[128 * step : 128 * step + 112, lanes] = part_scr[154 - k : 266 - k, :].astype(BF)
            wide_2[128 * step + 112 : 128 * step + 128, lanes] = jnp.where(
                fit_2[k], part_scr[266 - k : 282 - k, :], 0.0
            ).astype(BF)
        top = [
            jnp.where(left, taps[0], swap(taps[1])),
            jnp.where(left, taps[2], swap(taps[3])),
            taps[4],
        ]
        low = [
            jnp.where(left, swap(taps[0]), taps[1]),
            jnp.where(left, swap(taps[2]), taps[3]),
            swap(taps[4]),
        ]
        for place in range(3):
            lanes = slice(128 * place, 128 * place + 128)
            wide_1[256 * step : 256 * step + 128, lanes] = top[place].astype(BF)
            wide_1[256 * step + 128 : 256 * step + 256, lanes] = low[place].astype(BF)
    wait_for(copies[1:])
    lefts = jnp.concatenate([ref[:, 0:256] for ref in columns], axis=1)
    first = dot(lefts, wide_1[...])
    lefts = jnp.concatenate([ref[:, 256:384] for ref in columns], axis=1)
    second = dot(lefts, wide_2[...])
    left = half_lanes(512)
    for k in range(5):
        sum_2[512 * k : 512 * k + 512, :] = second[:, 128 * k : 128 * k + 128]
        tile = first[:, 128 * (k // 2) : 128 * (k // 2) + 128]
        turned = swap(tile)
        sum_1[512 * k : 512 * k + 512, :] = (
            jnp.where(left, tile, turned) if k % 2 == 0 else jnp.where(left, turned, tile)
        )
    left = half_lanes(10)
    head = jnp.concatenate([head_ref[...], jnp.zeros((1, 128), F32)], axis=0)
    sent = []
    for owner in range(128):
        row = 20 * owner
        slot = owner % 4
        mess[slot, 0:20, :] = sum_2[row : row + 20, :]
        mess[slot, 20:30, :] = jnp.where(
            left, sum_1[row : row + 10, :], sum_1[row + 10 : row + 20, :]
        )
        if owner < 4:
            mess[slot, 30:32, :] = head
        out_ref[owner] = mess[slot].astype(BF)
        if owner % 32 == 31:
            part = pl.ds(owner - 31, 32)
            sent.append(
                pltpu.make_async_copy(out_ref.at[part], out_hbm.at[part], out_sems.at[owner // 32])
            )
            sent[-1].start()
    wait_for(sent)


def term_part(columns, got, head_row, dp_index, seq_cell):
    return pl.pallas_call(
        term_kernel,
        out_shape=jax.ShapeDtypeStruct((128, 32, 128), BF),
        in_specs=[SMEM] * 2 + [ANY] * 2 + [HBM] * 8,
        out_specs=HBM,
        scratch_shapes=[
            pltpu.VMEM((8, 288, 128), BF),
            pltpu.VMEM((1, 128), F32),
        ]
        + [pltpu.VMEM((512, 384), BF)] * 8
        + [
            pltpu.VMEM((128, 32, 128), BF),
            pltpu.VMEM((288, 128), F32),
            pltpu.VMEM((2048, 384), BF),
            pltpu.VMEM((1024, 640), BF),
            pltpu.VMEM((2560, 128), F32),
            pltpu.VMEM((2560, 128), F32),
            pltpu.VMEM((4, 32, 128), F32),
            pltpu.SemaphoreType.DMA((10,)),
            pltpu.SemaphoreType.DMA((4,)),
        ],
        compiler_params=pltpu.CompilerParams(vmem_limit_bytes=52 * MEBI),
        cost_estimate=pl.CostEstimate(flops=3 * 10**9, bytes_accessed=5 * 10**6, transcendentals=0),
        name="terms",
    )(jnp.reshape(dp_index, (1,)), seq_cell, got, head_row, *columns)


def final_kernel(final_ref, first_ref, second_ref, head_ref):
    left = half_lanes(10)
    for pair in range(4):
        sums = []
        for block in (2 * pair, 2 * pair + 1):
            total = final_ref[16 * block].astype(F32)
            for source in range(1, 16):
                total = total + final_ref[16 * block + source].astype(F32)
            second_ref[:, 128 * block : 128 * block + 128] = total[0:20]
            sums.append(total[20:30])
        one, two = sums
        lanes = slice(128 * pair, 128 * pair + 128)
        first_ref[0:10, lanes] = jnp.where(left, one, swap(two))
        first_ref[10:20, lanes] = jnp.where(left, swap(one), two)
    left = half_lanes(16)
    for pair in range(8):
        sums = []
        for source in (2 * pair, 2 * pair + 1):
            total = final_ref[source, 16:32, :].astype(F32)
            for block in range(1, 8):
                total = total + final_ref[16 * block + source, 16:32, :].astype(F32)
            sums.append(total + swap(total))
        head_ref[pair : pair + 1, :] = jnp.where(left, sums[0], sums[1])[14:15]


def final_part(final):
    return pl.pallas_call(
        final_kernel,
        out_shape=[
            jax.ShapeDtypeStruct((20, 512), F32),
            jax.ShapeDtypeStruct((20, 1024), F32),
            jax.ShapeDtypeStruct((8, 128), F32),
        ],
        in_specs=[VMEM],
        out_specs=[VMEM] * 3,
        compiler_params=pltpu.CompilerParams(vmem_limit_bytes=50 * MEBI),
        name="final",
    )(final)


def per_device(
    seq_in, w_first, w_second, head_vec, track_cot, donor_pos, acceptor_pos, pair_cot, live_pairs
):
    seq_index = lax.axis_index("seq")
    seq_cell = jnp.reshape(seq_index, (1,))
    dp_index = lax.axis_index("dp")
    inputs, track = seq_in[0], track_cot[0]
    right = edges(inputs, track, 16)
    message, mine, slope_first, slope_second = forward_part(
        seq_cell, live_pairs[0], inputs, right, donor_pos, acceptor_pos, pair_cot,
        w_first, w_second,
    )
    got = lax.all_to_all(message, "seq", 0, 0, tiled=True)

    mine = mine.T

    def passed(value, step):
        return lax.ppermute(value, "dp", [(i, i ^ step) for i in range(8)])

    own = [mine] + [passed(mine, step) for step in (2, 4, 6)]
    sent, head_row = pair_part(seq_cell, got, head_vec)
    back = lax.all_to_all(sent, "seq", 0, 0, tiled=True)
    back, *own = lax.optimization_barrier((back, *own))
    message, grad_1, grad_y, scores = backward_part(
        seq_cell, live_pairs[0], back, track, right, slope_first, slope_second, w_second
    )
    other = [passed(value, 1) for value in own]
    columns = [(own, other)[step % 2][step // 2] for step in range(8)]
    grads = lax.all_to_all(message, "dp", 0, 0, tiled=True)
    grad_input, tail = input_part(seq_cell, grad_y, grad_1, w_first)
    before = lax.ppermute(tail, "seq", [(i, (i + 1) % 16) for i in range(16)])
    terms = term_part(columns, grads, head_row, dp_index, seq_cell)
    terms, before = lax.optimization_barrier((terms, before))
    grad_input = jnp.concatenate([before[4:], grad_input[:244]], axis=0)
    final = lax.all_to_all(terms, ("dp", "seq"), 0, 0, tiled=True)
    out_first, out_second, grad_head = final_part(final)
    return (scores, out_first, out_second, grad_input[None], grad_head.reshape(1024))


def solution(mesh):
    in_specs = (
        P("dp", "seq", None),
        P(),
        P(),
        P(),
        P("dp", "seq", None),
        P("dp", "seq"),
        P("dp", "seq"),
        P("dp", "seq"),
        P("dp", "seq"),
    )
    out_specs = (
        P("dp", "seq"),
        P(("dp", "seq"), None),
        P(("dp", "seq"), None),
        P("dp", "seq", None),
        P(),
    )
    return jax.shard_map(
        per_device, mesh=mesh, in_specs=in_specs, out_specs=out_specs, check_vma=False
    )
```

```python
import jax
import jax.numpy as jnp
from jax import lax
from jax.experimental import pallas as pl
from jax.experimental.pallas import tpu as pltpu
from jax.sharding import PartitionSpec as P

BF = jnp.bfloat16
F32 = jnp.float32
ROOT = 0.7978845608028654
CUBE = 0.044715


def gelu_both(pre):
    square = pre * pre
    bent = jnp.tanh(ROOT * pre * (1.0 + CUBE * square))
    half = 0.5 * (1.0 + bent)
    slope = half + 0.5 * pre * (1.0 - bent * bent) * (ROOT * (1.0 + 3.0 * CUBE * square))
    return pre * half, slope


def dot(left, right, dims=((1,), (0,))):
    return lax.dot_general(left, right, (dims, ((), ())), preferred_element_type=F32)


VMEM = pl.BlockSpec(memory_space=pltpu.VMEM)
SMEM = pl.BlockSpec(memory_space=pltpu.SMEM)
HBM = pl.BlockSpec(memory_space=pltpu.HBM)
ANY = pl.BlockSpec(memory_space=pl.ANY)
MEBI = 1024 * 1024


def rounded(value):
    return value.astype(BF).astype(F32)


def half_lanes(rows):
    return lax.broadcasted_iota(jnp.int32, (rows, 128), 1) < 64


def swap(value):
    return pltpu.roll(value, 64, 1)


def started(moves, sems):
    copies = []
    for place, (source, target) in enumerate(moves):
        copies.append(pltpu.make_async_copy(source, target, sems.at[place]))
        copies[place].start()
    return copies


def wait_for(copies):
    for copy in copies:
        copy.wait()


def within(rows, seam, shift, seq_index):
    row = lax.broadcasted_iota(jnp.int32, (rows, 1), 0)
    return ((row >= seam) == (row + shift >= seam)) | (seq_index != 15)


def edge_kernel(inputs_hbm, track_hbm, out_hbm, rows_scr, track_scr, out_scr, sems):
    wait_for(
        started(
            [
                (inputs_hbm.at[pl.ds(0, 32)], rows_scr),
                (track_hbm.at[pl.ds(0, 16)], track_scr),
            ],
            sems,
        )
    )
    track = track_scr[...].astype(F32)
    pieces = [rows_scr[...].astype(F32)[:24]]
    for row in range(9):
        pieces += [track[row : row + 1, :512], track[row : row + 1, 512:]]
    pieces.append(jnp.zeros((6, 512), F32))
    out_scr[...] = jnp.concatenate(pieces, axis=0).astype(BF)
    wait_for(started([(out_scr, out_hbm)], sems))


def edges(inputs, track, count):
    first = pl.pallas_call(
        edge_kernel,
        out_shape=jax.ShapeDtypeStruct((48, 512), BF),
        in_specs=[HBM] * 2,
        out_specs=HBM,
        scratch_shapes=[
            pltpu.VMEM((32, 512), BF),
            pltpu.VMEM((16, 1024), BF),
            pltpu.VMEM((48, 512), BF),
            pltpu.SemaphoreType.DMA((2,)),
        ],
        compiler_params=pltpu.CompilerParams(vmem_limit_bytes=56 * MEBI),
        name="edges",
    )(inputs, track)
    return lax.ppermute(first, "seq", [(i, (i - 1) % count) for i in range(count)])


def forward_kernel(seq_ref, live_ref, *refs):
    sources, outs, held, staged, work = refs[:7], refs[7:11], refs[11:18], refs[18:22], refs[22:]
    inputs_ref, right_ref, first_mat, second_mat, donor_ref, accept_ref, cot_ref = held
    mess_ref, mine_ref, slope_1_ref, slope_2_ref = staged
    ext, act_scr, wide, sems, out_sems = work
    copies = started(list(zip(sources, held)), sems)

    def send(place):
        copy = pltpu.make_async_copy(staged[place], outs[place], out_sems.at[place])
        copy.start()
        return copy

    seq_index = seq_ref[0]
    ext[0:32, :] = jnp.zeros((32, 512), F32)
    ext[288:320, :] = jnp.zeros((32, 512), F32)
    wait_for(copies[:2])
    ext[20:276, :] = inputs_ref[...].astype(F32)
    ext[276:300, :] = right_ref[...].astype(F32)[:24]
    taps = jnp.concatenate(
        [
            jnp.where(within(288, 260, k - 2, seq_index), ext[14 + k : 302 + k, :], 0.0).astype(BF)
            for k in range(5)
        ],
        axis=1,
    )
    copies[2].wait()
    pre = dot(taps, first_mat[...])
    act, slope = gelu_both(pre)
    slope_1_ref[...] = slope
    sent = [send(2)]
    y_first = ext[16:304, :] + act
    for tile in range(4):
        lanes = slice(128 * tile, 128 * tile + 128)
        act_scr[288 * tile : 288 * tile + 288, :] = y_first[:, lanes]
        even = act_scr[pl.ds(288 * tile, 144, 2), :]
        wide[8:152, lanes] = even + act_scr[pl.ds(288 * tile + 1, 144, 2), :]
    pooled = 0.5 * wide[8:152, :]
    wide[0:8, :] = jnp.zeros((8, 512), F32)
    wide[152:160, :] = jnp.zeros((8, 512), F32)
    wide[8:152, :] = pooled
    mine_ref[0:256, :] = ext[32:288, :].astype(BF)
    mine_ref[256:384, :] = wide[16:144, :].astype(BF)
    sent.append(send(1))
    taps = jnp.concatenate(
        [
            jnp.where(within(144, 130, k - 2, seq_index), wide[6 + k : 150 + k, :], 0.0).astype(BF)
            for k in range(5)
        ],
        axis=1,
    )
    copies[3].wait()
    pre = dot(taps, second_mat[...])
    act, slope = gelu_both(pre)
    slope_2_ref[0:144, :] = slope
    far = right_ref[...].astype(F32)
    far = [
        jnp.concatenate([far[row : row + 1], far[row + 1 : row + 2]], axis=1)
        for row in range(24, 42, 2)
    ]
    slope_2_ref[144:160, :] = jnp.concatenate(far + [jnp.zeros((7, 1024), F32)], axis=0)
    sent.append(send(3))
    wait_for(copies[4:])

    same = lax.broadcasted_iota(jnp.int32, (16, 16), 0) == lax.broadcasted_iota(
        jnp.int32, (16, 16), 1
    )

    def column(row):
        return jnp.sum(jnp.where(same, row, 0.0), axis=1, keepdims=True)

    donor, accept = (donor_ref[...] - 6) & 2047, (accept_ref[...] - 6) & 2047
    live = lax.broadcasted_iota(jnp.int32, (1, 16), 1) < live_ref[0]
    weight = column(jnp.where(live, cot_ref[...], 0.0) * (1024 ** -0.5))
    lane = lax.broadcasted_iota(jnp.int32, (16, 128), 1)
    info = jnp.zeros((16, 128), F32)
    for place, value in enumerate(
        [
            column((donor >> 6).astype(F32)),
            column((donor & 63).astype(F32)),
            column((accept >> 6).astype(F32)),
            column((accept & 63).astype(F32)),
            weight,
            weight - rounded(weight),
        ]
    ):
        info = jnp.where(lane == place, value, info)
    info = info.astype(BF)
    left = half_lanes(64)
    for pair in range(8):
        top = act[8:72, 128 * pair : 128 * pair + 128]
        low = act[72:136, 128 * pair : 128 * pair + 128]
        mess_ref[2 * pair, 0:64, :] = jnp.where(left, top, swap(low)).astype(BF)
        mess_ref[2 * pair + 1, 0:64, :] = jnp.where(left, swap(top), low).astype(BF)
    for target in range(16):
        mess_ref[target, 64:80, :] = info
    sent.append(send(0))
    wait_for(sent)


def forward_part(seq_index, live, inputs, right, donor, accept, cot, w_first, w_second):
    return pl.pallas_call(
        forward_kernel,
        out_shape=[
            jax.ShapeDtypeStruct((16, 80, 128), BF),
            jax.ShapeDtypeStruct((384, 512), BF),
            jax.ShapeDtypeStruct((288, 512), F32),
            jax.ShapeDtypeStruct((160, 1024), F32),
        ],
        in_specs=[SMEM, SMEM, HBM, ANY] + [HBM] * 5,
        out_specs=[HBM] * 4,
        scratch_shapes=[
            pltpu.VMEM((256, 512), BF),
            pltpu.VMEM((48, 512), BF),
            pltpu.VMEM((2560, 512), BF),
            pltpu.VMEM((2560, 1024), BF),
            pltpu.VMEM((1, 16), jnp.int32),
            pltpu.VMEM((1, 16), jnp.int32),
            pltpu.VMEM((1, 16), F32),
            pltpu.VMEM((16, 80, 128), BF),
            pltpu.VMEM((384, 512), BF),
            pltpu.VMEM((288, 512), F32),
            pltpu.VMEM((160, 1024), F32),
            pltpu.VMEM((320, 512), F32),
            pltpu.VMEM((1152, 128), F32),
            pltpu.VMEM((160, 512), F32),
            pltpu.SemaphoreType.DMA((7,)),
            pltpu.SemaphoreType.DMA((4,)),
        ],
        compiler_params=pltpu.CompilerParams(vmem_limit_bytes=56 * MEBI),
        cost_estimate=pl.CostEstimate(
            flops=15 * 10**8, bytes_accessed=10 * 10**6, transcendentals=3 * 10**5
        ),
        name="forward",
    )(
        seq_index, live, inputs, right,
        w_first.reshape(2560, 512), w_second.reshape(2560, 1024), donor, accept, cot,
    )


def pair_kernel(
    seq_ref, got_ref, head_hbm, sent_hbm, term_hbm, head_ref, sent_ref, term_ref, sems
):
    head_copy = started([(head_hbm, head_ref)], sems)
    seq_index = seq_ref[0]
    flat = jnp.concatenate([got_ref[i] for i in range(16)], axis=0)
    info = jnp.concatenate([got_ref[i, 64:80, :].astype(F32) for i in range(16)], axis=0)
    donor = (info[:, 0:1] * 64.0 + info[:, 1:2]).astype(jnp.int32)
    accept = (info[:, 2:3] * 64.0 + info[:, 3:4]).astype(jnp.int32)
    weight = info[:, 4:5] + info[:, 5:6]
    spots = jnp.concatenate([donor, accept], axis=0)
    row_of = (spots >> 7) * 80 + (spots & 63)
    pick = (row_of == lax.broadcasted_iota(jnp.int32, (512, 1280), 1)).astype(F32).astype(BF)
    rows = dot(pick, flat)
    rows = jnp.where((spots & 127) < 64, rows, swap(rows))[:, :64]
    donor_rows, accept_rows = rows[:256], rows[256:]
    both = donor_rows * accept_rows
    wait_for(head_copy)
    head_row = head_ref[pl.ds(seq_index // 2, 1), :]
    head_row = jnp.where(seq_index % 2 == 0, head_row, swap(head_row))[:, :64]
    partial = jnp.sum(both * head_row, axis=1, keepdims=True)
    term = jnp.sum(weight * both, axis=0, keepdims=True)
    term_high = rounded(term)
    term_ref[...] = jnp.concatenate([term_high, term - term_high], axis=1)
    copies = [pltpu.make_async_copy(term_ref, term_hbm, sems.at[4])]
    copies[0].start()
    scaled = weight * head_row
    grads = jnp.concatenate([scaled * accept_rows, scaled * donor_rows], axis=0)
    blank = jnp.zeros((512, 64), F32)
    grads = jnp.concatenate(
        [
            jnp.concatenate([grads, blank], axis=1),
            jnp.concatenate([blank, grads], axis=1),
        ],
        axis=0,
    ).astype(BF)
    lane = lax.broadcasted_iota(jnp.int32, (256, 128), 1)
    turned = jnp.where(
        lane == 0,
        donor.astype(F32),
        jnp.where(lane == 1, accept.astype(F32), jnp.where(lane == 2, partial, 0.0)),
    ).T
    spot_row = jnp.concatenate([turned[0:1, :], turned[1:2, :]], axis=1).astype(jnp.int32)
    high = rounded(turned[2:3, :])
    rest = turned[2:3, :] - high
    extra = jnp.concatenate(
        [
            jnp.zeros((4, 128), F32),
            high[:, :128],
            high[:, 128:],
            rest[:, :128],
            rest[:, 128:],
            jnp.zeros((8, 128), F32),
        ],
        axis=0,
    )
    index = lax.broadcasted_iota(jnp.int32, (80, 1), 0)
    low_row = jnp.where(index < 64, index, index - 67)
    high_row = index + 64
    for group in range(4):
        picks = []
        for target in range(4 * group, 4 * group + 4):
            base = 128 * target
            low_pick = jnp.where(index < 67, (low_row + base) & 2047, -1) == spot_row
            high_pick = jnp.where(index < 67, (high_row + base) & 2047, -1) == spot_row
            picks.append(jnp.concatenate([low_pick.astype(F32), high_pick.astype(F32)], axis=1))
        pieces = dot(jnp.concatenate(picks, axis=0).astype(BF), grads)
        for place in range(4):
            target = 4 * group + place
            piece = pieces[80 * place : 80 * place + 80]
            sent_ref[target, 0:64, :] = piece[0:64].astype(BF)
            sent_ref[target, 64:80, :] = (piece[64:80] + extra).astype(BF)
        part = pl.ds(4 * group, 4)
        copies.append(pltpu.make_async_copy(sent_ref.at[part], sent_hbm.at[part], sems.at[group]))
        copies[-1].start()
    wait_for(copies)


def pair_part(seq_index, got, head_vec):
    return pl.pallas_call(
        pair_kernel,
        out_shape=[
            jax.ShapeDtypeStruct((16, 80, 128), BF),
            jax.ShapeDtypeStruct((1, 128), F32),
        ],
        in_specs=[SMEM, VMEM, HBM],
        out_specs=[HBM] * 2,
        scratch_shapes=[
            pltpu.VMEM((8, 128), F32),
            pltpu.VMEM((16, 80, 128), BF),
            pltpu.VMEM((1, 128), F32),
            pltpu.SemaphoreType.DMA((5,)),
        ],
        compiler_params=pltpu.CompilerParams(vmem_limit_bytes=52 * MEBI),
        cost_estimate=pl.CostEstimate(
            flops=5 * 10**8, bytes_accessed=10**6, transcendentals=0
        ),
        name="pairs",
    )(seq_index, got, head_vec.reshape(8, 128))


def backward_kernel(seq_ref, live_ref, back_ref, *refs):
    sources, second_hbm, outs = refs[:3], refs[3], refs[4:8]
    held, second_mat, staged = refs[8:11], refs[11], refs[12:16]
    track_ref, slope_2_ref, slope_1_ref = held
    mess_ref, grad_1_ref, grad_y_ref, scores_ref = staged
    wide, grad_y, grad_1, sems, out_sems = refs[16:]
    seq_index = seq_ref[0]
    parts = [pl.ds(512 * k, 512) for k in range(5)]
    copies = started(
        list(zip(sources, held)) + [(second_hbm.at[part], second_mat.at[part]) for part in parts],
        sems,
    )

    def send(place, part, sem):
        copy = pltpu.make_async_copy(part(staged[place]), part(outs[place]), out_sems.at[sem])
        copy.start()
        return copy

    def all_of(ref):
        return ref

    left = half_lanes(64)
    edge = half_lanes(16)
    wide[0:16, :] = jnp.zeros((16, 1024), F32)
    wide[144:160, :] = jnp.zeros((16, 1024), F32)
    for pair in range(8):
        lanes = slice(128 * pair, 128 * pair + 128)
        one = back_ref[2 * pair, 0:64, :].astype(F32)
        two = back_ref[2 * pair + 1, 0:64, :].astype(F32)
        wide[16:80, lanes] = jnp.where(left, one, swap(two))
        wide[80:144, lanes] = jnp.where(left, swap(one), two)
        one = back_ref[2 * pair, 64:80, :].astype(F32)
        two = back_ref[2 * pair + 1, 64:80, :].astype(F32)
        wide[13:16, lanes] = jnp.where(edge, one, swap(two))[0:3]
        wide[144:147, lanes] = jnp.where(edge, swap(one), two)[0:3]
    copies[0].wait()
    wide[13:138, :] = wide[13:138, :] + track_ref[...].astype(F32)[3:128]
    copies[1].wait()
    wide[138:147, :] = wide[138:147, :] + slope_2_ref[144:153, :]
    wide[8:152, :] = wide[8:152, :] * slope_2_ref[0:144, :]
    for target in range(8):
        mess_ref[target, 144:288, :] = wide[8:152, 128 * target : 128 * target + 128].astype(BF)
    sent = [send(0, lambda ref: ref.at[:, pl.ds(144, 144)], 0)]
    pooled = jnp.zeros((144, 512), F32)
    for k in range(5):
        copies[3 + k].wait()
        pooled = pooled + dot(
            jnp.where(within(144, 130, 2 - k, seq_index), wide[10 - k : 154 - k, :], 0.0).astype(BF),
            second_mat[512 * k : 512 * k + 512, :],
            ((1,), (1,)),
        )
    pooled = 0.5 * pooled
    copies[2].wait()
    for tile in range(4):
        lanes = slice(128 * tile, 128 * tile + 128)
        grad_y[pl.ds(288 * tile, 144, 2), :] = pooled[:, lanes]
        grad_y[pl.ds(288 * tile + 1, 144, 2), :] = pooled[:, lanes]
        value = grad_y[288 * tile : 288 * tile + 288, :]
        grad_y_ref[:, lanes] = value[16:272]
        value = value * slope_1_ref[:, lanes]
        grad_1[:, lanes] = value
        grad_1_ref[:, lanes] = value.astype(BF)
    sent += [send(1, all_of, 1), send(2, all_of, 2)]
    left = half_lanes(144)
    for pair in range(4):
        lanes = slice(128 * pair, 128 * pair + 128)
        one = grad_1[8:152, lanes]
        two = grad_1[136:280, lanes]
        mess_ref[2 * pair, 0:144, :] = jnp.where(left, one, swap(two)).astype(BF)
        mess_ref[2 * pair + 1, 0:144, :] = jnp.where(left, swap(one), two).astype(BF)
    sent.append(send(0, lambda ref: ref.at[:, pl.ds(0, 144)], 3))
    total = jnp.zeros((16, 128), F32)
    for source in range(16):
        total = total + back_ref[source, 64:80, :].astype(F32)
    row = jnp.where(seq_index < 8, total[4:5] + total[6:7], total[5:6] + total[7:8])
    row = pltpu.roll(row, 128 - 16 * (seq_index % 8), 1)[:, :16]
    live = lax.broadcasted_iota(jnp.int32, (1, 16), 1) < live_ref[0]
    scores_ref[...] = jnp.where(live, row * (1024 ** -0.5), 0.0)
    sent.append(send(3, all_of, 4))
    wait_for(sent)


def backward_part(seq_cell, live, back, track, slope_first, slope_second, w_second):
    return pl.pallas_call(
        backward_kernel,
        out_shape=[
            jax.ShapeDtypeStruct((8, 288, 128), BF),
            jax.ShapeDtypeStruct((288, 512), BF),
            jax.ShapeDtypeStruct((256, 512), F32),
            jax.ShapeDtypeStruct((1, 16), F32),
        ],
        in_specs=[SMEM] * 2 + [VMEM] + [HBM] * 4,
        out_specs=[HBM] * 4,
        scratch_shapes=[
            pltpu.VMEM((128, 1024), BF),
            pltpu.VMEM((160, 1024), F32),
            pltpu.VMEM((288, 512), F32),
            pltpu.VMEM((2560, 1024), BF),
            pltpu.VMEM((8, 288, 128), BF),
            pltpu.VMEM((288, 512), BF),
            pltpu.VMEM((256, 512), F32),
            pltpu.VMEM((1, 16), F32),
            pltpu.VMEM((160, 1024), F32),
            pltpu.VMEM((1152, 128), F32),
            pltpu.VMEM((288, 512), F32),
            pltpu.SemaphoreType.DMA((8,)),
            pltpu.SemaphoreType.DMA((5,)),
        ],
        compiler_params=pltpu.CompilerParams(vmem_limit_bytes=52 * MEBI),
        cost_estimate=pl.CostEstimate(
            flops=8 * 10**8, bytes_accessed=10 * 10**6, transcendentals=0
        ),
        name="backward",
    )(
        seq_cell, live, back, track, slope_second, slope_first,
        w_second.reshape(2560, 1024),
    )


def input_kernel(seq_ref, *refs):
    sources, (out_ref, tail_ref), held, (grad_1, sems) = refs[:3], refs[3:5], refs[5:8], refs[8:]
    grad_ref, grad_y_ref, first_mat = held
    copies = started(list(zip(sources, held)), sems)
    copies[0].wait()
    grad_1[...] = grad_ref[...].astype(F32)
    wait_for(copies[1:])
    total = grad_y_ref[...]
    for k in range(5):
        rows = jnp.where(within(256, 244, 2 - k, seq_ref[0]), grad_1[18 - k : 274 - k, :], 0.0)
        total = total + dot(
            rows.astype(BF), first_mat[512 * k : 512 * k + 512, :], ((1,), (1,))
        )
    out_ref[...] = total.astype(BF)
    tail_ref[...] = total[240:256].astype(BF)


def input_part(seq_cell, grad_y, grad_first_pre, w_first):
    return pl.pallas_call(
        input_kernel,
        out_shape=[
            jax.ShapeDtypeStruct((256, 512), BF),
            jax.ShapeDtypeStruct((16, 512), BF),
        ],
        in_specs=[SMEM] + [HBM] * 3,
        out_specs=[VMEM] * 2,
        scratch_shapes=[
            pltpu.VMEM((288, 512), BF),
            pltpu.VMEM((256, 512), F32),
            pltpu.VMEM((2560, 512), BF),
            pltpu.VMEM((288, 512), F32),
            pltpu.SemaphoreType.DMA((3,)),
        ],
        compiler_params=pltpu.CompilerParams(vmem_limit_bytes=52 * MEBI),
        cost_estimate=pl.CostEstimate(
            flops=7 * 10**8, bytes_accessed=4 * 10**6, transcendentals=0
        ),
        name="inputs",
    )(seq_cell, grad_first_pre, grad_y, w_first.reshape(2560, 512))


def term_kernel(dp_ref, seq_ref, *refs):
    sources, out_hbm, held, out_ref = refs[:10], refs[10], refs[11:21], refs[21]
    part_scr, wide_1, wide_2, sum_1, sum_2, mess, sems, out_sems = refs[22:]
    got_ref, head_ref, columns = held[0], held[1], held[2:]
    copies = started(list(zip(sources, held)), sems)
    copies[0].wait()
    left = half_lanes(128)
    fit_1 = [half_lanes(16) | within(16, 4, 2 - k, seq_ref[0]) for k in range(5)]
    fit_2 = [within(16, 10, 2 - k, seq_ref[0]) for k in range(5)]
    for step in range(8):
        part_scr[...] = got_ref[dp_ref[0] ^ step].astype(F32)
        taps = []
        for k in range(5):
            ends = jnp.where(fit_1[k], part_scr[122 - k : 138 - k, :], 0.0)
            taps.append(jnp.concatenate([part_scr[10 - k : 122 - k, :], ends], axis=0))
            lanes = slice(128 * k, 128 * k + 128)
            wide_2[128 * step : 128 * step + 112, lanes] = part_scr[154 - k : 266 - k, :].astype(BF)
            wide_2[128 * step + 112 : 128 * step + 128, lanes] = jnp.where(
                fit_2[k], part_scr[266 - k : 282 - k, :], 0.0
            ).astype(BF)
        top = [
            jnp.where(left, taps[0], swap(taps[1])),
            jnp.where(left, taps[2], swap(taps[3])),
            taps[4],
        ]
        low = [
            jnp.where(left, swap(taps[0]), taps[1]),
            jnp.where(left, swap(taps[2]), taps[3]),
            swap(taps[4]),
        ]
        for place in range(3):
            lanes = slice(128 * place, 128 * place + 128)
            wide_1[256 * step : 256 * step + 128, lanes] = top[place].astype(BF)
            wide_1[256 * step + 128 : 256 * step + 256, lanes] = low[place].astype(BF)
    wait_for(copies[1:])
    lefts = jnp.concatenate([ref[:, 0:256] for ref in columns], axis=1)
    first = dot(lefts, wide_1[...])
    lefts = jnp.concatenate([ref[:, 256:384] for ref in columns], axis=1)
    second = dot(lefts, wide_2[...])
    left = half_lanes(512)
    for k in range(5):
        sum_2[512 * k : 512 * k + 512, :] = second[:, 128 * k : 128 * k + 128]
        tile = first[:, 128 * (k // 2) : 128 * (k // 2) + 128]
        turned = swap(tile)
        sum_1[512 * k : 512 * k + 512, :] = (
            jnp.where(left, tile, turned) if k % 2 == 0 else jnp.where(left, turned, tile)
        )
    left = half_lanes(10)
    head = jnp.concatenate([head_ref[...], jnp.zeros((1, 128), F32)], axis=0)
    sent = []
    for owner in range(128):
        row = 20 * owner
        slot = owner % 4
        mess[slot, 0:20, :] = sum_2[row : row + 20, :]
        mess[slot, 20:30, :] = jnp.where(
            left, sum_1[row : row + 10, :], sum_1[row + 10 : row + 20, :]
        )
        if owner < 4:
            mess[slot, 30:32, :] = head
        out_ref[owner] = mess[slot].astype(BF)
        if owner % 32 == 31:
            part = pl.ds(owner - 31, 32)
            sent.append(
                pltpu.make_async_copy(out_ref.at[part], out_hbm.at[part], out_sems.at[owner // 32])
            )
            sent[-1].start()
    wait_for(sent)


def term_part(columns, got, head_row, dp_index, seq_cell):
    return pl.pallas_call(
        term_kernel,
        out_shape=jax.ShapeDtypeStruct((128, 32, 128), BF),
        in_specs=[SMEM] * 2 + [ANY] * 2 + [HBM] * 8,
        out_specs=HBM,
        scratch_shapes=[
            pltpu.VMEM((8, 288, 128), BF),
            pltpu.VMEM((1, 128), F32),
        ]
        + [pltpu.VMEM((512, 384), BF)] * 8
        + [
            pltpu.VMEM((128, 32, 128), BF),
            pltpu.VMEM((288, 128), F32),
            pltpu.VMEM((2048, 384), BF),
            pltpu.VMEM((1024, 640), BF),
            pltpu.VMEM((2560, 128), F32),
            pltpu.VMEM((2560, 128), F32),
            pltpu.VMEM((4, 32, 128), F32),
            pltpu.SemaphoreType.DMA((10,)),
            pltpu.SemaphoreType.DMA((4,)),
        ],
        compiler_params=pltpu.CompilerParams(vmem_limit_bytes=52 * MEBI),
        cost_estimate=pl.CostEstimate(flops=3 * 10**9, bytes_accessed=5 * 10**6, transcendentals=0),
        name="terms",
    )(jnp.reshape(dp_index, (1,)), seq_cell, got, head_row, *columns)


def final_kernel(final_ref, first_ref, second_ref, head_ref):
    left = half_lanes(10)
    for pair in range(4):
        sums = []
        for block in (2 * pair, 2 * pair + 1):
            total = final_ref[16 * block].astype(F32)
            for source in range(1, 16):
                total = total + final_ref[16 * block + source].astype(F32)
            second_ref[:, 128 * block : 128 * block + 128] = total[0:20]
            sums.append(total[20:30])
        one, two = sums
        lanes = slice(128 * pair, 128 * pair + 128)
        first_ref[0:10, lanes] = jnp.where(left, one, swap(two))
        first_ref[10:20, lanes] = jnp.where(left, swap(one), two)
    left = half_lanes(16)
    for pair in range(8):
        sums = []
        for source in (2 * pair, 2 * pair + 1):
            total = final_ref[source, 16:32, :].astype(F32)
            for block in range(1, 8):
                total = total + final_ref[16 * block + source, 16:32, :].astype(F32)
            sums.append(total + swap(total))
        head_ref[pair : pair + 1, :] = jnp.where(left, sums[0], sums[1])[14:15]


def final_part(final):
    return pl.pallas_call(
        final_kernel,
        out_shape=[
            jax.ShapeDtypeStruct((20, 512), F32),
            jax.ShapeDtypeStruct((20, 1024), F32),
            jax.ShapeDtypeStruct((8, 128), F32),
        ],
        in_specs=[VMEM],
        out_specs=[VMEM] * 3,
        compiler_params=pltpu.CompilerParams(vmem_limit_bytes=50 * MEBI),
        name="final",
    )(final)


def per_device(
    seq_in, w_first, w_second, head_vec, track_cot, donor_pos, acceptor_pos, pair_cot, live_pairs
):
    seq_index = lax.axis_index("seq")
    seq_cell = jnp.reshape(seq_index, (1,))
    dp_index = lax.axis_index("dp")
    inputs, track = seq_in[0], track_cot[0]
    right = edges(inputs, track, 16)
    message, mine, slope_first, slope_second = forward_part(
        seq_cell, live_pairs[0], inputs, right, donor_pos, acceptor_pos, pair_cot,
        w_first, w_second,
    )
    got = lax.all_to_all(message, "seq", 0, 0, tiled=True)

    mine = mine.T

    def passed(value, step):
        return lax.ppermute(value, "dp", [(i, i ^ step) for i in range(8)])

    own = [mine] + [passed(mine, step) for step in (2, 4, 6)]
    sent, head_row = pair_part(seq_cell, got, head_vec)
    back = lax.all_to_all(sent, "seq", 0, 0, tiled=True)
    back, *own = lax.optimization_barrier((back, *own))
    message, grad_1, grad_y, scores = backward_part(
        seq_cell, live_pairs[0], back, track, slope_first, slope_second, w_second
    )
    other = [passed(value, 1) for value in own]
    columns = [(own, other)[step % 2][step // 2] for step in range(8)]
    grads = lax.all_to_all(message, "dp", 0, 0, tiled=True)
    grad_input, tail = input_part(seq_cell, grad_y, grad_1, w_first)
    before = lax.ppermute(tail, "seq", [(i, (i + 1) % 16) for i in range(16)])
    terms = term_part(columns, grads, head_row, dp_index, seq_cell)
    terms, before = lax.optimization_barrier((terms, before))
    grad_input = jnp.concatenate([before[4:], grad_input[:244]], axis=0)
    final = lax.all_to_all(terms, ("dp", "seq"), 0, 0, tiled=True)
    out_first, out_second, grad_head = final_part(final)
    return (scores, out_first, out_second, grad_input[None], grad_head.reshape(1024))


def solution(mesh):
    in_specs = (
        P("dp", "seq", None),
        P(),
        P(),
        P(),
        P("dp", "seq", None),
        P("dp", "seq"),
        P("dp", "seq"),
        P("dp", "seq"),
        P("dp", "seq"),
    )
    out_specs = (
        P("dp", "seq"),
        P(("dp", "seq"), None),
        P(("dp", "seq"), None),
        P("dp", "seq", None),
        P(),
    )
    return jax.shard_map(
        per_device, mesh=mesh, in_specs=in_specs, out_specs=out_specs, check_vma=False
    )
```

```python
import jax
import jax.numpy as jnp
from jax import lax
from jax.experimental import pallas as pl
from jax.experimental.pallas import tpu as pltpu
from jax.sharding import PartitionSpec as P

BF = jnp.bfloat16
F32 = jnp.float32
ROOT = 0.7978845608028654
CUBE = 0.044715


def gelu_both(pre):
    square = pre * pre
    bent = jnp.tanh(ROOT * pre * (1.0 + CUBE * square))
    half = 0.5 * (1.0 + bent)
    slope = half + 0.5 * pre * (1.0 - bent * bent) * (ROOT * (1.0 + 3.0 * CUBE * square))
    return pre * half, slope


def dot(left, right, dims=((1,), (0,))):
    return lax.dot_general(left, right, (dims, ((), ())), preferred_element_type=F32)


VMEM = pl.BlockSpec(memory_space=pltpu.VMEM)
SMEM = pl.BlockSpec(memory_space=pltpu.SMEM)
HBM = pl.BlockSpec(memory_space=pltpu.HBM)
ANY = pl.BlockSpec(memory_space=pl.ANY)
MEBI = 1024 * 1024


def rounded(value):
    return value.astype(BF).astype(F32)


def half_lanes(rows):
    return lax.broadcasted_iota(jnp.int32, (rows, 128), 1) < 64


def swap(value):
    return pltpu.roll(value, 64, 1)


def started(moves, sems):
    copies = []
    for place, (source, target) in enumerate(moves):
        copies.append(pltpu.make_async_copy(source, target, sems.at[place]))
        copies[place].start()
    return copies


def wait_for(copies):
    for copy in copies:
        copy.wait()


def within(rows, seam, shift, seq_index):
    row = lax.broadcasted_iota(jnp.int32, (rows, 1), 0)
    return ((row >= seam) == (row + shift >= seam)) | (seq_index != 15)


def edge_kernel(inputs_hbm, track_hbm, out_hbm, rows_scr, track_scr, out_scr, sems):
    wait_for(
        started(
            [
                (inputs_hbm.at[pl.ds(0, 32)], rows_scr),
                (track_hbm.at[pl.ds(0, 16)], track_scr),
            ],
            sems,
        )
    )
    track = track_scr[...].astype(F32)
    pieces = [rows_scr[...].astype(F32)[:24]]
    for row in range(9):
        pieces += [track[row : row + 1, :512], track[row : row + 1, 512:]]
    pieces.append(jnp.zeros((6, 512), F32))
    out_scr[...] = jnp.concatenate(pieces, axis=0).astype(BF)
    wait_for(started([(out_scr, out_hbm)], sems))


def edges(inputs, track, count):
    first = pl.pallas_call(
        edge_kernel,
        out_shape=jax.ShapeDtypeStruct((48, 512), BF),
        in_specs=[HBM] * 2,
        out_specs=HBM,
        scratch_shapes=[
            pltpu.VMEM((32, 512), BF),
            pltpu.VMEM((16, 1024), BF),
            pltpu.VMEM((48, 512), BF),
            pltpu.SemaphoreType.DMA((2,)),
        ],
        compiler_params=pltpu.CompilerParams(vmem_limit_bytes=56 * MEBI),
        name="edges",
    )(inputs, track)
    return lax.ppermute(first, "seq", [(i, (i - 1) % count) for i in range(count)])


def forward_kernel(seq_ref, live_ref, *refs):
    sources, outs, held, staged, work = refs[:7], refs[7:11], refs[11:18], refs[18:22], refs[22:]
    inputs_ref, right_ref, first_mat, second_mat, donor_ref, accept_ref, cot_ref = held
    mess_ref, mine_ref, slope_1_ref, slope_2_ref = staged
    ext, act_scr, wide, sems, out_sems = work
    copies = started(list(zip(sources, held)), sems)

    def send(place):
        copy = pltpu.make_async_copy(staged[place], outs[place], out_sems.at[place])
        copy.start()
        return copy

    seq_index = seq_ref[0]
    ext[0:32, :] = jnp.zeros((32, 512), F32)
    ext[288:320, :] = jnp.zeros((32, 512), F32)
    wait_for(copies[:2])
    ext[20:276, :] = inputs_ref[...].astype(F32)
    ext[276:300, :] = right_ref[...].astype(F32)[:24]
    taps = jnp.concatenate(
        [
            jnp.where(within(288, 260, k - 2, seq_index), ext[14 + k : 302 + k, :], 0.0).astype(BF)
            for k in range(5)
        ],
        axis=1,
    )
    copies[2].wait()
    pre = dot(taps, first_mat[...])
    act, slope = gelu_both(pre)
    slope_1_ref[...] = slope
    sent = [send(2)]
    y_first = ext[16:304, :] + act
    for tile in range(4):
        lanes = slice(128 * tile, 128 * tile + 128)
        act_scr[288 * tile : 288 * tile + 288, :] = y_first[:, lanes]
        even = act_scr[pl.ds(288 * tile, 144, 2), :]
        wide[8:152, lanes] = even + act_scr[pl.ds(288 * tile + 1, 144, 2), :]
    pooled = 0.5 * wide[8:152, :]
    wide[0:8, :] = jnp.zeros((8, 512), F32)
    wide[152:160, :] = jnp.zeros((8, 512), F32)
    wide[8:152, :] = pooled
    mine_ref[0:256, :] = ext[32:288, :].astype(BF)
    mine_ref[256:384, :] = wide[16:144, :].astype(BF)
    sent.append(send(1))
    taps = jnp.concatenate(
        [
            jnp.where(within(144, 130, k - 2, seq_index), wide[6 + k : 150 + k, :], 0.0).astype(BF)
            for k in range(5)
        ],
        axis=1,
    )
    copies[3].wait()
    pre = dot(taps, second_mat[...])
    act, slope = gelu_both(pre)
    slope_2_ref[0:144, :] = slope
    far = right_ref[...].astype(F32)
    far = [
        jnp.concatenate([far[row : row + 1], far[row + 1 : row + 2]], axis=1)
        for row in range(24, 42, 2)
    ]
    slope_2_ref[144:160, :] = jnp.concatenate(far + [jnp.zeros((7, 1024), F32)], axis=0)
    sent.append(send(3))
    wait_for(copies[4:])

    same = lax.broadcasted_iota(jnp.int32, (16, 16), 0) == lax.broadcasted_iota(
        jnp.int32, (16, 16), 1
    )

    def column(row):
        return jnp.sum(jnp.where(same, row, 0.0), axis=1, keepdims=True)

    donor, accept = (donor_ref[...] - 6) & 2047, (accept_ref[...] - 6) & 2047
    live = lax.broadcasted_iota(jnp.int32, (1, 16), 1) < live_ref[0]
    weight = column(jnp.where(live, cot_ref[...], 0.0) * (1024 ** -0.5))
    lane = lax.broadcasted_iota(jnp.int32, (16, 128), 1)
    info = jnp.zeros((16, 128), F32)
    for place, value in enumerate(
        [
            column((donor >> 6).astype(F32)),
            column((donor & 63).astype(F32)),
            column((accept >> 6).astype(F32)),
            column((accept & 63).astype(F32)),
            weight,
            weight - rounded(weight),
        ]
    ):
        info = jnp.where(lane == place, value, info)
    info = info.astype(BF)
    left = half_lanes(64)
    for pair in range(8):
        top = act[8:72, 128 * pair : 128 * pair + 128]
        low = act[72:136, 128 * pair : 128 * pair + 128]
        mess_ref[2 * pair, 0:64, :] = jnp.where(left, top, swap(low)).astype(BF)
        mess_ref[2 * pair + 1, 0:64, :] = jnp.where(left, swap(top), low).astype(BF)
    for target in range(16):
        mess_ref[target, 64:80, :] = info
    sent.append(send(0))
    wait_for(sent)


def forward_part(seq_index, live, inputs, right, donor, accept, cot, w_first, w_second):
    return pl.pallas_call(
        forward_kernel,
        out_shape=[
            jax.ShapeDtypeStruct((16, 80, 128), BF),
            jax.ShapeDtypeStruct((384, 512), BF),
            jax.ShapeDtypeStruct((288, 512), F32),
            jax.ShapeDtypeStruct((160, 1024), F32),
        ],
        in_specs=[SMEM, SMEM, HBM, ANY] + [HBM] * 5,
        out_specs=[HBM] * 4,
        scratch_shapes=[
            pltpu.VMEM((256, 512), BF),
            pltpu.VMEM((48, 512), BF),
            pltpu.VMEM((2560, 512), BF),
            pltpu.VMEM((2560, 1024), BF),
            pltpu.VMEM((1, 16), jnp.int32),
            pltpu.VMEM((1, 16), jnp.int32),
            pltpu.VMEM((1, 16), F32),
            pltpu.VMEM((16, 80, 128), BF),
            pltpu.VMEM((384, 512), BF),
            pltpu.VMEM((288, 512), F32),
            pltpu.VMEM((160, 1024), F32),
            pltpu.VMEM((320, 512), F32),
            pltpu.VMEM((1168, 128), F32),
            pltpu.VMEM((160, 512), F32),
            pltpu.SemaphoreType.DMA((7,)),
            pltpu.SemaphoreType.DMA((4,)),
        ],
        compiler_params=pltpu.CompilerParams(vmem_limit_bytes=56 * MEBI),
        cost_estimate=pl.CostEstimate(
            flops=15 * 10**8, bytes_accessed=10 * 10**6, transcendentals=3 * 10**5
        ),
        name="forward",
    )(
        seq_index, live, inputs, right,
        w_first.reshape(2560, 512), w_second.reshape(2560, 1024), donor, accept, cot,
    )


def pair_kernel(
    seq_ref, got_ref, head_hbm, sent_hbm, term_hbm, head_ref, sent_ref, term_ref, sems
):
    head_copy = started([(head_hbm, head_ref)], sems)
    seq_index = seq_ref[0]
    flat = jnp.concatenate([got_ref[i] for i in range(16)], axis=0)
    info = jnp.concatenate([got_ref[i, 64:80, :].astype(F32) for i in range(16)], axis=0)
    donor = (info[:, 0:1] * 64.0 + info[:, 1:2]).astype(jnp.int32)
    accept = (info[:, 2:3] * 64.0 + info[:, 3:4]).astype(jnp.int32)
    weight = info[:, 4:5] + info[:, 5:6]
    spots = jnp.concatenate([donor, accept], axis=0)
    row_of = (spots >> 7) * 80 + (spots & 63)
    pick = (row_of == lax.broadcasted_iota(jnp.int32, (512, 1280), 1)).astype(F32).astype(BF)
    rows = dot(pick, flat)
    rows = jnp.where((spots & 127) < 64, rows, swap(rows))[:, :64]
    donor_rows, accept_rows = rows[:256], rows[256:]
    both = donor_rows * accept_rows
    wait_for(head_copy)
    head_row = head_ref[pl.ds(seq_index // 2, 1), :]
    head_row = jnp.where(seq_index % 2 == 0, head_row, swap(head_row))[:, :64]
    partial = jnp.sum(both * head_row, axis=1, keepdims=True)
    term = jnp.sum(weight * both, axis=0, keepdims=True)
    term_high = rounded(term)
    term_ref[...] = jnp.concatenate([term_high, term - term_high], axis=1)
    copies = [pltpu.make_async_copy(term_ref, term_hbm, sems.at[4])]
    copies[0].start()
    scaled = weight * head_row
    grads = jnp.concatenate([scaled * accept_rows, scaled * donor_rows], axis=0)
    blank = jnp.zeros((512, 64), F32)
    grads = jnp.concatenate(
        [
            jnp.concatenate([grads, blank], axis=1),
            jnp.concatenate([blank, grads], axis=1),
        ],
        axis=0,
    ).astype(BF)
    lane = lax.broadcasted_iota(jnp.int32, (256, 128), 1)
    turned = jnp.where(
        lane == 0,
        donor.astype(F32),
        jnp.where(lane == 1, accept.astype(F32), jnp.where(lane == 2, partial, 0.0)),
    ).T
    spot_row = jnp.concatenate([turned[0:1, :], turned[1:2, :]], axis=1).astype(jnp.int32)
    high = rounded(turned[2:3, :])
    rest = turned[2:3, :] - high
    extra = jnp.concatenate(
        [
            jnp.zeros((4, 128), F32),
            high[:, :128],
            high[:, 128:],
            rest[:, :128],
            rest[:, 128:],
            jnp.zeros((8, 128), F32),
        ],
        axis=0,
    )
    index = lax.broadcasted_iota(jnp.int32, (80, 1), 0)
    low_row = jnp.where(index < 64, index, index - 67)
    high_row = index + 64
    for group in range(4):
        picks = []
        for target in range(4 * group, 4 * group + 4):
            base = 128 * target
            low_pick = jnp.where(index < 67, (low_row + base) & 2047, -1) == spot_row
            high_pick = jnp.where(index < 67, (high_row + base) & 2047, -1) == spot_row
            picks.append(jnp.concatenate([low_pick.astype(F32), high_pick.astype(F32)], axis=1))
        pieces = dot(jnp.concatenate(picks, axis=0).astype(BF), grads)
        for place in range(4):
            target = 4 * group + place
            piece = pieces[80 * place : 80 * place + 80]
            sent_ref[target, 0:64, :] = piece[0:64].astype(BF)
            sent_ref[target, 64:80, :] = (piece[64:80] + extra).astype(BF)
        part = pl.ds(4 * group, 4)
        copies.append(pltpu.make_async_copy(sent_ref.at[part], sent_hbm.at[part], sems.at[group]))
        copies[-1].start()
    wait_for(copies)


def pair_part(seq_index, got, head_vec):
    return pl.pallas_call(
        pair_kernel,
        out_shape=[
            jax.ShapeDtypeStruct((16, 80, 128), BF),
            jax.ShapeDtypeStruct((1, 128), F32),
        ],
        in_specs=[SMEM, VMEM, HBM],
        out_specs=[HBM] * 2,
        scratch_shapes=[
            pltpu.VMEM((8, 128), F32),
            pltpu.VMEM((16, 80, 128), BF),
            pltpu.VMEM((1, 128), F32),
            pltpu.SemaphoreType.DMA((5,)),
        ],
        compiler_params=pltpu.CompilerParams(vmem_limit_bytes=52 * MEBI),
        cost_estimate=pl.CostEstimate(
            flops=5 * 10**8, bytes_accessed=10**6, transcendentals=0
        ),
        name="pairs",
    )(seq_index, got, head_vec.reshape(8, 128))


def backward_kernel(seq_ref, live_ref, back_ref, *refs):
    sources, second_hbm, outs = refs[:3], refs[3], refs[4:8]
    held, second_mat, staged = refs[8:11], refs[11], refs[12:16]
    track_ref, slope_2_ref, slope_1_ref = held
    mess_ref, grad_1_ref, grad_y_ref, scores_ref = staged
    wide, grad_y, grad_1, sems, out_sems = refs[16:]
    seq_index = seq_ref[0]
    parts = [pl.ds(512 * k, 512) for k in range(5)]
    copies = started(
        list(zip(sources, held)) + [(second_hbm.at[part], second_mat.at[part]) for part in parts],
        sems,
    )

    def send(place, part, sem):
        copy = pltpu.make_async_copy(part(staged[place]), part(outs[place]), out_sems.at[sem])
        copy.start()
        return copy

    def all_of(ref):
        return ref

    left = half_lanes(64)
    edge = half_lanes(16)
    wide[0:16, :] = jnp.zeros((16, 1024), F32)
    wide[144:160, :] = jnp.zeros((16, 1024), F32)
    for pair in range(8):
        lanes = slice(128 * pair, 128 * pair + 128)
        one = back_ref[2 * pair, 0:64, :].astype(F32)
        two = back_ref[2 * pair + 1, 0:64, :].astype(F32)
        wide[16:80, lanes] = jnp.where(left, one, swap(two))
        wide[80:144, lanes] = jnp.where(left, swap(one), two)
        one = back_ref[2 * pair, 64:80, :].astype(F32)
        two = back_ref[2 * pair + 1, 64:80, :].astype(F32)
        wide[13:16, lanes] = jnp.where(edge, one, swap(two))[0:3]
        wide[144:147, lanes] = jnp.where(edge, swap(one), two)[0:3]
    copies[0].wait()
    wide[13:138, :] = wide[13:138, :] + track_ref[...].astype(F32)[3:128]
    copies[1].wait()
    wide[138:147, :] = wide[138:147, :] + slope_2_ref[144:153, :]
    wide[8:152, :] = wide[8:152, :] * slope_2_ref[0:144, :]
    for target in range(8):
        mess_ref[target, 144:288, :] = wide[8:152, 128 * target : 128 * target + 128].astype(BF)
    sent = [send(0, lambda ref: ref.at[:, pl.ds(144, 144)], 0)]
    pooled = jnp.zeros((144, 512), F32)
    for k in range(5):
        copies[3 + k].wait()
        pooled = pooled + dot(
            jnp.where(within(144, 130, 2 - k, seq_index), wide[10 - k : 154 - k, :], 0.0).astype(BF),
            second_mat[512 * k : 512 * k + 512, :],
            ((1,), (1,)),
        )
    pooled = 0.5 * pooled
    copies[2].wait()
    for tile in range(4):
        lanes = slice(128 * tile, 128 * tile + 128)
        grad_y[pl.ds(288 * tile, 144, 2), :] = pooled[:, lanes]
        grad_y[pl.ds(288 * tile + 1, 144, 2), :] = pooled[:, lanes]
        value = grad_y[288 * tile : 288 * tile + 288, :]
        grad_y_ref[:, lanes] = value[16:272]
        value = value * slope_1_ref[:, lanes]
        grad_1[:, lanes] = value
        grad_1_ref[:, lanes] = value.astype(BF)
    sent += [send(1, all_of, 1), send(2, all_of, 2)]
    left = half_lanes(144)
    for pair in range(4):
        lanes = slice(128 * pair, 128 * pair + 128)
        one = grad_1[8:152, lanes]
        two = grad_1[136:280, lanes]
        mess_ref[2 * pair, 0:144, :] = jnp.where(left, one, swap(two)).astype(BF)
        mess_ref[2 * pair + 1, 0:144, :] = jnp.where(left, swap(one), two).astype(BF)
    sent.append(send(0, lambda ref: ref.at[:, pl.ds(0, 144)], 3))
    total = jnp.zeros((16, 128), F32)
    for source in range(16):
        total = total + back_ref[source, 64:80, :].astype(F32)
    row = jnp.where(seq_index < 8, total[4:5] + total[6:7], total[5:6] + total[7:8])
    row = pltpu.roll(row, 128 - 16 * (seq_index % 8), 1)[:, :16]
    live = lax.broadcasted_iota(jnp.int32, (1, 16), 1) < live_ref[0]
    scores_ref[...] = jnp.where(live, row * (1024 ** -0.5), 0.0)
    sent.append(send(3, all_of, 4))
    wait_for(sent)


def backward_part(seq_cell, live, back, track, slope_first, slope_second, w_second):
    return pl.pallas_call(
        backward_kernel,
        out_shape=[
            jax.ShapeDtypeStruct((8, 288, 128), BF),
            jax.ShapeDtypeStruct((288, 512), BF),
            jax.ShapeDtypeStruct((256, 512), F32),
            jax.ShapeDtypeStruct((1, 16), F32),
        ],
        in_specs=[SMEM] * 2 + [VMEM] + [HBM] * 4,
        out_specs=[HBM] * 4,
        scratch_shapes=[
            pltpu.VMEM((128, 1024), BF),
            pltpu.VMEM((160, 1024), F32),
            pltpu.VMEM((288, 512), F32),
            pltpu.VMEM((2560, 1024), BF),
            pltpu.VMEM((8, 288, 128), BF),
            pltpu.VMEM((288, 512), BF),
            pltpu.VMEM((256, 512), F32),
            pltpu.VMEM((1, 16), F32),
            pltpu.VMEM((160, 1024), F32),
            pltpu.VMEM((1168, 128), F32),
            pltpu.VMEM((288, 512), F32),
            pltpu.SemaphoreType.DMA((8,)),
            pltpu.SemaphoreType.DMA((5,)),
        ],
        compiler_params=pltpu.CompilerParams(vmem_limit_bytes=52 * MEBI),
        cost_estimate=pl.CostEstimate(
            flops=8 * 10**8, bytes_accessed=10 * 10**6, transcendentals=0
        ),
        name="backward",
    )(
        seq_cell, live, back, track, slope_second, slope_first,
        w_second.reshape(2560, 1024),
    )


def input_kernel(seq_ref, *refs):
    sources, (out_ref, tail_ref), held, (grad_1, sems) = refs[:3], refs[3:5], refs[5:8], refs[8:]
    grad_ref, grad_y_ref, first_mat = held
    copies = started(list(zip(sources, held)), sems)
    copies[0].wait()
    grad_1[...] = grad_ref[...].astype(F32)
    wait_for(copies[1:])
    total = grad_y_ref[...]
    for k in range(5):
        rows = jnp.where(within(256, 244, 2 - k, seq_ref[0]), grad_1[18 - k : 274 - k, :], 0.0)
        total = total + dot(
            rows.astype(BF), first_mat[512 * k : 512 * k + 512, :], ((1,), (1,))
        )
    out_ref[...] = total.astype(BF)
    tail_ref[...] = total[240:256].astype(BF)


def input_part(seq_cell, grad_y, grad_first_pre, w_first):
    return pl.pallas_call(
        input_kernel,
        out_shape=[
            jax.ShapeDtypeStruct((256, 512), BF),
            jax.ShapeDtypeStruct((16, 512), BF),
        ],
        in_specs=[SMEM] + [HBM] * 3,
        out_specs=[VMEM] * 2,
        scratch_shapes=[
            pltpu.VMEM((288, 512), BF),
            pltpu.VMEM((256, 512), F32),
            pltpu.VMEM((2560, 512), BF),
            pltpu.VMEM((288, 512), F32),
            pltpu.SemaphoreType.DMA((3,)),
        ],
        compiler_params=pltpu.CompilerParams(vmem_limit_bytes=52 * MEBI),
        cost_estimate=pl.CostEstimate(
            flops=7 * 10**8, bytes_accessed=4 * 10**6, transcendentals=0
        ),
        name="inputs",
    )(seq_cell, grad_first_pre, grad_y, w_first.reshape(2560, 512))


def term_kernel(dp_ref, seq_ref, *refs):
    sources, out_hbm, held, out_ref = refs[:10], refs[10], refs[11:21], refs[21]
    part_scr, wide_1, wide_2, sum_1, sum_2, mess, sems, out_sems = refs[22:]
    got_ref, head_ref, columns = held[0], held[1], held[2:]
    copies = started(list(zip(sources, held)), sems)
    copies[0].wait()
    left = half_lanes(128)
    fit_1 = [half_lanes(16) | within(16, 4, 2 - k, seq_ref[0]) for k in range(5)]
    fit_2 = [within(16, 10, 2 - k, seq_ref[0]) for k in range(5)]
    for step in range(8):
        part_scr[...] = got_ref[dp_ref[0] ^ step].astype(F32)
        taps = []
        for k in range(5):
            ends = jnp.where(fit_1[k], part_scr[122 - k : 138 - k, :], 0.0)
            taps.append(jnp.concatenate([part_scr[10 - k : 122 - k, :], ends], axis=0))
            lanes = slice(128 * k, 128 * k + 128)
            wide_2[128 * step : 128 * step + 112, lanes] = part_scr[154 - k : 266 - k, :].astype(BF)
            wide_2[128 * step + 112 : 128 * step + 128, lanes] = jnp.where(
                fit_2[k], part_scr[266 - k : 282 - k, :], 0.0
            ).astype(BF)
        top = [
            jnp.where(left, taps[0], swap(taps[1])),
            jnp.where(left, taps[2], swap(taps[3])),
            taps[4],
        ]
        low = [
            jnp.where(left, swap(taps[0]), taps[1]),
            jnp.where(left, swap(taps[2]), taps[3]),
            swap(taps[4]),
        ]
        for place in range(3):
            lanes = slice(128 * place, 128 * place + 128)
            wide_1[256 * step : 256 * step + 128, lanes] = top[place].astype(BF)
            wide_1[256 * step + 128 : 256 * step + 256, lanes] = low[place].astype(BF)
    wait_for(copies[1:])
    lefts = jnp.concatenate([ref[:, 0:256] for ref in columns], axis=1)
    first = dot(lefts, wide_1[...])
    lefts = jnp.concatenate([ref[:, 256:384] for ref in columns], axis=1)
    second = dot(lefts, wide_2[...])
    left = half_lanes(512)
    for k in range(5):
        sum_2[512 * k : 512 * k + 512, :] = second[:, 128 * k : 128 * k + 128]
        tile = first[:, 128 * (k // 2) : 128 * (k // 2) + 128]
        turned = swap(tile)
        sum_1[512 * k : 512 * k + 512, :] = (
            jnp.where(left, tile, turned) if k % 2 == 0 else jnp.where(left, turned, tile)
        )
    left = half_lanes(10)
    head = jnp.concatenate([head_ref[...], jnp.zeros((1, 128), F32)], axis=0)
    sent = []
    for owner in range(128):
        row = 20 * owner
        slot = owner % 4
        mess[slot, 0:20, :] = sum_2[row : row + 20, :]
        mess[slot, 20:30, :] = jnp.where(
            left, sum_1[row : row + 10, :], sum_1[row + 10 : row + 20, :]
        )
        if owner < 4:
            mess[slot, 30:32, :] = head
        out_ref[owner] = mess[slot, 0:32, :].astype(BF)
        if owner % 32 == 31:
            part = pl.ds(owner - 31, 32)
            sent.append(
                pltpu.make_async_copy(out_ref.at[part], out_hbm.at[part], out_sems.at[owner // 32])
            )
            sent[-1].start()
    wait_for(sent)


def term_part(columns, got, head_row, dp_index, seq_cell):
    return pl.pallas_call(
        term_kernel,
        out_shape=jax.ShapeDtypeStruct((128, 32, 128), BF),
        in_specs=[SMEM] * 2 + [ANY] * 2 + [HBM] * 8,
        out_specs=HBM,
        scratch_shapes=[
            pltpu.VMEM((8, 288, 128), BF),
            pltpu.VMEM((1, 128), F32),
        ]
        + [pltpu.VMEM((512, 384), BF)] * 8
        + [
            pltpu.VMEM((128, 32, 128), BF),
            pltpu.VMEM((288, 128), F32),
            pltpu.VMEM((2048, 384), BF),
            pltpu.VMEM((1024, 640), BF),
            pltpu.VMEM((2576, 128), F32),
            pltpu.VMEM((2576, 128), F32),
            pltpu.VMEM((4, 48, 128), F32),
            pltpu.SemaphoreType.DMA((10,)),
            pltpu.SemaphoreType.DMA((4,)),
        ],
        compiler_params=pltpu.CompilerParams(vmem_limit_bytes=52 * MEBI),
        cost_estimate=pl.CostEstimate(flops=3 * 10**9, bytes_accessed=5 * 10**6, transcendentals=0),
        name="terms",
    )(jnp.reshape(dp_index, (1,)), seq_cell, got, head_row, *columns)


def final_kernel(final_ref, first_ref, second_ref, head_ref):
    left = half_lanes(10)
    for pair in range(4):
        sums = []
        for block in (2 * pair, 2 * pair + 1):
            total = final_ref[16 * block].astype(F32)
            for source in range(1, 16):
                total = total + final_ref[16 * block + source].astype(F32)
            second_ref[:, 128 * block : 128 * block + 128] = total[0:20]
            sums.append(total[20:30])
        one, two = sums
        lanes = slice(128 * pair, 128 * pair + 128)
        first_ref[:, lanes] = jnp.concatenate(
            [jnp.where(left, one, swap(two)), jnp.where(left, swap(one), two)], axis=0
        )
    left = half_lanes(16)
    for pair in range(8):
        sums = []
        for source in (2 * pair, 2 * pair + 1):
            total = final_ref[source, 16:32, :].astype(F32)
            for block in range(1, 8):
                total = total + final_ref[16 * block + source, 16:32, :].astype(F32)
            sums.append(total + swap(total))
        head_ref[pair : pair + 1, :] = jnp.where(left, sums[0], sums[1])[14:15]


def final_part(final):
    return pl.pallas_call(
        final_kernel,
        out_shape=[
            jax.ShapeDtypeStruct((20, 512), F32),
            jax.ShapeDtypeStruct((20, 1024), F32),
            jax.ShapeDtypeStruct((8, 128), F32),
        ],
        in_specs=[VMEM],
        out_specs=[VMEM] * 3,
        compiler_params=pltpu.CompilerParams(vmem_limit_bytes=50 * MEBI),
        name="final",
    )(final)


def per_device(
    seq_in, w_first, w_second, head_vec, track_cot, donor_pos, acceptor_pos, pair_cot, live_pairs
):
    seq_index = lax.axis_index("seq")
    seq_cell = jnp.reshape(seq_index, (1,))
    dp_index = lax.axis_index("dp")
    inputs, track = seq_in[0], track_cot[0]
    right = edges(inputs, track, 16)
    message, mine, slope_first, slope_second = forward_part(
        seq_cell, live_pairs[0], inputs, right, donor_pos, acceptor_pos, pair_cot,
        w_first, w_second,
    )
    got = lax.all_to_all(message, "seq", 0, 0, tiled=True)

    mine = mine.T

    def passed(value, step):
        return lax.ppermute(value, "dp", [(i, i ^ step) for i in range(8)])

    own = [mine] + [passed(mine, step) for step in (2, 4, 6)]
    sent, head_row = pair_part(seq_cell, got, head_vec)
    back = lax.all_to_all(sent, "seq", 0, 0, tiled=True)
    back, *own = lax.optimization_barrier((back, *own))
    message, grad_1, grad_y, scores = backward_part(
        seq_cell, live_pairs[0], back, track, slope_first, slope_second, w_second
    )
    other = [passed(value, 1) for value in own]
    columns = [(own, other)[step % 2][step // 2] for step in range(8)]
    grads = lax.all_to_all(message, "dp", 0, 0, tiled=True)
    grad_input, tail = input_part(seq_cell, grad_y, grad_1, w_first)
    before = lax.ppermute(tail, "seq", [(i, (i + 1) % 16) for i in range(16)])
    terms = term_part(columns, grads, head_row, dp_index, seq_cell)
    terms, before = lax.optimization_barrier((terms, before))
    grad_input = jnp.concatenate([before[4:], grad_input[:244]], axis=0)
    final = lax.all_to_all(terms, ("dp", "seq"), 0, 0, tiled=True)
    out_first, out_second, grad_head = final_part(final)
    return (scores, out_first, out_second, grad_input[None], grad_head.reshape(1024))


def solution(mesh):
    in_specs = (
        P("dp", "seq", None),
        P(),
        P(),
        P(),
        P("dp", "seq", None),
        P("dp", "seq"),
        P("dp", "seq"),
        P("dp", "seq"),
        P("dp", "seq"),
    )
    out_specs = (
        P("dp", "seq"),
        P(("dp", "seq"), None),
        P(("dp", "seq"), None),
        P("dp", "seq", None),
        P(),
    )
    return jax.shard_map(
        per_device, mesh=mesh, in_specs=in_specs, out_specs=out_specs, check_vma=False
    )
```

```python
import jax
import jax.numpy as jnp
from jax import lax
from jax.experimental import pallas as pl
from jax.experimental.pallas import tpu as pltpu
from jax.sharding import PartitionSpec as P

BF = jnp.bfloat16
F32 = jnp.float32
ROOT = 0.7978845608028654
CUBE = 0.044715


def gelu_both(pre):
    square = pre * pre
    bent = jnp.tanh(ROOT * pre * (1.0 + CUBE * square))
    half = 0.5 * (1.0 + bent)
    slope = half + 0.5 * pre * (1.0 - bent * bent) * (ROOT * (1.0 + 3.0 * CUBE * square))
    return pre * half, slope


def dot(left, right, dims=((1,), (0,))):
    return lax.dot_general(left, right, (dims, ((), ())), preferred_element_type=F32)


VMEM = pl.BlockSpec(memory_space=pltpu.VMEM)
SMEM = pl.BlockSpec(memory_space=pltpu.SMEM)
HBM = pl.BlockSpec(memory_space=pltpu.HBM)
ANY = pl.BlockSpec(memory_space=pl.ANY)
MEBI = 1024 * 1024


def rounded(value):
    return value.astype(BF).astype(F32)


def half_lanes(rows):
    return lax.broadcasted_iota(jnp.int32, (rows, 128), 1) < 64


def swap(value):
    return pltpu.roll(value, 64, 1)


def started(moves, sems):
    copies = []
    for place, (source, target) in enumerate(moves):
        copies.append(pltpu.make_async_copy(source, target, sems.at[place]))
        copies[place].start()
    return copies


def wait_for(copies):
    for copy in copies:
        copy.wait()


def within(rows, seam, shift, seq_index):
    row = lax.broadcasted_iota(jnp.int32, (rows, 1), 0)
    return ((row >= seam) == (row + shift >= seam)) | (seq_index != 15)


def edge_kernel(inputs_hbm, track_hbm, out_hbm, rows_scr, track_scr, out_scr, sems):
    wait_for(
        started(
            [
                (inputs_hbm.at[pl.ds(0, 32)], rows_scr),
                (track_hbm.at[pl.ds(0, 16)], track_scr),
            ],
            sems,
        )
    )
    track = track_scr[...].astype(F32)
    pieces = [rows_scr[...].astype(F32)[:24]]
    for row in range(9):
        pieces += [track[row : row + 1, :512], track[row : row + 1, 512:]]
    pieces.append(jnp.zeros((6, 512), F32))
    out_scr[...] = jnp.concatenate(pieces, axis=0).astype(BF)
    wait_for(started([(out_scr, out_hbm)], sems))


def edges(inputs, track, count):
    first = pl.pallas_call(
        edge_kernel,
        out_shape=jax.ShapeDtypeStruct((48, 512), BF),
        in_specs=[HBM] * 2,
        out_specs=HBM,
        scratch_shapes=[
            pltpu.VMEM((32, 512), BF),
            pltpu.VMEM((16, 1024), BF),
            pltpu.VMEM((48, 512), BF),
            pltpu.SemaphoreType.DMA((2,)),
        ],
        compiler_params=pltpu.CompilerParams(vmem_limit_bytes=56 * MEBI),
        name="edges",
    )(inputs, track)
    return lax.ppermute(first, "seq", [(i, (i - 1) % count) for i in range(count)])


def forward_kernel(seq_ref, live_ref, *refs):
    sources, outs, held, staged, work = refs[:7], refs[7:11], refs[11:18], refs[18:22], refs[22:]
    inputs_ref, right_ref, first_mat, second_mat, donor_ref, accept_ref, cot_ref = held
    mess_ref, mine_ref, slope_1_ref, slope_2_ref = staged
    ext, act_scr, wide, sems, out_sems = work
    copies = started(list(zip(sources, held)), sems)

    def send(place):
        copy = pltpu.make_async_copy(staged[place], outs[place], out_sems.at[place])
        copy.start()
        return copy

    seq_index = seq_ref[0]
    ext[0:32, :] = jnp.zeros((32, 512), F32)
    ext[288:320, :] = jnp.zeros((32, 512), F32)
    wait_for(copies[:2])
    ext[20:276, :] = inputs_ref[...].astype(F32)
    ext[276:300, :] = right_ref[...].astype(F32)[:24]
    taps = jnp.concatenate(
        [
            jnp.where(within(288, 260, k - 2, seq_index), ext[14 + k : 302 + k, :], 0.0).astype(BF)
            for k in range(5)
        ],
        axis=1,
    )
    copies[2].wait()
    pre = dot(taps, first_mat[...])
    act, slope = gelu_both(pre)
    slope_1_ref[...] = slope
    sent = [send(2)]
    y_first = ext[16:304, :] + act
    for tile in range(4):
        lanes = slice(128 * tile, 128 * tile + 128)
        act_scr[288 * tile : 288 * tile + 288, :] = y_first[:, lanes]
        even = act_scr[pl.ds(288 * tile, 144, 2), :]
        wide[8:152, lanes] = even + act_scr[pl.ds(288 * tile + 1, 144, 2), :]
    pooled = 0.5 * wide[8:152, :]
    wide[0:8, :] = jnp.zeros((8, 512), F32)
    wide[152:160, :] = jnp.zeros((8, 512), F32)
    wide[8:152, :] = pooled
    mine_ref[0:256, :] = ext[32:288, :].astype(BF)
    mine_ref[256:384, :] = wide[16:144, :].astype(BF)
    sent.append(send(1))
    taps = jnp.concatenate(
        [
            jnp.where(within(144, 130, k - 2, seq_index), wide[6 + k : 150 + k, :], 0.0).astype(BF)
            for k in range(5)
        ],
        axis=1,
    )
    copies[3].wait()
    pre = dot(taps, second_mat[...])
    act, slope = gelu_both(pre)
    slope_2_ref[0:144, :] = slope
    far = right_ref[...].astype(F32)
    far = [
        jnp.concatenate([far[row : row + 1], far[row + 1 : row + 2]], axis=1)
        for row in range(24, 42, 2)
    ]
    slope_2_ref[144:160, :] = jnp.concatenate(far + [jnp.zeros((7, 1024), F32)], axis=0)
    sent.append(send(3))
    wait_for(copies[4:])

    same = lax.broadcasted_iota(jnp.int32, (16, 16), 0) == lax.broadcasted_iota(
        jnp.int32, (16, 16), 1
    )

    def column(row):
        return jnp.sum(jnp.where(same, row, 0.0), axis=1, keepdims=True)

    donor, accept = (donor_ref[...] - 6) & 2047, (accept_ref[...] - 6) & 2047
    live = lax.broadcasted_iota(jnp.int32, (1, 16), 1) < live_ref[0]
    weight = column(jnp.where(live, cot_ref[...], 0.0) * (1024 ** -0.5))
    lane = lax.broadcasted_iota(jnp.int32, (16, 128), 1)
    info = jnp.zeros((16, 128), F32)
    for place, value in enumerate(
        [
            column((donor >> 6).astype(F32)),
            column((donor & 63).astype(F32)),
            column((accept >> 6).astype(F32)),
            column((accept & 63).astype(F32)),
            weight,
            weight - rounded(weight),
        ]
    ):
        info = jnp.where(lane == place, value, info)
    info = info.astype(BF)
    for target in range(16):
        mess_ref[target, 64:80, :] = info
    left = half_lanes(64)
    for pair in range(8):
        top = act[8:72, 128 * pair : 128 * pair + 128]
        low = act[72:136, 128 * pair : 128 * pair + 128]
        mess_ref[2 * pair, 0:64, :] = jnp.where(left, top, swap(low)).astype(BF)
        mess_ref[2 * pair + 1, 0:64, :] = jnp.where(left, swap(top), low).astype(BF)
        if pair % 2 == 1:
            part = pl.ds(2 * pair - 2, 4)
            sent.append(
                pltpu.make_async_copy(
                    mess_ref.at[part], outs[0].at[part], out_sems.at[4 + pair // 2]
                )
            )
            sent[-1].start()
    wait_for(sent)


def forward_part(seq_index, live, inputs, right, donor, accept, cot, w_first, w_second):
    return pl.pallas_call(
        forward_kernel,
        out_shape=[
            jax.ShapeDtypeStruct((16, 80, 128), BF),
            jax.ShapeDtypeStruct((384, 512), BF),
            jax.ShapeDtypeStruct((288, 512), F32),
            jax.ShapeDtypeStruct((160, 1024), F32),
        ],
        in_specs=[SMEM, SMEM, HBM, ANY] + [HBM] * 5,
        out_specs=[HBM] * 4,
        scratch_shapes=[
            pltpu.VMEM((256, 512), BF),
            pltpu.VMEM((48, 512), BF),
            pltpu.VMEM((2560, 512), BF),
            pltpu.VMEM((2560, 1024), BF),
            pltpu.VMEM((1, 16), jnp.int32),
            pltpu.VMEM((1, 16), jnp.int32),
            pltpu.VMEM((1, 16), F32),
            pltpu.VMEM((16, 80, 128), BF),
            pltpu.VMEM((384, 512), BF),
            pltpu.VMEM((288, 512), F32),
            pltpu.VMEM((160, 1024), F32),
            pltpu.VMEM((320, 512), F32),
            pltpu.VMEM((1168, 128), F32),
            pltpu.VMEM((160, 512), F32),
            pltpu.SemaphoreType.DMA((7,)),
            pltpu.SemaphoreType.DMA((8,)),
        ],
        compiler_params=pltpu.CompilerParams(vmem_limit_bytes=56 * MEBI),
        cost_estimate=pl.CostEstimate(
            flops=15 * 10**8, bytes_accessed=10 * 10**6, transcendentals=3 * 10**5
        ),
        name="forward",
    )(
        seq_index, live, inputs, right,
        w_first.reshape(2560, 512), w_second.reshape(2560, 1024), donor, accept, cot,
    )


def pair_kernel(
    seq_ref, got_ref, head_hbm, sent_hbm, term_hbm, head_ref, sent_ref, term_ref, sems
):
    head_copy = started([(head_hbm, head_ref)], sems)
    seq_index = seq_ref[0]
    flat = jnp.concatenate([got_ref[i] for i in range(16)], axis=0)
    info = jnp.concatenate([got_ref[i, 64:80, :].astype(F32) for i in range(16)], axis=0)
    donor = (info[:, 0:1] * 64.0 + info[:, 1:2]).astype(jnp.int32)
    accept = (info[:, 2:3] * 64.0 + info[:, 3:4]).astype(jnp.int32)
    weight = info[:, 4:5] + info[:, 5:6]
    spots = jnp.concatenate([donor, accept], axis=0)
    row_of = (spots >> 7) * 80 + (spots & 63)
    pick = (row_of == lax.broadcasted_iota(jnp.int32, (512, 1280), 1)).astype(F32).astype(BF)
    rows = dot(pick, flat)
    rows = jnp.where((spots & 127) < 64, rows, swap(rows))[:, :64]
    donor_rows, accept_rows = rows[:256], rows[256:]
    both = donor_rows * accept_rows
    wait_for(head_copy)
    head_row = head_ref[pl.ds(seq_index // 2, 1), :]
    head_row = jnp.where(seq_index % 2 == 0, head_row, swap(head_row))[:, :64]
    partial = jnp.sum(both * head_row, axis=1, keepdims=True)
    term = jnp.sum(weight * both, axis=0, keepdims=True)
    term_high = rounded(term)
    term_ref[...] = jnp.concatenate([term_high, term - term_high], axis=1)
    copies = [pltpu.make_async_copy(term_ref, term_hbm, sems.at[4])]
    copies[0].start()
    scaled = weight * head_row
    grads = jnp.concatenate([scaled * accept_rows, scaled * donor_rows], axis=0)
    blank = jnp.zeros((512, 64), F32)
    grads = jnp.concatenate(
        [
            jnp.concatenate([grads, blank], axis=1),
            jnp.concatenate([blank, grads], axis=1),
        ],
        axis=0,
    ).astype(BF)
    lane = lax.broadcasted_iota(jnp.int32, (256, 128), 1)
    turned = jnp.where(
        lane == 0,
        donor.astype(F32),
        jnp.where(lane == 1, accept.astype(F32), jnp.where(lane == 2, partial, 0.0)),
    ).T
    spot_row = jnp.concatenate([turned[0:1, :], turned[1:2, :]], axis=1).astype(jnp.int32)
    high = rounded(turned[2:3, :])
    rest = turned[2:3, :] - high
    extra = jnp.concatenate(
        [
            jnp.zeros((4, 128), F32),
            high[:, :128],
            high[:, 128:],
            rest[:, :128],
            rest[:, 128:],
            jnp.zeros((8, 128), F32),
        ],
        axis=0,
    )
    index = lax.broadcasted_iota(jnp.int32, (80, 1), 0)
    low_row = jnp.where(index < 64, index, index - 67)
    high_row = index + 64
    for group in range(4):
        picks = []
        for target in range(4 * group, 4 * group + 4):
            base = 128 * target
            low_pick = jnp.where(index < 67, (low_row + base) & 2047, -1) == spot_row
            high_pick = jnp.where(index < 67, (high_row + base) & 2047, -1) == spot_row
            picks.append(jnp.concatenate([low_pick.astype(F32), high_pick.astype(F32)], axis=1))
        pieces = dot(jnp.concatenate(picks, axis=0).astype(BF), grads)
        for place in range(4):
            target = 4 * group + place
            piece = pieces[80 * place : 80 * place + 80]
            sent_ref[target, 0:64, :] = piece[0:64].astype(BF)
            sent_ref[target, 64:80, :] = (piece[64:80] + extra).astype(BF)
        part = pl.ds(4 * group, 4)
        copies.append(pltpu.make_async_copy(sent_ref.at[part], sent_hbm.at[part], sems.at[group]))
        copies[-1].start()
    wait_for(copies)


def pair_part(seq_index, got, head_vec):
    return pl.pallas_call(
        pair_kernel,
        out_shape=[
            jax.ShapeDtypeStruct((16, 80, 128), BF),
            jax.ShapeDtypeStruct((1, 128), F32),
        ],
        in_specs=[SMEM, VMEM, HBM],
        out_specs=[HBM] * 2,
        scratch_shapes=[
            pltpu.VMEM((8, 128), F32),
            pltpu.VMEM((16, 80, 128), BF),
            pltpu.VMEM((1, 128), F32),
            pltpu.SemaphoreType.DMA((5,)),
        ],
        compiler_params=pltpu.CompilerParams(vmem_limit_bytes=52 * MEBI),
        cost_estimate=pl.CostEstimate(
            flops=5 * 10**8, bytes_accessed=10**6, transcendentals=0
        ),
        name="pairs",
    )(seq_index, got, head_vec.reshape(8, 128))


def backward_kernel(seq_ref, live_ref, back_ref, *refs):
    sources, second_hbm, outs = refs[:3], refs[3], refs[4:8]
    held, second_mat, staged = refs[8:11], refs[11], refs[12:16]
    track_ref, slope_2_ref, slope_1_ref = held
    mess_ref, grad_1_ref, grad_y_ref, scores_ref = staged
    wide, grad_y, grad_1, sems, out_sems = refs[16:]
    seq_index = seq_ref[0]
    parts = [pl.ds(512 * k, 512) for k in range(5)]
    copies = started(
        list(zip(sources, held)) + [(second_hbm.at[part], second_mat.at[part]) for part in parts],
        sems,
    )

    def send(place, part, sem):
        copy = pltpu.make_async_copy(part(staged[place]), part(outs[place]), out_sems.at[sem])
        copy.start()
        return copy

    def all_of(ref):
        return ref

    left = half_lanes(64)
    edge = half_lanes(16)
    wide[0:16, :] = jnp.zeros((16, 1024), F32)
    wide[144:160, :] = jnp.zeros((16, 1024), F32)
    for pair in range(8):
        lanes = slice(128 * pair, 128 * pair + 128)
        one = back_ref[2 * pair, 0:64, :].astype(F32)
        two = back_ref[2 * pair + 1, 0:64, :].astype(F32)
        wide[16:80, lanes] = jnp.where(left, one, swap(two))
        wide[80:144, lanes] = jnp.where(left, swap(one), two)
        one = back_ref[2 * pair, 64:80, :].astype(F32)
        two = back_ref[2 * pair + 1, 64:80, :].astype(F32)
        wide[13:16, lanes] = jnp.where(edge, one, swap(two))[0:3]
        wide[144:147, lanes] = jnp.where(edge, swap(one), two)[0:3]
    copies[0].wait()
    wide[13:138, :] = wide[13:138, :] + track_ref[...].astype(F32)[3:128]
    copies[1].wait()
    wide[138:147, :] = wide[138:147, :] + slope_2_ref[144:153, :]
    wide[8:152, :] = wide[8:152, :] * slope_2_ref[0:144, :]
    for target in range(8):
        mess_ref[target, 144:288, :] = wide[8:152, 128 * target : 128 * target + 128].astype(BF)
    sent = [send(0, lambda ref: ref.at[:, pl.ds(144, 144)], 0)]
    pooled = jnp.zeros((144, 512), F32)
    for k in range(5):
        copies[3 + k].wait()
        pooled = pooled + dot(
            jnp.where(within(144, 130, 2 - k, seq_index), wide[10 - k : 154 - k, :], 0.0).astype(BF),
            second_mat[512 * k : 512 * k + 512, :],
            ((1,), (1,)),
        )
    pooled = 0.5 * pooled
    copies[2].wait()
    for tile in range(4):
        lanes = slice(128 * tile, 128 * tile + 128)
        grad_y[pl.ds(288 * tile, 144, 2), :] = pooled[:, lanes]
        grad_y[pl.ds(288 * tile + 1, 144, 2), :] = pooled[:, lanes]
        value = grad_y[288 * tile : 288 * tile + 288, :]
        grad_y_ref[:, lanes] = value[16:272]
        value = value * slope_1_ref[:, lanes]
        grad_1[:, lanes] = value
        grad_1_ref[:, lanes] = value.astype(BF)
    sent += [send(1, all_of, 1), send(2, all_of, 2)]
    left = half_lanes(144)
    for pair in range(4):
        lanes = slice(128 * pair, 128 * pair + 128)
        one = grad_1[8:152, lanes]
        two = grad_1[136:280, lanes]
        mess_ref[2 * pair, 0:144, :] = jnp.where(left, one, swap(two)).astype(BF)
        mess_ref[2 * pair + 1, 0:144, :] = jnp.where(left, swap(one), two).astype(BF)
        part = pl.ds(2 * pair, 2)
        sent.append(send(0, lambda ref, part=part: ref.at[part, pl.ds(0, 144)], 5 + pair))
    total = jnp.zeros((16, 128), F32)
    for source in range(16):
        total = total + back_ref[source, 64:80, :].astype(F32)
    row = jnp.where(seq_index < 8, total[4:5] + total[6:7], total[5:6] + total[7:8])
    row = pltpu.roll(row, 128 - 16 * (seq_index % 8), 1)[:, :16]
    live = lax.broadcasted_iota(jnp.int32, (1, 16), 1) < live_ref[0]
    scores_ref[...] = jnp.where(live, row * (1024 ** -0.5), 0.0)
    sent.append(send(3, all_of, 4))
    wait_for(sent)


def backward_part(seq_cell, live, back, track, slope_first, slope_second, w_second):
    return pl.pallas_call(
        backward_kernel,
        out_shape=[
            jax.ShapeDtypeStruct((8, 288, 128), BF),
            jax.ShapeDtypeStruct((288, 512), BF),
            jax.ShapeDtypeStruct((256, 512), F32),
            jax.ShapeDtypeStruct((1, 16), F32),
        ],
        in_specs=[SMEM] * 2 + [VMEM] + [HBM] * 4,
        out_specs=[HBM] * 4,
        scratch_shapes=[
            pltpu.VMEM((128, 1024), BF),
            pltpu.VMEM((160, 1024), F32),
            pltpu.VMEM((288, 512), F32),
            pltpu.VMEM((2560, 1024), BF),
            pltpu.VMEM((8, 288, 128), BF),
            pltpu.VMEM((288, 512), BF),
            pltpu.VMEM((256, 512), F32),
            pltpu.VMEM((1, 16), F32),
            pltpu.VMEM((160, 1024), F32),
            pltpu.VMEM((1168, 128), F32),
            pltpu.VMEM((288, 512), F32),
            pltpu.SemaphoreType.DMA((8,)),
            pltpu.SemaphoreType.DMA((9,)),
        ],
        compiler_params=pltpu.CompilerParams(vmem_limit_bytes=52 * MEBI),
        cost_estimate=pl.CostEstimate(
            flops=8 * 10**8, bytes_accessed=10 * 10**6, transcendentals=0
        ),
        name="backward",
    )(
        seq_cell, live, back, track, slope_second, slope_first,
        w_second.reshape(2560, 1024),
    )


def input_kernel(seq_ref, *refs):
    sources, (out_ref, tail_ref), held, (grad_1, sems) = refs[:3], refs[3:5], refs[5:8], refs[8:]
    grad_ref, grad_y_ref, first_mat = held
    copies = started(list(zip(sources, held)), sems)
    copies[0].wait()
    grad_1[...] = grad_ref[...].astype(F32)
    wait_for(copies[1:])
    total = grad_y_ref[...]
    for k in range(5):
        rows = jnp.where(within(256, 244, 2 - k, seq_ref[0]), grad_1[18 - k : 274 - k, :], 0.0)
        total = total + dot(
            rows.astype(BF), first_mat[512 * k : 512 * k + 512, :], ((1,), (1,))
        )
    out_ref[...] = total.astype(BF)
    tail_ref[...] = total[240:256].astype(BF)


def input_part(seq_cell, grad_y, grad_first_pre, w_first):
    return pl.pallas_call(
        input_kernel,
        out_shape=[
            jax.ShapeDtypeStruct((256, 512), BF),
            jax.ShapeDtypeStruct((16, 512), BF),
        ],
        in_specs=[SMEM] + [HBM] * 3,
        out_specs=[VMEM] * 2,
        scratch_shapes=[
            pltpu.VMEM((288, 512), BF),
            pltpu.VMEM((256, 512), F32),
            pltpu.VMEM((2560, 512), BF),
            pltpu.VMEM((288, 512), F32),
            pltpu.SemaphoreType.DMA((3,)),
        ],
        compiler_params=pltpu.CompilerParams(vmem_limit_bytes=52 * MEBI),
        cost_estimate=pl.CostEstimate(
            flops=7 * 10**8, bytes_accessed=4 * 10**6, transcendentals=0
        ),
        name="inputs",
    )(seq_cell, grad_first_pre, grad_y, w_first.reshape(2560, 512))


def term_kernel(dp_ref, seq_ref, *refs):
    sources, out_hbm, held, out_ref = refs[:10], refs[10], refs[11:21], refs[21]
    part_scr, wide_1, wide_2, sum_1, sum_2, mess, sems, out_sems = refs[22:]
    got_ref, head_ref, columns = held[0], held[1], held[2:]
    copies = started(list(zip(sources, held)), sems)
    copies[0].wait()
    left = half_lanes(128)
    fit_1 = [half_lanes(16) | within(16, 4, 2 - k, seq_ref[0]) for k in range(5)]
    fit_2 = [within(16, 10, 2 - k, seq_ref[0]) for k in range(5)]
    for step in range(8):
        part_scr[...] = got_ref[dp_ref[0] ^ step].astype(F32)
        taps = []
        for k in range(5):
            ends = jnp.where(fit_1[k], part_scr[122 - k : 138 - k, :], 0.0)
            taps.append(jnp.concatenate([part_scr[10 - k : 122 - k, :], ends], axis=0))
            lanes = slice(128 * k, 128 * k + 128)
            wide_2[128 * step : 128 * step + 112, lanes] = part_scr[154 - k : 266 - k, :].astype(BF)
            wide_2[128 * step + 112 : 128 * step + 128, lanes] = jnp.where(
                fit_2[k], part_scr[266 - k : 282 - k, :], 0.0
            ).astype(BF)
        top = [
            jnp.where(left, taps[0], swap(taps[1])),
            jnp.where(left, taps[2], swap(taps[3])),
            taps[4],
        ]
        low = [
            jnp.where(left, swap(taps[0]), taps[1]),
            jnp.where(left, swap(taps[2]), taps[3]),
            swap(taps[4]),
        ]
        for place in range(3):
            lanes = slice(128 * place, 128 * place + 128)
            wide_1[256 * step : 256 * step + 128, lanes] = top[place].astype(BF)
            wide_1[256 * step + 128 : 256 * step + 256, lanes] = low[place].astype(BF)
    wait_for(copies[1:])
    lefts = jnp.concatenate([ref[:, 0:256] for ref in columns], axis=1)
    first = dot(lefts, wide_1[...])
    lefts = jnp.concatenate([ref[:, 256:384] for ref in columns], axis=1)
    second = dot(lefts, wide_2[...])
    left = half_lanes(512)
    for k in range(5):
        sum_2[512 * k : 512 * k + 512, :] = second[:, 128 * k : 128 * k + 128]
        tile = first[:, 128 * (k // 2) : 128 * (k // 2) + 128]
        turned = swap(tile)
        sum_1[512 * k : 512 * k + 512, :] = (
            jnp.where(left, tile, turned) if k % 2 == 0 else jnp.where(left, turned, tile)
        )
    left = half_lanes(10)
    head = jnp.concatenate([head_ref[...], jnp.zeros((1, 128), F32)], axis=0)
    sent = []
    for owner in range(128):
        row = 20 * owner
        slot = owner % 4
        mess[slot, 0:20, :] = sum_2[row : row + 20, :]
        mess[slot, 20:30, :] = jnp.where(
            left, sum_1[row : row + 10, :], sum_1[row + 10 : row + 20, :]
        )
        if owner < 4:
            mess[slot, 30:32, :] = head
        out_ref[owner] = mess[slot, 0:32, :].astype(BF)
        if owner % 32 == 31:
            part = pl.ds(owner - 31, 32)
            sent.append(
                pltpu.make_async_copy(out_ref.at[part], out_hbm.at[part], out_sems.at[owner // 32])
            )
            sent[-1].start()
    wait_for(sent)


def term_part(columns, got, head_row, dp_index, seq_cell):
    return pl.pallas_call(
        term_kernel,
        out_shape=jax.ShapeDtypeStruct((128, 32, 128), BF),
        in_specs=[SMEM] * 2 + [ANY] * 2 + [HBM] * 8,
        out_specs=HBM,
        scratch_shapes=[
            pltpu.VMEM((8, 288, 128), BF),
            pltpu.VMEM((1, 128), F32),
        ]
        + [pltpu.VMEM((512, 384), BF)] * 8
        + [
            pltpu.VMEM((128, 32, 128), BF),
            pltpu.VMEM((288, 128), F32),
            pltpu.VMEM((2048, 384), BF),
            pltpu.VMEM((1024, 640), BF),
            pltpu.VMEM((2576, 128), F32),
            pltpu.VMEM((2576, 128), F32),
            pltpu.VMEM((4, 48, 128), F32),
            pltpu.SemaphoreType.DMA((10,)),
            pltpu.SemaphoreType.DMA((4,)),
        ],
        compiler_params=pltpu.CompilerParams(vmem_limit_bytes=52 * MEBI),
        cost_estimate=pl.CostEstimate(flops=3 * 10**9, bytes_accessed=5 * 10**6, transcendentals=0),
        name="terms",
    )(jnp.reshape(dp_index, (1,)), seq_cell, got, head_row, *columns)


def final_kernel(final_ref, first_ref, second_ref, head_ref):
    left = half_lanes(10)
    for pair in range(4):
        sums = []
        for block in (2 * pair, 2 * pair + 1):
            total = final_ref[16 * block].astype(F32)
            for source in range(1, 16):
                total = total + final_ref[16 * block + source].astype(F32)
            second_ref[:, 128 * block : 128 * block + 128] = total[0:20]
            sums.append(total[20:30])
        one, two = sums
        lanes = slice(128 * pair, 128 * pair + 128)
        first_ref[:, lanes] = jnp.concatenate(
            [jnp.where(left, one, swap(two)), jnp.where(left, swap(one), two)], axis=0
        )
    left = half_lanes(16)
    for pair in range(8):
        sums = []
        for source in (2 * pair, 2 * pair + 1):
            total = final_ref[source, 16:32, :].astype(F32)
            for block in range(1, 8):
                total = total + final_ref[16 * block + source, 16:32, :].astype(F32)
            sums.append(total + swap(total))
        head_ref[pair : pair + 1, :] = jnp.where(left, sums[0], sums[1])[14:15]


def final_part(final):
    return pl.pallas_call(
        final_kernel,
        out_shape=[
            jax.ShapeDtypeStruct((20, 512), F32),
            jax.ShapeDtypeStruct((20, 1024), F32),
            jax.ShapeDtypeStruct((8, 128), F32),
        ],
        in_specs=[VMEM],
        out_specs=[VMEM] * 3,
        compiler_params=pltpu.CompilerParams(vmem_limit_bytes=50 * MEBI),
        name="final",
    )(final)


def per_device(
    seq_in, w_first, w_second, head_vec, track_cot, donor_pos, acceptor_pos, pair_cot, live_pairs
):
    seq_index = lax.axis_index("seq")
    seq_cell = jnp.reshape(seq_index, (1,))
    dp_index = lax.axis_index("dp")
    inputs, track = seq_in[0], track_cot[0]
    right = edges(inputs, track, 16)
    message, mine, slope_first, slope_second = forward_part(
        seq_cell, live_pairs[0], inputs, right, donor_pos, acceptor_pos, pair_cot,
        w_first, w_second,
    )
    got = lax.all_to_all(message, "seq", 0, 0, tiled=True)

    mine = mine.T

    def passed(value, step):
        return lax.ppermute(value, "dp", [(i, i ^ step) for i in range(8)])

    own = [mine] + [passed(mine, step) for step in (2, 4, 6)]
    sent, head_row = pair_part(seq_cell, got, head_vec)
    back = lax.all_to_all(sent, "seq", 0, 0, tiled=True)
    back, *own = lax.optimization_barrier((back, *own))
    message, grad_1, grad_y, scores = backward_part(
        seq_cell, live_pairs[0], back, track, slope_first, slope_second, w_second
    )
    other = [passed(value, 1) for value in own]
    columns = [(own, other)[step % 2][step // 2] for step in range(8)]
    grads = lax.all_to_all(message, "dp", 0, 0, tiled=True)
    grad_input, tail = input_part(seq_cell, grad_y, grad_1, w_first)
    before = lax.ppermute(tail, "seq", [(i, (i + 1) % 16) for i in range(16)])
    terms = term_part(columns, grads, head_row, dp_index, seq_cell)
    terms, before = lax.optimization_barrier((terms, before))
    grad_input = jnp.concatenate([before[4:], grad_input[:244]], axis=0)
    final = lax.all_to_all(terms, ("dp", "seq"), 0, 0, tiled=True)
    out_first, out_second, grad_head = final_part(final)
    return (scores, out_first, out_second, grad_input[None], grad_head.reshape(1024))


def solution(mesh):
    in_specs = (
        P("dp", "seq", None),
        P(),
        P(),
        P(),
        P("dp", "seq", None),
        P("dp", "seq"),
        P("dp", "seq"),
        P("dp", "seq"),
        P("dp", "seq"),
    )
    out_specs = (
        P("dp", "seq"),
        P(("dp", "seq"), None),
        P(("dp", "seq"), None),
        P("dp", "seq", None),
        P(),
    )
    return jax.shard_map(
        per_device, mesh=mesh, in_specs=in_specs, out_specs=out_specs, check_vma=False
    )
```
